128 devices in a mesh: expert: 32 (over z, y, core), tensor: 4 (over x).
Axes of the slice: x: 4, y: 4, z: 4, core: 2. Of those that a mesh axis runs over, the one named last changes fastest.
Arguments:
- inputs: bfloat16 [16384, 2048], P(('expert', 'tensor')), may hold values from -6 to 6
- attn_gain: float32 [2048], replicated, may hold values from 0.25 to 1.75
- w_query: bfloat16 [2048, 4096], P(None, 'tensor'), may hold values from -0.125 to 0.125
- w_key: bfloat16 [2048, 512], P(None, 'tensor'), may hold values from -0.125 to 0.125
- w_value: bfloat16 [2048, 512], P(None, 'tensor'), may hold values from -0.125 to 0.125
- q_gain: float32 [128], replicated, may hold values from 0.25 to 1.75
- k_gain: float32 [128], replicated, may hold values from 0.25 to 1.75
- w_out: bfloat16 [4096, 2048], P('tensor'), may hold values from -0.75 to 0.75
- mlp_gain: float32 [2048], replicated, may hold values from 0.25 to 1.75
- w_router: bfloat16 [2048, 64], replicated, may hold values from -0.0625 to 0.0625
- w_gate: bfloat16 [64, 2048, 768], P('expert', None, 'tensor'), may hold values from -0.125 to 0.125
- w_up: bfloat16 [64, 2048, 768], P('expert', None, 'tensor'), may hold values from -0.125 to 0.125
- w_down: bfloat16 [64, 768, 2048], P('expert', 'tensor'), may hold values from -0.875 to 0.875
- routes: int32 [16384, 8], P(('expert', 'tensor')), may hold values from 0 to 63, all different within a row; in each aligned block of 128 rows (0 to 127, 128 to 255, ...) at most 20 rows name the same one
- grad_out: bfloat16 [16384, 2048], P(('expert', 'tensor')), may hold values from -6 to 6
Outputs:
- output: bfloat16 [16384, 2048], P(('expert', 'tensor'))
- grad_inputs: bfloat16 [16384, 2048], P(('expert', 'tensor'))
- grad_attn_gain: float32 [2048], replicated
- grad_w_query: float32 [2048, 4096], P(None, 'tensor')
- grad_w_key: float32 [2048, 512], P(None, 'tensor')
- grad_w_value: float32 [2048, 512], P(None, 'tensor')
- grad_q_gain: float32 [128], replicated
- grad_k_gain: float32 [128], replicated
- grad_w_out: float32 [4096, 2048], P('tensor')
- grad_mlp_gain: float32 [2048], replicated
- grad_w_router: float32 [2048, 64], replicated
- grad_w_gate: float32 [64, 2048, 768], P('expert', None, 'tensor')
- grad_w_up: float32 [64, 2048, 768], P('expert', None, 'tensor')
- grad_w_down: float32 [64, 768, 2048], P('expert', 'tensor')
The draws below stay inside these ranges and needn't reach their ends.
Inputs may be any that keep to these rules, and one draw needn't show every extreme that they name: `routes`: each row names 8 different experts. Among the 128 rows of one device no expert is named more than 20 times, and in every draw some expert is named exactly 20 times by the rows of some device.
All inputs are finite; a program needn't handle non-finite values.
Results may differ from the reference program's by a relative error of at most 0.025.
Values may be sent and summed in bfloat16 or wider, within the bound.
A program may use at most 384 MiB of HBM per device.

```python
import math
import jax
import jax.numpy as jnp
import numpy as np
from jax import lax

D = 2048
HEADS = 32
KV_HEADS = 4
HEAD = 128
FF = 768
TOP = 8
TOK_DEV = 128
SEQ = 512
TOKENS = 16384
EXPERTS = 64
CAP = 20
N_EXPERT = 32


def block_scale(rng, shape, shards, smallest, top_value):
    level, own = 1.0, jax.random.fold_in(rng, 6)
    for axis_at, blocks in shards:
        draws = jnp.exp(jax.random.uniform(jax.random.fold_in(own, axis_at), (blocks,), jnp.float32, smallest / len(shards), top_value / len(shards)))
        level = level * jnp.repeat(draws, shape[axis_at] // blocks).reshape([-1 if axis == axis_at else 1 for axis in range(len(shape))])
    return level


def shared_out(rng, own, number, rows, number_of, top, bound, skew):
    order = jax.random.permutation(rng, number_of)
    crowded, common = portions_of(number_of, rows * top, bound, skew, True), portions_of(number_of, rows * top, bound, skew, False)
    places = jnp.arange(number_of)

    def named(lengths, rotation):
        used = int((lengths > 0).sum())
        fixed = max(1, used // 4)
        passed = fixed + (places - fixed + rotation * (used - fixed)) % max(1, number_of - fixed)
        return jnp.zeros((number_of,), jnp.int32).at[order[jnp.where(places < fixed, places, passed)]].set(jnp.asarray(lengths, jnp.int32))

    lengths = jnp.where(number % 4 == 0, named(crowded, number // 4), named(common, number - number // 4 - 1))
    mixed = jax.random.permutation(jax.random.fold_in(own, 3), number_of)
    source_of, receiver = mixed[0:number_of // 2 * 2:2], mixed[1:number_of // 2 * 2:2]
    slack = jnp.minimum(lengths[source_of] - 1, bound - lengths[receiver]) // 2
    slack = jnp.where((source_of == order[0]) | (receiver == order[0]) | (lengths[receiver] == 0), 0, jnp.maximum(slack, 0))
    passed = jax.random.randint(jax.random.fold_in(own, 4), (number_of // 2,), 0, 1 << 20) % (slack + 1)
    lengths = lengths.at[source_of].add(-passed).at[receiver].add(passed)
    items = jnp.searchsorted(jnp.cumsum(lengths), jnp.arange(rows * top), side="right").astype(jnp.int32)
    listing = items.reshape(top, rows).T
    listing = listing[jax.random.permutation(jax.random.fold_in(own, 1), rows)]
    rotation = jax.random.randint(jax.random.fold_in(own, 2), (rows, 1), 0, top)
    return jnp.take_along_axis(listing, (jnp.arange(top)[None, :] + rotation) % top, axis=1)


def portions_of(number_of, total, limit, slope, full):
    portions = [(1 << 20) // math.isqrt(grade ** slope) + 1 for grade in range(1, number_of + 1)]
    largest = limit if full else min(limit, max(-(-total // number_of), total * portions[0] // sum(portions)))
    least = 1 if total - largest >= number_of - 1 else 0
    holding, spare = [largest] + [least] * (number_of - 1), total - largest - least * (number_of - 1)
    while spare > 0:
        free = [i for i in range(1, number_of) if holding[i] < largest] or [i for i in range(1, number_of) if holding[i] < limit]
        pool, budget = sum([portions[i] for i in free]), spare
        for i in free:
            more = min(limit - holding[i], max(1, budget * portions[i] // pool), spare)
            holding[i] = holding[i] + more
            spare = spare - more
    return np.array(holding)


def centred(key, dims, spread, reach, shards=(), kind=jnp.bfloat16):
    loudness = block_scale(key, dims, shards, -0.22, 0.18) if shards else 1.0
    values = jax.random.normal(key, dims, jnp.float32) * spread * loudness
    return jnp.minimum(jnp.maximum(values, -reach), reach).astype(kind)


def setup_inputs(seed: int = 0) -> dict:
    keys = jax.random.split(jax.random.key(seed), 16)
    inputs = centred(keys[0], (TOKENS, D), 1.0, 6.0, ((0, 128),))
    attn_gain = jnp.clip(1.0 + 0.15 * jax.random.normal(keys[1], (D,), jnp.float32), 0.25, 1.75)
    w_query = centred(keys[2], (D, HEADS * HEAD), D ** -0.5, 0.125, ((1, 4),))
    w_key = centred(keys[3], (D, KV_HEADS * HEAD), D ** -0.5, 0.125, ((1, 4),))
    w_value = centred(keys[4], (D, KV_HEADS * HEAD), D ** -0.5, 0.125, ((1, 4),))
    q_gain = jnp.clip(1.0 + 0.15 * jax.random.normal(keys[5], (HEAD,), jnp.float32), 0.25, 1.75)
    k_gain = jnp.clip(1.0 + 0.15 * jax.random.normal(keys[6], (HEAD,), jnp.float32), 0.25, 1.75)
    w_out = centred(keys[7], (HEADS * HEAD, D), (HEADS * HEAD // 64) ** -0.5, 0.75, ((0, 4),))
    mlp_gain = jnp.clip(1.0 + 0.15 * jax.random.normal(keys[8], (D,), jnp.float32), 0.25, 1.75)
    w_router = centred(keys[9], (D, EXPERTS), (4 * D) ** -0.5, 0.0625)
    w_gate = centred(keys[10], (EXPERTS, D, FF), D ** -0.5, 0.125, ((0, 32), (2, 4)))
    w_up = centred(keys[11], (EXPERTS, D, FF), D ** -0.5, 0.125, ((0, 32), (2, 4)))
    w_down = centred(keys[12], (EXPERTS, FF, D), (FF // 16) ** -0.5, 0.875, ((0, 32), (1, 4)))
    routes_keys = jax.random.split(jax.random.fold_in(keys[13], 1), TOKENS // TOK_DEV)
    routes_turns = jax.random.permutation(jax.random.fold_in(keys[13], 3), TOKENS // TOK_DEV)
    routes = jax.vmap(lambda own, number: shared_out(jax.random.fold_in(keys[13], 2), own, number, TOK_DEV, EXPERTS, TOP, CAP, 2))(routes_keys, routes_turns).reshape((TOKENS, TOP))
    grad_out = centred(keys[14], (TOKENS, D), 1.0, 6.0, ((0, 128),))
    return dict(inputs=inputs, attn_gain=attn_gain, w_query=w_query, w_key=w_key, w_value=w_value, q_gain=q_gain, k_gain=k_gain, w_out=w_out, mlp_gain=mlp_gain, w_router=w_router, w_gate=w_gate, w_up=w_up, w_down=w_down, routes=routes, grad_out=grad_out)


EPSILON = 1e-06
ROPE_BASE = 1000000.0
MASK_VALUE = -1e+30
HIGHEST = lax.Precision.HIGHEST

@jax.custom_vjp
def low(v):
    return lax.optimization_barrier(v.astype(jnp.bfloat16)).astype(jnp.float32)

@jax.custom_vjp
def low_back(v):
    return v

def low_keep(v):
    return (low(v), None)

def low_pass(kept, grad):
    return (grad,)

def back_keep(v):
    return (v, None)

def back_low(kept, grad):
    return (low(grad),)
low.defvjp(low_keep, low_pass)
low_back.defvjp(back_keep, back_low)

def matmul(left, right):
    return jnp.dot(left, right, precision=HIGHEST)

def angles(length, head_size):
    position = jnp.arange(length, dtype=jnp.float32)[:, None]
    index_half = jnp.arange(head_size // 2, dtype=jnp.float32)[None, :]
    frequency = jnp.exp(index_half * (-2.0 / head_size) * jnp.log(ROPE_BASE))
    turned = position * frequency
    turned = jnp.concatenate([turned, turned], axis=1)
    return (jnp.cos(turned)[:, None, :], jnp.sin(turned)[:, None, :])

def rotate(values, cosine, sine):
    halfway = values.shape[-1] // 2
    turned = jnp.concatenate([-values[..., halfway:], values[..., :halfway]], axis=-1)
    return values * cosine + turned * sine

def rms_norm(values, gain):
    return values * lax.rsqrt(lax.optimization_barrier(jnp.mean(values * values, axis=-1, keepdims=True)) + EPSILON) * gain

def slot_table(routes):
    blocks = TOKENS // TOK_DEV
    per_block = TOK_DEV * TOP
    expert_ids = routes.reshape(blocks, per_block).astype(jnp.int32)
    onehot = (expert_ids[:, :, None] == jnp.arange(EXPERTS, dtype=jnp.int32)[None, None, :]).astype(jnp.int32)
    counted = jnp.cumsum(onehot, axis=1).astype(jnp.int32)
    slot_index = lax.optimization_barrier(jnp.sum(onehot * (counted - 1), axis=2)).astype(jnp.int32)
    block_ids = jnp.arange(blocks, dtype=jnp.int32)[:, None]
    row_place = (expert_ids * (blocks * CAP) + block_ids * CAP + slot_index).reshape(-1).astype(jnp.int32)
    owners = (jnp.arange(TOKENS * TOP, dtype=jnp.int32) // TOP).astype(jnp.int32)
    row_table = jnp.full((EXPERTS * blocks * CAP,), TOKENS, dtype=jnp.int32).at[row_place].set(owners)
    return (row_table.reshape(EXPERTS, blocks * CAP), row_place.reshape(TOKENS, TOP))

def forward_layer(arrays, row_table, row_place, chosen):
    inputs, attn_gain, w_query, w_key, w_value, q_gain, k_gain, w_out, mlp_gain, w_router, w_gate, w_up, w_down = arrays
    cosine, sine = angles(SEQ, HEAD)
    scale_factor = HEAD ** (-0.5)
    group_size = HEADS // KV_HEADS
    causal = jnp.arange(SEQ)[:, None] >= jnp.arange(SEQ)[None, :]

    def attend(sequence):
        normed = low(rms_norm(sequence, attn_gain))
        queries = low_back(matmul(normed, w_query)).reshape(SEQ, HEADS, HEAD)
        keys_raw = low_back(matmul(normed, w_key)).reshape(SEQ, KV_HEADS, HEAD)
        values_low = low_back(low(matmul(normed, w_value))).reshape(SEQ, KV_HEADS, HEAD)
        query_rot = low(rotate(rms_norm(queries, q_gain), cosine, sine)).reshape(SEQ, KV_HEADS, group_size, HEAD)
        key_rot = low(rotate(rms_norm(keys_raw, k_gain), cosine, sine))
        scores = low_back(jnp.einsum('skgd,tkd->kgst', query_rot, key_rot, precision=HIGHEST) * scale_factor)
        scores = jnp.where(causal, scores, MASK_VALUE)
        row_peak = lax.optimization_barrier(jnp.max(scores, axis=-1, keepdims=True))
        exp_scores = jnp.exp(scores - row_peak)
        attn_probs = exp_scores / lax.optimization_barrier(jnp.sum(exp_scores, axis=-1, keepdims=True))
        context = jnp.einsum('kgst,tkd->skgd', low(attn_probs), values_low, precision=HIGHEST).reshape(SEQ, HEADS * HEAD)
        context = low_back(low(context))
        return low_back(matmul(context, w_out))
    attended = lax.map(jax.checkpoint(attend), inputs.reshape(N_EXPERT, SEQ, D)).reshape(TOKENS, D)
    hidden = inputs + attended
    mixed_in = low(rms_norm(hidden, mlp_gain))
    logits = low_back(matmul(mixed_in, w_router))
    router_peak = lax.optimization_barrier(jnp.max(logits, axis=-1, keepdims=True))
    router_exp = jnp.exp(logits - router_peak)
    router_probs = router_exp / lax.optimization_barrier(jnp.sum(router_exp, axis=-1, keepdims=True))
    picked = lax.optimization_barrier(jnp.sum(chosen * router_probs[:, None, :], axis=-1))
    gate_values = picked / lax.optimization_barrier(jnp.sum(picked, axis=-1, keepdims=True))
    padded = jnp.concatenate([mixed_in, jnp.zeros((1, D), dtype=mixed_in.dtype)], axis=0)

    def expert(item):
        indices, gate_w, up_w, down_w = item
        taken = low_back(padded[indices])
        gate_pre = low_back(matmul(taken, gate_w))
        up_pre = low_back(matmul(taken, up_w))
        middle = low(gate_pre / (1.0 + jnp.exp(-gate_pre)) * up_pre)
        return low_back(low(matmul(middle, down_w)))
    produced = lax.map(jax.checkpoint(expert), (row_table, w_gate, w_up, w_down))
    flat_rows = produced.reshape(EXPERTS * row_table.shape[1], D)
    expert_mix = jnp.zeros_like(hidden)
    for pick_index in range(TOP):
        expert_mix = expert_mix + gate_values[:, pick_index:pick_index + 1] * flat_rows[row_place[:, pick_index]]
    return hidden + expert_mix

def reference(inputs, attn_gain, w_query, w_key, w_value, q_gain, k_gain, w_out, mlp_gain, w_router, w_gate, w_up, w_down, routes, grad_out):
    row_table, row_place = slot_table(routes)
    chosen = (routes[:, :, None] == jnp.arange(EXPERTS, dtype=jnp.int32)[None, None, :]).astype(jnp.float32)
    floats = [array_in.astype(jnp.float32) for array_in in (inputs, attn_gain, w_query, w_key, w_value, q_gain, k_gain, w_out, mlp_gain, w_router, w_gate, w_up, w_down)]

    def forward(*arrays):
        return forward_layer(arrays, row_table, row_place, chosen)
    result, pullback = jax.vjp(forward, *floats)
    gradients = pullback(grad_out.astype(jnp.float32))
    return (result.astype(jnp.bfloat16), gradients[0].astype(jnp.bfloat16), gradients[1], gradients[2], gradients[3], gradients[4], gradients[5], gradients[6], gradients[7], gradients[8], gradients[9], gradients[10], gradients[11], gradients[12])
```

```python
import functools

import jax
import jax.numpy as jnp
from jax import lax
from jax.experimental import pallas as pl
from jax.experimental.pallas import tpu as pltpu
from jax.sharding import PartitionSpec as P

MESH = pl.DeviceIdType.MESH


class Place:
    def __init__(self):
        e = lax.axis_index("expert")
        self.x = lax.axis_index("tensor")
        self.z = e // 8
        self.y = (e // 2) % 4
        self.core = e % 2

    def block(self, axis="z", a=0, b=0, other=0):
        dz, dy = (a, b) if axis == "z" else (b, a)
        core = (self.core + other) % 2
        return ((self.z + dz) % 4) * 8 + ((self.y + dy) % 4) * 2 + core

    def device(self, axis="z", a=0, b=0, other=0):
        return (self.block(axis, a, b, other), self.x)


def greet(devices):
    barrier = pltpu.get_barrier_semaphore()
    for device in devices:
        pl.semaphore_signal(barrier, inc=1, device_id=device, device_id_type=MESH)
    pl.semaphore_wait(barrier, len(devices))


def plane_neighbours(place):
    return [
        place.device("z", 1),
        place.device("z", -1),
        place.device("y", 1),
        place.device("y", -1),
        place.device(other=1),
    ]


OTHER = {"z": "y", "y": "z"}


def gather_plan():
    stages = [[], [], [], []]
    for half, first in ((0, "y"), (1, "z")):
        for side in (-1, 1):
            stages[0].append((first, half, side, 0, None, ("f", side)))
            stages[0].append((first, half, 0, side, None, ("s", side)))
    for half, first in ((0, "y"), (1, "z")):
        for quarter, side in ((0, -1), (1, 1)):
            stages[1].append((first, half, 2, 0, quarter, ("f", side)))
        for f in (-1, 1):
            for side in (-1, 1):
                stages[1].append((first, half, f, side, None, ("s", side)))
        for quarter, side in ((0, -1), (1, 1)):
            stages[1].append((first, half, 0, 2, quarter, ("s", side)))
    for half, first in ((0, "y"), (1, "z")):
        for quarter in (0, 1):
            for side in (-1, 1):
                stages[2].append((first, half, 2, side, quarter, ("s", side)))
        for f in (-1, 1):
            for quarter, side in ((0, -1), (1, 1)):
                stages[2].append((first, half, f, 2, quarter, ("s", side)))
    for half, first in ((0, "y"), (1, "z")):
        for quarter, side in ((0, -1), (1, 1)):
            stages[3].append((first, half, 2, 2, quarter, ("s", side)))
    return [piece for stage in stages for piece in stage]


PIECES = gather_plan()
PIECE_AT = {piece: at for at, piece in enumerate(PIECES)}


def gather_kernel(x_ref, out_ref, own_sem, send_sems, recv_sems, core_send, core_recv):
    place = Place()
    rows = x_ref.shape[0]
    greet(plane_neighbours(place))

    def span(half, quarter):
        if quarter is None:
            return pl.ds(half * (rows // 2), rows // 2)
        return pl.ds(half * (rows // 2) + quarter * (rows // 4), rows // 4)

    def view(piece):
        first, half, f, s, quarter, _ = piece
        return out_ref.at[place.block(first, f, s), span(half, quarter)]

    def sent(source, piece):
        first, half, f, s, quarter, (leg, side) = piece
        axis = first if leg == "f" else OTHER[first]
        f_here, s_here = (f - side, s) if leg == "f" else (f, s - side)
        at = PIECE_AT[piece]
        return pltpu.make_async_remote_copy(
            src_ref=source,
            dst_ref=out_ref.at[place.block(first, f_here, s_here), span(half, quarter)],
            send_sem=send_sems.at[at],
            recv_sem=recv_sems.at[at],
            device_id=place.device(axis, -side),
            device_id_type=MESH,
        )

    def to_core(at, block, where, source):
        return pltpu.make_async_remote_copy(
            src_ref=source,
            dst_ref=out_ref.at[block, where],
            send_sem=core_send.at[at],
            recv_sem=core_recv.at[at],
            device_id=place.device(other=1),
            device_id_type=MESH,
        )

    own = pltpu.make_async_copy(x_ref, out_ref.at[place.block()], own_sem)
    own.start()
    started = []

    def forward(piece_here, targets):
        for target in targets:
            first, half, f, s, quarter, (leg, side) = target
            if piece_here is None:
                source = x_ref.at[span(half, quarter)]
            else:
                f_here, s_here = (f - side, s) if leg == "f" else (f, s - side)
                source = out_ref.at[place.block(first, f_here, s_here), span(half, quarter)]
            copy = sent(source, target)
            copy.start()
            started.append(copy)

    for piece in PIECES[:8]:
        forward(None, [piece])
    whole = to_core(len(PIECES), place.block(), pl.ds(0, rows), x_ref)
    whole.start()
    core_copies = [whole]

    for at, piece in enumerate(PIECES):
        first, half, f, s, quarter, (leg, side) = piece
        pltpu.make_async_remote_copy(
            src_ref=view(piece),
            dst_ref=view(piece),
            send_sem=send_sems.at[at],
            recv_sem=recv_sems.at[at],
            device_id=place.device(first, 1),
            device_id_type=MESH,
        ).wait_recv()
        next_pieces = []
        for target in PIECES:
            t_first, t_half, t_f, t_s, t_quarter, (t_leg, t_side) = target
            if t_half != half:
                continue
            back = (t_f - t_side, t_s) if t_leg == "f" else (t_f, t_s - t_side)
            if back == (0, 0) or back != (f, s):
                alt = None
                if t_leg == "f" and t_f == 2 and leg == "f" and f == t_side and s == 0 and t_s == 0:
                    alt = True
                if t_leg == "s" and t_s == 2 and s == t_side and f == t_f:
                    alt = True
                if alt is None:
                    continue
            if t_leg == "s" and t_s in (-1, 1) and not (s == 0 and f == t_f):
                continue
            if quarter is not None and t_quarter != quarter:
                continue
            next_pieces.append(target)
        for target in next_pieces:
            t_first, t_half, t_f, t_s, t_quarter, (t_leg, t_side) = target
            axis = t_first if t_leg == "f" else OTHER[t_first]
            here = out_ref.at[place.block(first, f, s), span(t_half, t_quarter)]
            copy = pltpu.make_async_remote_copy(
                src_ref=here,
                dst_ref=here,
                send_sem=send_sems.at[PIECE_AT[target]],
                recv_sem=recv_sems.at[PIECE_AT[target]],
                device_id=place.device(axis, -t_side),
                device_id_type=MESH,
            )
            copy.start()
            started.append(copy)
        core_copy = to_core(at, place.block(first, f, s), span(half, quarter), view(piece))
        core_copy.start()
        core_copies.append(core_copy)
    assert len(started) == len(PIECES), (len(started), len(PIECES))
    for copy in started:
        copy.wait_send()
    for at, piece in enumerate(PIECES):
        first, half, f, s, quarter, _ = piece
        there = out_ref.at[place.block(first, f, s, 1), span(half, quarter)]
        pltpu.make_async_remote_copy(
            src_ref=view(piece), dst_ref=there, send_sem=core_send.at[at],
            recv_sem=core_recv.at[at], device_id=place.device(other=1), device_id_type=MESH,
        ).wait()
    pltpu.make_async_remote_copy(
        src_ref=x_ref, dst_ref=out_ref.at[place.block(other=1)], send_sem=core_send.at[len(PIECES)],
        recv_sem=core_recv.at[len(PIECES)], device_id=place.device(other=1), device_id_type=MESH,
    ).wait()
    own.wait()


def gather_plane(x, collective_id):
    count = len(PIECES)
    return pl.pallas_call(
        gather_kernel,
        out_shape=jax.ShapeDtypeStruct((32, *x.shape), x.dtype),
        in_specs=[pl.BlockSpec(memory_space=pl.ANY)],
        out_specs=pl.BlockSpec(memory_space=pl.ANY),
        scratch_shapes=[
            pltpu.SemaphoreType.DMA,
            pltpu.SemaphoreType.DMA((count,)),
            pltpu.SemaphoreType.DMA((count,)),
            pltpu.SemaphoreType.DMA((count + 1,)),
            pltpu.SemaphoreType.DMA((count + 1,)),
        ],
        compiler_params=pltpu.CompilerParams(collective_id=collective_id, has_side_effects=True),
        name="gather_plane",
    )(x)


def scatter_kernel(
    c_ref, out_ref, held, other, in_a, in_b, in_c, in_d,
    load_sems, core_send, core_recv, send_sems, recv_sems,
):
    place = Place()
    rows = c_ref.shape[1]
    half_rows, quarter_rows = rows // 2, rows // 4
    greet(plane_neighbours(place))
    order = [(2, 2), (2, 1), (1, 2), (2, 3), (3, 2), (2, 0), (0, 2)]
    order += [(1, 1), (1, 3), (3, 1), (3, 3), (1, 0), (0, 1), (3, 0), (0, 3), (0, 0)]
    loads, cores = {}, {}
    for dz, dy in order:
        at = dz * 4 + dy
        cores[at] = pltpu.make_async_remote_copy(
            src_ref=c_ref.at[place.block("z", dz, dy, 1)],
            dst_ref=other.at[at],
            send_sem=core_send.at[at],
            recv_sem=core_recv.at[at],
            device_id=place.device(other=1),
            device_id_type=MESH,
        )
        cores[at].start()
        loads[at] = pltpu.make_async_copy(
            c_ref.at[place.block("z", dz, dy)], held.at[at], load_sems.at[at]
        )
        loads[at].start()
    ready = set()

    def slot(axis, a, b):
        dz, dy = (a, b) if axis == "z" else (b, a)
        return (dz % 4) * 4 + dy % 4

    def add_rows(into, at, start, count, source, s_at):
        @pl.loop(0, count, step=16)
        def _(row):
            here = (at, pl.ds(start + row, 16))
            there = (*s_at, pl.ds(row, 16))
            total = into[here].astype(jnp.float32) + source[there].astype(jnp.float32)
            into[here] = total.astype(jnp.bfloat16)

    def make_ready(at):
        if at in ready:
            return
        ready.add(at)
        loads[at].wait()
        cores[at].wait_recv()
        add_rows(held, at, 0, rows, other, (at,))

    sent = []

    def send(source, target, number, device):
        copy = pltpu.make_async_remote_copy(
            src_ref=source, dst_ref=target, send_sem=send_sems.at[number],
            recv_sem=recv_sems.at[number], device_id=device, device_id_type=MESH,
        )
        copy.start()
        sent.append(copy)

    def arrive(target, number):
        pltpu.make_async_remote_copy(
            src_ref=target, dst_ref=target, send_sem=send_sems.at[number],
            recv_sem=recv_sems.at[number], device_id=place.device("z", 1), device_id_type=MESH,
        ).wait_recv()

    axes = (("z", "y"), ("y", "z"))
    lines = (2, 1, 3, 0)
    for line in lines:
        for half, (first, second) in enumerate(axes):
            at = slot(first, 2, line)
            make_ready(at)
            for quarter, side in ((0, 1), (1, -1)):
                where = pl.ds(half * half_rows + quarter * quarter_rows, quarter_rows)
                send(held.at[at, where], in_a.at[half, line, quarter],
                     ((half * 4 + line) * 2 + quarter), place.device(first, side))
    for line in lines:
        for half, (first, second) in enumerate(axes):
            for quarter, side in ((0, 1), (1, -1)):
                at = slot(first, side, line)
                make_ready(at)
                number = (half * 4 + line) * 2 + quarter
                arrive(in_a.at[half, line, quarter], number)
                add_rows(held, at, half * half_rows + quarter * quarter_rows, quarter_rows,
                         in_a, (half, line, quarter))
                send(held.at[at, pl.ds(half * half_rows, half_rows)],
                     in_b.at[half, line, quarter], 16 + number, place.device(first, side))
    for line in lines:
        for half, (first, second) in enumerate(axes):
            at = slot(first, 0, line)
            make_ready(at)
            for quarter in (0, 1):
                number = (half * 4 + line) * 2 + quarter
                arrive(in_b.at[half, line, quarter], 16 + number)
                add_rows(held, at, half * half_rows, half_rows, in_b, (half, line, quarter))
            if line == 2:
                for quarter, side in ((0, 1), (1, -1)):
                    where = pl.ds(half * half_rows + quarter * quarter_rows, quarter_rows)
                    send(held.at[at, where], in_c.at[half, quarter],
                         32 + half * 2 + quarter, place.device(second, side))
            if line in (1, 3):
                quarter, side = (0, 1) if line == 1 else (1, -1)
                number = 32 + half * 2 + quarter
                arrive(in_c.at[half, quarter], number)
                add_rows(held, at, half * half_rows + quarter * quarter_rows, quarter_rows,
                         in_c, (half, quarter))
                send(held.at[at, pl.ds(half * half_rows, half_rows)], in_d.at[half, quarter],
                     36 + half * 2 + quarter, place.device(second, side))
    for half in (0, 1):
        for quarter in (0, 1):
            arrive(in_d.at[half, quarter], 36 + half * 2 + quarter)

        @pl.loop(0, half_rows, step=16)
        def _(row):
            here = pl.ds(half * half_rows + row, 16)
            total = held[0, here].astype(jnp.float32)
            for quarter in (0, 1):
                total = total + in_d[half, quarter, pl.ds(row, 16)].astype(jnp.float32)
            out_ref[here] = total
    for copy in sent:
        copy.wait_send()
    for at in cores:
        cores[at].wait_send()


def scatter_plane(c, collective_id):
    _, rows, width = c.shape
    bf16 = jnp.bfloat16
    return pl.pallas_call(
        scatter_kernel,
        out_shape=jax.ShapeDtypeStruct((rows, width), jnp.float32),
        in_specs=[pl.BlockSpec(memory_space=pl.ANY)],
        out_specs=pl.BlockSpec(memory_space=pltpu.VMEM),
        scratch_shapes=[
            pltpu.VMEM((16, rows, width), bf16),
            pltpu.VMEM((16, rows, width), bf16),
            pltpu.VMEM((2, 4, 2, rows // 4, width), bf16),
            pltpu.VMEM((2, 4, 2, rows // 2, width), bf16),
            pltpu.VMEM((2, 2, rows // 4, width), bf16),
            pltpu.VMEM((2, 2, rows // 2, width), bf16),
            pltpu.SemaphoreType.DMA((16,)),
            pltpu.SemaphoreType.DMA((16,)),
            pltpu.SemaphoreType.DMA((16,)),
            pltpu.SemaphoreType.DMA((40,)),
            pltpu.SemaphoreType.DMA((40,)),
        ],
        compiler_params=pltpu.CompilerParams(
            collective_id=collective_id, has_side_effects=True, vmem_limit_bytes=48 * 2**20
        ),
        name="scatter_plane",
    )(c)


def line_neighbours(place):
    e = place.block()
    return [(e, (place.x + 1) % 4), (e, (place.x + 3) % 4)]


def line_gather_kernel(x_ref, out_ref, own_sem, send_sems, recv_sems):
    place = Place()
    rows = x_ref.shape[0]
    after, before = line_neighbours(place)
    greet([after, before])
    own = pltpu.make_async_copy(x_ref, out_ref.at[place.x], own_sem)
    own.start()

    def copy(source, block, where, number, device):
        return pltpu.make_async_remote_copy(
            src_ref=source, dst_ref=out_ref.at[block, where], send_sem=send_sems.at[number],
            recv_sem=recv_sems.at[number], device_id=device, device_id_type=MESH,
        )

    every, low, high = pl.ds(0, rows), pl.ds(0, rows // 2), pl.ds(rows // 2, rows // 2)
    first = [copy(x_ref, place.x, every, 0, after), copy(x_ref, place.x, every, 1, before)]
    for c in first:
        c.start()
    left, right, far = (place.x + 3) % 4, (place.x + 1) % 4, (place.x + 2) % 4
    copy(x_ref, left, every, 0, after).wait_recv()
    third = copy(out_ref.at[left, low], left, low, 2, after)
    third.start()
    copy(x_ref, right, every, 1, before).wait_recv()
    fourth = copy(out_ref.at[right, high], right, high, 3, before)
    fourth.start()
    copy(out_ref.at[far, low], far, low, 2, after).wait_recv()
    copy(out_ref.at[far, high], far, high, 3, before).wait_recv()
    for c in (*first, third, fourth):
        c.wait_send()
    own.wait()


def gather_line(x, collective_id):
    return pl.pallas_call(
        line_gather_kernel,
        out_shape=jax.ShapeDtypeStruct((4, *x.shape), x.dtype),
        in_specs=[pl.BlockSpec(memory_space=pl.ANY)],
        out_specs=pl.BlockSpec(memory_space=pl.ANY),
        scratch_shapes=[
            pltpu.SemaphoreType.DMA,
            pltpu.SemaphoreType.DMA((4,)),
            pltpu.SemaphoreType.DMA((4,)),
        ],
        compiler_params=pltpu.CompilerParams(collective_id=collective_id, has_side_effects=True),
        name="gather_line",
    )(x)


def line_scatter_kernel(c_ref, out_ref, in_a, in_b, send_sems, recv_sems):
    place = Place()
    rows = c_ref.shape[1]
    after, before = line_neighbours(place)
    left, right, far = (place.x + 3) % 4, (place.x + 1) % 4, (place.x + 2) % 4
    half = rows // 2
    greet([after, before])

    def copy(source, target, number, device):
        return pltpu.make_async_remote_copy(
            src_ref=source, dst_ref=target, send_sem=send_sems.at[number],
            recv_sem=recv_sems.at[number], device_id=device, device_id_type=MESH,
        )

    copies = [
        copy(c_ref.at[far, pl.ds(0, half)], in_a.at[0], 0, after),
        copy(c_ref.at[far, pl.ds(half, half)], in_a.at[1], 1, before),
    ]
    for c in copies:
        c.start()

    def add(block, start, source):
        @pl.loop(0, half, step=16)
        def _(row):
            here = (block, pl.ds(start + row, 16))
            total = c_ref[here].astype(jnp.float32) + source[pl.ds(row, 16)].astype(jnp.float32)
            c_ref[here] = total.astype(jnp.bfloat16)

    copies[0].wait_recv()
    add(right, 0, in_a.at[0])
    copies.append(copy(c_ref.at[right], in_b.at[0], 2, after))
    copies[2].start()
    copies[1].wait_recv()
    add(left, half, in_a.at[1])
    copies.append(copy(c_ref.at[left], in_b.at[1], 3, before))
    copies[3].start()
    copies[2].wait_recv()
    copies[3].wait_recv()

    @pl.loop(0, rows, step=16)
    def _(row):
        here = pl.ds(row, 16)
        total = c_ref[place.x, here].astype(jnp.float32) + in_b[0, here].astype(jnp.float32)
        out_ref[here] = total + in_b[1, here].astype(jnp.float32)

    for c in copies:
        c.wait_send()


def line_scatter_outer(c_ref, out_ref, held, load_sem, *rest):
    load = pltpu.make_async_copy(c_ref, held, load_sem)
    load.start()
    load.wait()
    line_scatter_kernel(held, out_ref, *rest)


def scatter_line(c, collective_id):
    _, rows, width = c.shape
    return pl.pallas_call(
        line_scatter_outer,
        out_shape=jax.ShapeDtypeStruct((rows, width), jnp.float32),
        in_specs=[pl.BlockSpec(memory_space=pl.ANY)],
        out_specs=pl.BlockSpec(memory_space=pltpu.VMEM),
        scratch_shapes=[
            pltpu.VMEM((4, rows, width), jnp.bfloat16),
            pltpu.SemaphoreType.DMA,
            pltpu.VMEM((2, rows // 2, width), jnp.bfloat16),
            pltpu.VMEM((2, rows, width), jnp.bfloat16),
            pltpu.SemaphoreType.DMA((4,)),
            pltpu.SemaphoreType.DMA((4,)),
        ],
        compiler_params=pltpu.CompilerParams(
            collective_id=collective_id, has_side_effects=True, vmem_limit_bytes=16 * 2**20
        ),
        name="scatter_line",
    )(c)


SLOTS = 80
NT = (((1,), (1,)), ((), ()))
TN = (((0,), (0,)), ((), ()))
NN = (((1,), (0,)), ((), ()))


def dot(left, right, dims):
    return lax.dot_general(left, right, dims, preferred_element_type=jnp.float32)


def chosen_rows(slots, first):
    value = slots.astype(jnp.float32)
    lane = lax.broadcasted_iota(jnp.int32, value.shape, 1)
    slot = lax.broadcasted_iota(jnp.int32, (value.shape[0], 2 * SLOTS), 1).astype(jnp.float32)
    found = []
    for j in range(2):
        mine = jnp.sum(jnp.where(lane == first + j, value, 0.0), axis=1, keepdims=True)
        found.append(jnp.where(mine >= 0.0, mine + float(j * SLOTS), -1.0))
    return jnp.where((slot == found[0]) | (slot == found[1]), 1.0, 0.0).astype(jnp.bfloat16)


def select_kernel(first_ref, tokens_ref, slots_ref, a_ref, b_ref, gate_a_ref, gate_b_ref):
    first = first_ref[0]
    table = chosen_rows(slots_ref[...], first)
    width = a_ref.shape[1]
    rows = dot(table, tokens_ref[...], TN)
    a_ref[...] = rows[:SLOTS, :width].astype(jnp.bfloat16)
    b_ref[...] = rows[SLOTS:, :width].astype(jnp.bfloat16)
    tail = rows[:, width:]
    lane = lax.broadcasted_iota(jnp.int32, tail.shape, 1) % 64
    for j, ref in enumerate((gate_a_ref, gate_b_ref)):
        part = tail[j * SLOTS : (j + 1) * SLOTS]
        mine = lane[j * SLOTS : (j + 1) * SLOTS] == first + j
        gate = jnp.sum(jnp.where(mine, part, 0.0), axis=1, keepdims=True)
        ref[...] = jnp.broadcast_to(gate, ref.shape)


def select_rows(first, tokens, slot_source):
    count, full = tokens.shape
    width = full - 128
    groups = count // 512
    out = jax.ShapeDtypeStruct((groups * SLOTS, width), jnp.bfloat16)
    gate = jax.ShapeDtypeStruct((groups * SLOTS, 128), jnp.float32)
    return pl.pallas_call(
        select_kernel,
        grid=(groups,),
        out_shape=(out, out, gate, gate),
        in_specs=[
            pl.BlockSpec(memory_space=pltpu.SMEM),
            pl.BlockSpec((512, full), lambda i: (i, 0)),
            pl.BlockSpec((512, 128), lambda i: (i, width // 128)),
        ],
        out_specs=(
            pl.BlockSpec((SLOTS, width), lambda i: (i, 0)),
            pl.BlockSpec((SLOTS, width), lambda i: (i, 0)),
            pl.BlockSpec((SLOTS, 128), lambda i: (i, 0)),
            pl.BlockSpec((SLOTS, 128), lambda i: (i, 0)),
        ),
        compiler_params=pltpu.CompilerParams(vmem_limit_bytes=24 * 2**20),
        cost_estimate=pl.CostEstimate(
            flops=2 * count * 160 * full, bytes_accessed=count * full * 2 + groups * 160 * full * 2,
            transcendentals=0,
        ),
        name="select_rows",
    )(first, tokens, slot_source)


def combine_kernel(first_ref, a_ref, b_ref, slots_ref, out_ref):
    table = chosen_rows(slots_ref[...], first_ref[0])
    rows = jnp.concatenate([a_ref[...], b_ref[...]], axis=0)
    out_ref[...] = dot(table, rows, NN).astype(jnp.bfloat16)


def combine_rows(first, rows_a, rows_b, slot_source):
    width = rows_a.shape[1]
    groups = rows_a.shape[0] // SLOTS
    lanes = slot_source.shape[1] // 128 - 1
    return pl.pallas_call(
        combine_kernel,
        grid=(groups,),
        out_shape=jax.ShapeDtypeStruct((groups * 512, width), jnp.bfloat16),
        in_specs=[
            pl.BlockSpec(memory_space=pltpu.SMEM),
            pl.BlockSpec((SLOTS, width), lambda i: (i, 0)),
            pl.BlockSpec((SLOTS, width), lambda i: (i, 0)),
            pl.BlockSpec((512, 128), lambda i: (i, lanes)),
        ],
        out_specs=pl.BlockSpec((512, width), lambda i: (i, 0)),
        compiler_params=pltpu.CompilerParams(vmem_limit_bytes=24 * 2**20),
        cost_estimate=pl.CostEstimate(
            flops=2 * groups * 512 * 160 * width,
            bytes_accessed=(groups * 512 + groups * 160) * width * 2, transcendentals=0,
        ),
        name="combine_rows",
    )(first, rows_a, rows_b, slot_source)


def expert_kernel(
    expert_ref, own_ref, left_ref, right_ref, far0_ref, far1_ref, x_hbm, d_hbm, gate_hbm,
    p_hbm, rb_hbm, gw_hbm,
    w, x, d, gate, rg, middle, ggp, gup, p, rb, dots, turned, gw, in_sems, out_sems, gw_sems,
):
    f32, bf16 = jnp.float32, jnp.bfloat16
    rows, width = x.shape
    hidden = middle.shape[1]
    chunk = 256
    shard = own_ref.shape[1]
    loads = [
        pltpu.make_async_copy(x_hbm, x, in_sems.at[0]),
        pltpu.make_async_copy(d_hbm, d, in_sems.at[1]),
        pltpu.make_async_copy(gate_hbm, gate, in_sems.at[2]),
    ]
    at = 0
    for i, ref in enumerate((own_ref, left_ref, right_ref, far0_ref, far1_ref)):
        size = ref.shape[1]
        loads.append(pltpu.make_async_copy(ref, w.at[:, pl.ds(at, size)], in_sems.at[3 + i]))
        at += size
    for load in loads:
        load.start()
    for load in loads:
        load.wait()

    @pl.loop(0, rows, step=16)
    def _(r):
        here = pl.ds(r, 16)
        scaled = d[here].astype(f32) * gate[here, 0:1]
        rg[here] = scaled.astype(bf16)

    for c in range(0, hidden, chunk):
        here = pl.ds(c, chunk)
        gate_pre = dot(x[...], w[0, here], NT)
        up_pre = dot(x[...], w[1, here], NT)
        grad_mid = dot(rg[...], w[2, here], NT)
        sig = 1.0 / (1.0 + jnp.exp(-gate_pre))
        act = gate_pre * sig
        middle[:, here] = (act * up_pre).astype(bf16)
        ggp[:, here] = (grad_mid * up_pre * sig * (1.0 + gate_pre * (1.0 - sig))).astype(bf16)
        gup[:, here] = (grad_mid * act).astype(bf16)

    dots[...] = jnp.zeros_like(dots)

    for n in range(0, width, chunk):
        here = pl.ds(n, chunk)
        out = dot(middle[...], w[2, :, here], NN).astype(bf16).astype(f32)
        p[:, here] = (out * gate[:, 0:1]).astype(bf16)
        along = out * d[:, here].astype(f32)
        dots[...] += along[:, :128] + along[:, 128:]
        back = dot(ggp[...], w[0, :, here], NN) + dot(gup[...], w[1, :, here], NN)
        rb[:, here] = back.astype(bf16)

    expert = expert_ref[0]
    total = jnp.sum(dots[...], axis=1, keepdims=True)
    high = total.astype(bf16).astype(f32)
    lane = lax.broadcasted_iota(jnp.int32, (rows, 128), 1)
    tail = jnp.where(lane == expert, high, jnp.where(lane == expert + 64, total - high, 0.0))
    rb[:, pl.ds(width, 128)] = tail.astype(bf16)
    outs = [
        pltpu.make_async_copy(rb, rb_hbm, out_sems.at[0]),
        pltpu.make_async_copy(p, p_hbm, out_sems.at[1]),
    ]
    for out in outs:
        out.start()

    for i, (left, right) in enumerate(((ggp, x), (gup, x), (middle, rg))):
        turned[...] = left[...].T

        for c in range(0, hidden, chunk):
            here = pl.ds(c, chunk)
            for n in range(0, width, 512):
                there = pl.ds(n, 512)
                gw[i, here, there] = dot(turned[here], right[:, there], NN).astype(bf16)

        save = pltpu.make_async_copy(gw.at[i], gw_hbm.at[i], gw_sems.at[i])
        save.start()
        outs.append(save)
    for out in outs:
        out.wait()


def expert_layer(expert, weights, x, d, gate):
    bf16 = jnp.bfloat16
    rows, width = x.shape
    hidden = sum(part.shape[1] for part in weights)
    any_spec = pl.BlockSpec(memory_space=pl.ANY)
    return pl.pallas_call(
        expert_kernel,
        out_shape=(
            jax.ShapeDtypeStruct((rows, width), bf16),
            jax.ShapeDtypeStruct((rows, width + 128), bf16),
            jax.ShapeDtypeStruct((3, hidden, width), bf16),
        ),
        in_specs=[pl.BlockSpec(memory_space=pltpu.SMEM)] + [any_spec] * 8,
        out_specs=(any_spec, any_spec, any_spec),
        scratch_shapes=[
            pltpu.VMEM((3, hidden, width), bf16),
            pltpu.VMEM((rows, width), bf16),
            pltpu.VMEM((rows, width), bf16),
            pltpu.VMEM((rows, 128), jnp.float32),
            pltpu.VMEM((rows, width), bf16),
            pltpu.VMEM((rows, hidden), bf16),
            pltpu.VMEM((rows, hidden), bf16),
            pltpu.VMEM((rows, hidden), bf16),
            pltpu.VMEM((rows, width), bf16),
            pltpu.VMEM((rows, width + 128), bf16),
            pltpu.VMEM((rows, 128), jnp.float32),
            pltpu.VMEM((hidden, rows), bf16),
            pltpu.VMEM((3, hidden, width), bf16),
            pltpu.SemaphoreType.DMA((8,)),
            pltpu.SemaphoreType.DMA((2,)),
            pltpu.SemaphoreType.DMA((3,)),
        ],
        compiler_params=pltpu.CompilerParams(vmem_limit_bytes=56 * 2**20),
        cost_estimate=pl.CostEstimate(
            flops=18 * rows * hidden * width,
            bytes_accessed=12 * hidden * width + 10 * rows * width,
            transcendentals=rows * hidden,
        ),
        name="expert_layer",
    )(expert, *weights, x, d, gate)


EPSILON = 1e-06
ROPE_BASE = 1000000.0
MASK_VALUE = -1e30
F32 = jnp.float32
BF16 = jnp.bfloat16


def angles(length, head_size):
    position = jnp.arange(length, dtype=jnp.float32)[:, None]
    index_half = jnp.arange(head_size // 2, dtype=jnp.float32)[None, :]
    frequency = jnp.exp(index_half * (-2.0 / head_size) * jnp.log(ROPE_BASE))
    turned = position * frequency
    turned = jnp.concatenate([turned, turned], axis=1)
    return (jnp.cos(turned)[:, None, :], jnp.sin(turned)[:, None, :])


def rotate(values, cosine, sine):
    halfway = values.shape[-1] // 2
    turned = jnp.concatenate([-values[..., halfway:], values[..., :halfway]], axis=-1)
    return values * cosine + turned * sine


def rotate_back(grads, cosine, sine):
    halfway = grads.shape[-1] // 2
    along = grads * sine
    return grads * cosine + jnp.concatenate([along[..., halfway:], -along[..., :halfway]], axis=-1)


def inverse_rms(values):
    return lax.rsqrt(jnp.mean(values * values, axis=-1, keepdims=True) + EPSILON)


def norm_back(values, scales, gain, grads):
    weighted = grads * gain
    return scales * weighted - values * scales * scales * scales * jnp.mean(
        weighted * values, axis=-1, keepdims=True
    )


def along_line(value, step):
    return lax.ppermute(value, "tensor", [(i, (i + step) % 4) for i in range(4)])


def line_weights(own):
    half = own.shape[1] // 2
    left = along_line(own, 1)
    right = along_line(own, -1)
    far_low = along_line(left[:, :half], 1)
    far_high = along_line(right[:, half:], -1)
    return (own, left, right, far_low, far_high)


def line_grads(grads):
    shard = grads.shape[1] // 4
    half = shard // 2
    far = 3 * shard
    low = along_line(grads[:, far : far + half], -1)
    high = along_line(grads[:, far + half :], 1)

    def plus(a, b):
        return (a.astype(F32) + b.astype(F32)).astype(BF16)

    left = jnp.concatenate(
        [plus(grads[:, shard : shard + half], low), grads[:, shard + half : 2 * shard]], axis=1
    )
    right = jnp.concatenate(
        [grads[:, 2 * shard : 2 * shard + half], plus(grads[:, 2 * shard + half : far], high)], axis=1
    )
    from_right = along_line(left, -1)
    from_left = along_line(right, 1)
    return grads[:, :shard].astype(F32) + from_right.astype(F32) + from_left.astype(F32)


def per_device(
    inputs,
    attn_gain,
    w_query,
    w_key,
    w_value,
    q_gain,
    k_gain,
    w_out,
    mlp_gain,
    w_router,
    w_gate,
    w_up,
    w_down,
    routes,
    grad_out,
):
    f32, bf16 = F32, BF16
    row_count, model_width = inputs.shape
    head_size = q_gain.shape[0]
    expert_count = w_router.shape[1]
    query_heads = w_query.shape[1] // head_size
    key_heads = w_key.shape[1] // head_size
    group_size = query_heads // key_heads
    scale_factor = head_size ** (-0.5)
    place = lax.axis_index("expert")
    first = (2 * place).astype(jnp.int32).reshape(1)

    chosen = routes[:, :, None] == jnp.arange(expert_count, dtype=jnp.int32)[None, None, :]
    picks = jnp.sum(chosen.astype(f32), axis=1)
    before = (jnp.arange(row_count)[:, None] > jnp.arange(row_count)[None, :]).astype(bf16)
    rank = jnp.dot(before, picks.astype(bf16), preferred_element_type=f32)
    slots = jnp.where(picks > 0.0, rank + (20 * (place % 4)).astype(f32), -1.0)
    slots = jnp.concatenate([slots, jnp.full_like(slots, -1.0)], axis=1).astype(bf16)
    dout_all = lax.all_gather(
        jnp.concatenate([grad_out, slots], axis=1), "expert", axis=0, tiled=True
    )

    float_in = inputs.astype(f32)
    first_scale = inverse_rms(float_in)
    normed = (float_in * first_scale * attn_gain).astype(bf16)
    seq_rows = gather_line(normed, 0).reshape(-1, model_width)

    gate_t = jnp.swapaxes(w_gate, 1, 2)
    up_t = jnp.swapaxes(w_up, 1, 2)
    own = [jnp.stack([gate_t[j], up_t[j], w_down[j]]) for j in range(2)]
    seq_rows, own[0], own[1] = lax.optimization_barrier((seq_rows, own[0], own[1]))
    weights = [line_weights(part) for part in own]

    length = seq_rows.shape[0]
    queries = jnp.dot(seq_rows, w_query, preferred_element_type=f32).reshape(
        length, query_heads, head_size
    )
    keys_raw = jnp.dot(seq_rows, w_key, preferred_element_type=f32).reshape(
        length, key_heads, head_size
    )
    values_low = (
        jnp.dot(seq_rows, w_value, preferred_element_type=f32)
        .astype(bf16)
        .reshape(length, key_heads, head_size)
    )
    cosine, sine = angles(length, head_size)
    query_scale = inverse_rms(queries)
    key_scale = inverse_rms(keys_raw)
    query_rot = rotate(queries * query_scale * q_gain, cosine, sine).astype(bf16)
    key_rot = rotate(keys_raw * key_scale * k_gain, cosine, sine).astype(bf16)
    query_group = query_rot.reshape(length, key_heads, group_size, head_size)
    causal = jnp.arange(length)[:, None] >= jnp.arange(length)[None, :]
    scores = (
        jnp.einsum("skgd,tkd->kgst", query_group, key_rot, preferred_element_type=f32)
        * scale_factor
    )
    scores = jnp.where(causal, scores, MASK_VALUE)
    row_peak = jnp.max(scores, axis=-1, keepdims=True)
    exp_scores = jnp.exp(scores - row_peak)
    denominator = jnp.sum(exp_scores, axis=-1, keepdims=True)
    attn_probs = exp_scores / denominator
    log_norm = row_peak + jnp.log(denominator)
    context = jnp.einsum(
        "kgst,tkd->skgd", attn_probs.astype(bf16), values_low, preferred_element_type=f32
    )
    context = context.reshape(length, query_heads * head_size).astype(bf16)
    partial = jnp.dot(context, w_out, preferred_element_type=f32).astype(bf16)
    attended = scatter_line(partial.reshape(4, row_count, model_width), 1)

    hidden = float_in + attended
    second_scale = inverse_rms(hidden)
    mixed_in = (hidden * second_scale * mlp_gain).astype(bf16)
    logits = jnp.dot(mixed_in, w_router, preferred_element_type=f32)
    router_peak = jnp.max(logits, axis=-1, keepdims=True)
    router_exp = jnp.exp(logits - router_peak)
    router_probs = router_exp / jnp.sum(router_exp, axis=-1, keepdims=True)
    picked_total = jnp.sum(picks * router_probs, axis=-1, keepdims=True)
    gate_values = picks * router_probs / picked_total
    gate_high = gate_values.astype(bf16)
    gate_low = (gate_values - gate_high.astype(f32)).astype(bf16)

    mixed_all = gather_plane(jnp.concatenate([mixed_in, gate_high, gate_low], axis=1), 2)
    mixed_all = mixed_all.reshape(-1, model_width + 128)
    grad_a, grad_b, _, _ = select_rows(first, dout_all, dout_all)
    rows_a, rows_b, gate_a, gate_b = select_rows(first, mixed_all, dout_all)
    out_a, back_a, gw_a = expert_layer(first, weights[0], rows_a, grad_a, gate_a)
    out_b, back_b, gw_b = expert_layer(first + 1, weights[1], rows_b, grad_b, gate_b)
    back = combine_rows(first, back_a, back_b, dout_all)
    shares = combine_rows(first, out_a, out_b, dout_all)
    back = scatter_plane(back.reshape(-1, row_count, model_width + 128), 3)
    expert_mix = lax.psum_scatter(shares, "expert", scatter_dimension=0, tiled=True)
    output = (hidden + expert_mix.astype(f32)).astype(bf16)
    gw_a = line_grads(gw_a)
    gw_b = line_grads(gw_b)

    dout = grad_out.astype(f32)
    tail = back[:, model_width:]
    gate_grad = tail[:, :expert_count] + tail[:, expert_count:]
    prob_grad = (
        picks
        * (gate_grad - jnp.sum(gate_grad * gate_values, axis=-1, keepdims=True))
        / picked_total
    )
    logit_grad = (
        router_probs * (prob_grad - jnp.sum(prob_grad * router_probs, axis=-1, keepdims=True))
    ).astype(bf16)
    grad_router = jnp.dot(mixed_in.T, logit_grad, preferred_element_type=f32)
    grad_mixed = back[:, :model_width] + jnp.dot(
        logit_grad, w_router.T, preferred_element_type=f32
    )
    grad_hidden = dout + norm_back(hidden, second_scale, mlp_gain, grad_mixed)
    mlp_gain_grad = jnp.sum(grad_mixed * hidden * second_scale, axis=0)
    grad_router, mlp_gain_grad = lax.psum((grad_router, mlp_gain_grad), ("expert", "tensor"))

    grad_att = grad_hidden.astype(bf16)
    grad_seq_rows = gather_line(grad_att, 4).reshape(-1, model_width)
    grad_out_w = jnp.dot(context.T, grad_seq_rows, preferred_element_type=f32)
    grad_out_w = lax.psum(grad_out_w.astype(bf16), "expert").astype(f32)
    grad_context = jnp.dot(grad_seq_rows, w_out.T, preferred_element_type=f32).astype(bf16)
    grad_context = grad_context.reshape(length, key_heads, group_size, head_size)
    again = (
        jnp.einsum("skgd,tkd->kgst", query_group, key_rot, preferred_element_type=f32)
        * scale_factor
    )
    again = jnp.where(causal, again, MASK_VALUE)
    probs_again = jnp.exp(again - log_norm)
    grad_probs = jnp.einsum("skgd,tkd->kgst", grad_context, values_low, preferred_element_type=f32)
    grad_values = jnp.einsum(
        "kgst,skgd->tkd", probs_again.astype(bf16), grad_context, preferred_element_type=f32
    )
    grad_values = grad_values.astype(bf16).reshape(length, key_heads * head_size)
    grad_scores = probs_again * (
        grad_probs - jnp.sum(grad_probs * probs_again, axis=-1, keepdims=True)
    )
    grad_scores = grad_scores.astype(bf16)
    grad_query_rot = (
        jnp.einsum("kgst,tkd->skgd", grad_scores, key_rot, preferred_element_type=f32)
        * scale_factor
    )
    grad_key_rot = (
        jnp.einsum("kgst,skgd->tkd", grad_scores, query_group, preferred_element_type=f32)
        * scale_factor
    )
    grad_q_norm = rotate_back(grad_query_rot.reshape(length, query_heads, head_size), cosine, sine)
    grad_k_norm = rotate_back(grad_key_rot, cosine, sine)
    q_gain_grad = jnp.sum(grad_q_norm * queries * query_scale, axis=(0, 1))
    k_gain_grad = jnp.sum(grad_k_norm * keys_raw * key_scale, axis=(0, 1))
    grad_queries = (
        norm_back(queries, query_scale, q_gain, grad_q_norm)
        .astype(bf16)
        .reshape(length, query_heads * head_size)
    )
    grad_keys = (
        norm_back(keys_raw, key_scale, k_gain, grad_k_norm)
        .astype(bf16)
        .reshape(length, key_heads * head_size)
    )
    grad_query_w = jnp.dot(seq_rows.T, grad_queries, preferred_element_type=f32)
    grad_key_w = jnp.dot(seq_rows.T, grad_keys, preferred_element_type=f32)
    grad_value_w = jnp.dot(seq_rows.T, grad_values, preferred_element_type=f32)
    summed = jnp.dot(grad_queries, w_query.T, preferred_element_type=f32)
    summed = summed + jnp.dot(grad_keys, w_key.T, preferred_element_type=f32)
    summed = summed + jnp.dot(grad_values, w_value.T, preferred_element_type=f32)
    grad_normed = scatter_line(summed.astype(bf16).reshape(4, row_count, model_width), 5)
    grad_inputs = (grad_hidden + norm_back(float_in, first_scale, attn_gain, grad_normed)).astype(
        bf16
    )
    attn_gain_grad = jnp.sum(grad_normed * float_in * first_scale, axis=0)
    attn_gain_grad, q_gain_grad, k_gain_grad = lax.psum(
        (attn_gain_grad, q_gain_grad, k_gain_grad), ("expert", "tensor")
    )
    attn_w = jnp.concatenate(
        [grad_query_w.astype(bf16), grad_key_w.astype(bf16), grad_value_w.astype(bf16)], axis=1
    )
    query_width = w_query.shape[1]
    key_width = w_key.shape[1]
    attn_w = scatter_plane(attn_w.reshape(32, -1, attn_w.shape[1]), 6)
    attn_w = gather_plane(attn_w.astype(bf16), 7).reshape(model_width, -1).astype(f32)
    gw = [jnp.swapaxes(jnp.stack([gw_a[i], gw_b[i]]), 1, 2) for i in range(2)]
    return (
        output,
        grad_inputs,
        attn_gain_grad,
        attn_w[:, :query_width],
        attn_w[:, query_width : query_width + key_width],
        attn_w[:, query_width + key_width :],
        q_gain_grad,
        k_gain_grad,
        grad_out_w,
        mlp_gain_grad,
        grad_router,
        gw[0],
        gw[1],
        jnp.stack([gw_a[2], gw_b[2]]),
    )


def solution(mesh):
    placed = (
        P(("expert", "tensor"), None),
        P(),
        P(None, "tensor"),
        P(None, "tensor"),
        P(None, "tensor"),
        P(),
        P(),
        P("tensor", None),
        P(),
        P(),
        P("expert", None, "tensor"),
        P("expert", None, "tensor"),
        P("expert", "tensor", None),
        P(("expert", "tensor"), None),
        P(("expert", "tensor"), None),
    )
    return jax.shard_map(
        per_device,
        mesh=mesh,
        in_specs=placed,
        out_specs=(
            P(("expert", "tensor"), None),
            P(("expert", "tensor"), None),
            P(),
            P(None, "tensor"),
            P(None, "tensor"),
            P(None, "tensor"),
            P(),
            P(),
            P("tensor", None),
            P(),
            P(),
            P("expert", None, "tensor"),
            P("expert", None, "tensor"),
            P("expert", "tensor", None),
        ),
        check_vma=False,
    )
```

```python
import functools

import jax
import jax.numpy as jnp
from jax import lax
from jax.experimental import pallas as pl
from jax.experimental.pallas import tpu as pltpu
from jax.sharding import PartitionSpec as P

MESH = pl.DeviceIdType.MESH
F32 = jnp.float32
BF16 = jnp.bfloat16
EPSILON = 1e-06
ROPE_BASE = 1000000.0
MASK_VALUE = -1e30
NT = (((1,), (1,)), ((), ()))
TN = (((0,), (0,)), ((), ()))
NN = (((1,), (0,)), ((), ()))
OTHER = {"z": "y", "y": "z"}
ANY = pl.BlockSpec(memory_space=pl.ANY)
VMEM = pl.BlockSpec(memory_space=pltpu.VMEM)
SMEM = pl.BlockSpec(memory_space=pltpu.SMEM)


def dot(left, right, dims):
    return lax.dot_general(left, right, dims, preferred_element_type=F32)


def shape(dims, dtype=BF16):
    return jax.ShapeDtypeStruct(tuple(dims), dtype)


def dma_sems(*counts):
    return [pltpu.SemaphoreType.DMA((count,)) for count in counts]


class Place:
    def __init__(self):
        e = lax.axis_index("expert")
        self.x = lax.axis_index("tensor")
        self.z = e // 8
        self.y = (e // 2) % 4
        self.core = e % 2

    def block(self, axis="z", a=0, b=0, other=0):
        dz, dy = (a, b) if axis == "z" else (b, a)
        core = (self.core + other) % 2
        return ((self.z + dz) % 4) * 8 + ((self.y + dy) % 4) * 2 + core

    def device(self, axis="z", a=0, b=0, other=0):
        return (self.block(axis, a, b, other), self.x)

    def on_line(self, step):
        return (self.block(), (self.x + step) % 4)


def greet(devices):
    barrier = pltpu.get_barrier_semaphore()
    for device in devices:
        pl.semaphore_signal(barrier, inc=1, device_id=device, device_id_type=MESH)
    pl.semaphore_wait(barrier, len(devices))


def plane_neighbours(place):
    return [
        place.device("z", 1),
        place.device("z", -1),
        place.device("y", 1),
        place.device("y", -1),
        place.device(other=1),
    ]


def run(steps):
    for _ in steps:
        pass


def remote(source, target, send_sem, recv_sem, device):
    return pltpu.make_async_remote_copy(
        src_ref=source, dst_ref=target, send_sem=send_sem, recv_sem=recv_sem,
        device_id=device, device_id_type=MESH,
    )


def gather_plan():
    stages = [[], [], [], []]
    for half, first in ((0, "y"), (1, "z")):
        for side in (-1, 1):
            stages[0].append((first, half, side, 0, None, ("f", side)))
            stages[0].append((first, half, 0, side, None, ("s", side)))
    for half, first in ((0, "y"), (1, "z")):
        for quarter, side in ((0, -1), (1, 1)):
            stages[1].append((first, half, 2, 0, quarter, ("f", side)))
        for f in (-1, 1):
            for side in (-1, 1):
                stages[1].append((first, half, f, side, None, ("s", side)))
        for quarter, side in ((0, -1), (1, 1)):
            stages[1].append((first, half, 0, 2, quarter, ("s", side)))
    for half, first in ((0, "y"), (1, "z")):
        for quarter in (0, 1):
            for side in (-1, 1):
                stages[2].append((first, half, 2, side, quarter, ("s", side)))
        for f in (-1, 1):
            for quarter, side in ((0, -1), (1, 1)):
                stages[2].append((first, half, f, 2, quarter, ("s", side)))
    for half, first in ((0, "y"), (1, "z")):
        for quarter, side in ((0, -1), (1, 1)):
            stages[3].append((first, half, 2, 2, quarter, ("s", side)))
    return stages


STAGES = gather_plan()
PIECES = [piece for stage in STAGES for piece in stage]
PIECE_AT = {piece: at for at, piece in enumerate(PIECES)}


def onward(piece):
    first, half, f, s, quarter, (leg, side) = piece
    found = []
    for target in PIECES:
        _, t_half, t_f, t_s, t_quarter, (t_leg, t_side) = target
        if t_half != half or (quarter is not None and t_quarter != quarter):
            continue
        if t_leg == "f":
            take = t_f == 2 and leg == "f" and f == t_side and s == 0
        elif t_s == 2:
            take = leg == "s" and s == t_side and f == t_f
        else:
            take = leg == "f" and s == 0 and f == t_f
        if take:
            found.append(target)
    return found


def plane_gather_steps(place, x_ref, blocks, sems):
    send_sems, recv_sems, core_send, core_recv = sems
    rows = x_ref.shape[0]
    sibling = place.device(other=1)

    def span(half, quarter):
        if quarter is None:
            return pl.ds(half * (rows // 2), rows // 2)
        return pl.ds(half * (rows // 2) + quarter * (rows // 4), rows // 4)

    def send(target, source, f, s):
        first, half, _, _, quarter, (leg, side) = target
        at = PIECE_AT[target]
        copy = remote(
            source.at[span(half, quarter)],
            blocks(place.block(first, f, s)).at[span(half, quarter)],
            send_sems.at[at], recv_sems.at[at],
            place.device(first if leg == "f" else OTHER[first], -side),
        )
        copy.start()
        return copy

    started = [send(piece, x_ref, 0, 0) for piece in STAGES[0]]
    last = len(PIECES)
    core_copies = [
        remote(x_ref, blocks(place.block()), core_send.at[last], core_recv.at[last], sibling)
    ]
    core_copies[0].start()
    yield -1
    for number, stage in enumerate(STAGES):
        for piece in stage:
            first, half, f, s, quarter, _ = piece
            at = PIECE_AT[piece]
            block = blocks(place.block(first, f, s))
            view = block.at[span(half, quarter)]
            remote(view, view, send_sems.at[at], recv_sems.at[at], sibling).wait_recv()
            for target in onward(piece):
                started.append(send(target, block, f, s))
            copy = remote(view, view, core_send.at[at], core_recv.at[at], sibling)
            copy.start()
            core_copies.append(copy)
            yield number
        if number == 0:
            other = blocks(place.block(other=1))
            remote(other, other, core_send.at[last], core_recv.at[last], sibling).wait_recv()
        for piece in stage:
            first, half, f, s, quarter, _ = piece
            at = PIECE_AT[piece]
            view = blocks(place.block(first, f, s, 1)).at[span(half, quarter)]
            remote(view, view, core_send.at[at], core_recv.at[at], sibling).wait_recv()
        yield number + 100
    for copy in started + core_copies:
        copy.wait_send()


def gather_sems():
    count = len(PIECES)
    return dma_sems(count, count, count + 1, count + 1)


def scatter_scratch(rows, width):
    return [
        pltpu.VMEM((16, rows, width), BF16),
        pltpu.VMEM((2, 4, 2, rows // 4, width), BF16),
        pltpu.VMEM((2, 4, 2, rows // 2, width), BF16),
        pltpu.VMEM((2, 2, rows // 4, width), BF16),
        pltpu.VMEM((2, 2, rows // 2, width), BF16),
        *dma_sems(16, 16, 40, 40),
    ]


def plane_scatter_steps(place, rows, make, block, scratch, finish):
    other, in_a, in_b, in_c, in_d, core_send, core_recv, send_sems, recv_sems = scratch
    half_rows, quarter_rows = rows // 2, rows // 4
    exchanged, ready, sent = {}, set(), []

    def exchange(dz, dy):
        at = dz * 4 + dy
        if at in exchanged:
            return
        make(dz, dy)
        exchanged[at] = remote(
            block(dz, dy, 1), other.at[at], core_send.at[at], core_recv.at[at],
            place.device(other=1),
        )
        exchanged[at].start()

    def add_rows(into, start, count, source):
        @pl.loop(0, count, step=16)
        def _(row):
            here = pl.ds(start + row, 16)
            total = into[here].astype(F32) + source[pl.ds(row, 16)].astype(F32)
            into[here] = total.astype(BF16)

    def where(axis, a, b):
        dz, dy = (a, b) if axis == "z" else (b, a)
        return dz % 4, dy % 4

    def ready_block(axis, a, b):
        dz, dy = where(axis, a, b)
        at = dz * 4 + dy
        if at not in ready:
            ready.add(at)
            exchange(dz, dy)
            exchanged[at].wait_recv()
            add_rows(block(dz, dy, 0), 0, rows, other.at[at])
        return block(dz, dy, 0)

    def send(source, target, number, device):
        copy = remote(source, target, send_sems.at[number], recv_sems.at[number], device)
        copy.start()
        sent.append(copy)

    def arrive(target, number):
        remote(
            target, target, send_sems.at[number], recv_sems.at[number], place.device("z", 1)
        ).wait_recv()

    axes = (("z", "y"), ("y", "z"))
    sides = ((0, 1), (1, -1))
    lines = (2, 1, 3, 0)
    first_needs = []
    for line in lines:
        for first, _ in axes:
            if where(first, 2, line) not in first_needs:
                first_needs.append(where(first, 2, line))
    for dz, dy in first_needs[:4]:
        exchange(dz, dy)
    yield
    for line in lines:
        for half, (first, second) in enumerate(axes):
            for dz, dy in first_needs:
                if (dz, dy) not in [where(first, 2, line)] and dz * 4 + dy not in exchanged:
                    exchange(dz, dy)
                    break
            held = ready_block(first, 2, line)
            for quarter, side in sides:
                rows_here = pl.ds(half * half_rows + quarter * quarter_rows, quarter_rows)
                send(held.at[rows_here], in_a.at[half, line, quarter],
                     (half * 4 + line) * 2 + quarter, place.device(first, side))
        yield
    for dz in (1, 3, 0, 2):
        for dy in (1, 3, 0, 2):
            exchange(dz, dy)
    yield
    for line in lines:
        for half, (first, second) in enumerate(axes):
            for quarter, side in sides:
                held = ready_block(first, side, line)
                number = (half * 4 + line) * 2 + quarter
                arrive(in_a.at[half, line, quarter], number)
                add_rows(held, half * half_rows + quarter * quarter_rows, quarter_rows,
                         in_a.at[half, line, quarter])
                send(held.at[pl.ds(half * half_rows, half_rows)],
                     in_b.at[half, line, quarter], 16 + number, place.device(first, side))
        yield
    for line in lines:
        for half, (first, second) in enumerate(axes):
            held = ready_block(first, 0, line)
            for quarter in (0, 1):
                number = (half * 4 + line) * 2 + quarter
                arrive(in_b.at[half, line, quarter], 16 + number)
                add_rows(held, half * half_rows, half_rows, in_b.at[half, line, quarter])
            if line == 2:
                for quarter, side in sides:
                    rows_here = pl.ds(half * half_rows + quarter * quarter_rows, quarter_rows)
                    send(held.at[rows_here], in_c.at[half, quarter],
                         32 + half * 2 + quarter, place.device(second, side))
            if line in (1, 3):
                quarter, side = sides[0] if line == 1 else sides[1]
                number = 32 + half * 2 + quarter
                arrive(in_c.at[half, quarter], number)
                add_rows(held, half * half_rows + quarter * quarter_rows, quarter_rows,
                         in_c.at[half, quarter])
                send(held.at[pl.ds(half * half_rows, half_rows)], in_d.at[half, quarter],
                     36 + half * 2 + quarter, place.device(second, side))
        yield
    held = block(0, 0, 0)
    for half in (0, 1):
        for quarter in (0, 1):
            arrive(in_d.at[half, quarter], 36 + half * 2 + quarter)

        @pl.loop(0, half_rows, step=16)
        def _(row):
            here = pl.ds(half * half_rows + row, 16)
            total = held[here].astype(F32)
            for quarter in (0, 1):
                total = total + in_d[half, quarter, pl.ds(row, 16)].astype(F32)
            finish(half * half_rows + row, total)

    for copy in sent:
        copy.wait_send()
    for at in exchanged:
        exchanged[at].wait_send()


def line_gather_steps(place, out_ref, rows, sems):
    send_sems, recv_sems = sems
    half = rows // 2

    def part(step, start, count):
        return out_ref.at[pl.ds(((place.x + step) % 4) * rows + start, count)]

    def copy(view, number, side):
        return remote(view, view, send_sems.at[number], recv_sems.at[number], place.on_line(side))

    copies = [copy(part(0, 0, rows), 0, 1), copy(part(0, 0, rows), 1, -1)]
    for c in copies:
        c.start()
    yield
    copy(part(-1, 0, rows), 0, 1).wait_recv()
    copies.append(copy(part(-1, 0, half), 2, 1))
    copies[2].start()
    copy(part(1, 0, rows), 1, -1).wait_recv()
    copies.append(copy(part(1, half, half), 3, -1))
    copies[3].start()
    yield
    copy(part(2, 0, half), 2, 1).wait_recv()
    copy(part(2, half, half), 3, -1).wait_recv()
    for c in copies:
        c.wait_send()


def line_scatter_scratch(rows, width):
    return [
        pltpu.VMEM((2, rows // 2, width), BF16),
        pltpu.VMEM((2, rows, width), BF16),
        *dma_sems(4, 4),
    ]


def line_scatter_steps(place, c_ref, rows, scratch):
    in_a, in_b, send_sems, recv_sems = scratch
    half = rows // 2

    def part(step, start, count):
        return c_ref.at[pl.ds(((place.x + step) % 4) * rows + start, count)]

    def copy(source, target, number, side):
        return remote(
            source, target, send_sems.at[number], recv_sems.at[number], place.on_line(side)
        )

    copies = [
        copy(part(2, 0, half), in_a.at[0], 0, 1),
        copy(part(2, half, half), in_a.at[1], 1, -1),
    ]
    for c in copies:
        c.start()
    yield

    def add(view, source):
        @pl.loop(0, half, step=16)
        def _(row):
            here = pl.ds(row, 16)
            view[here] = (view[here].astype(F32) + source[here].astype(F32)).astype(BF16)

    copies[0].wait_recv()
    add(part(1, 0, half), in_a.at[0])
    copies.append(copy(part(1, 0, rows), in_b.at[0], 2, 1))
    copies[2].start()
    copies[1].wait_recv()
    add(part(-1, half, half), in_a.at[1])
    copies.append(copy(part(-1, 0, rows), in_b.at[1], 3, -1))
    copies[3].start()
    yield
    copies[2].wait_recv()
    copies[3].wait_recv()
    for c in copies:
        c.wait_send()


SLOTS = 80
GROUPS = [(dz, dy) for dz in (0, 1, 3, 2) for dy in (0, 1)]


def chosen_rows(slots, first):
    value = slots.astype(F32)
    lane = lax.broadcasted_iota(jnp.int32, value.shape, 1)
    slot = lax.broadcasted_iota(jnp.int32, (value.shape[0], 2 * SLOTS), 1).astype(F32)
    found = []
    for j in range(2):
        mine = jnp.sum(jnp.where(lane == first + j, value, 0.0), axis=1, keepdims=True)
        found.append(jnp.where(mine >= 0.0, mine + float(j * SLOTS), -1.0))
    return jnp.where((slot == found[0]) | (slot == found[1]), 1.0, 0.0).astype(BF16)


def group_blocks(place, dz, dy):
    z = (place.z + dz) % 4
    return [z * 8 + ((place.y + dy + two) % 4) * 2 for two in (0, 2)]


def gather_select_kernel(
    x_ref, grads_ref, all_ref, grad_a_ref, grad_b_ref, row_a_ref, row_b_ref, gate_a_ref, gate_b_ref,
    tokens, slots, rows_a, rows_b, grads_a, grads_b, gates_a, gates_b,
    own_sem, load_sems, slot_sems, save_sems, *sems,
):
    place = Place()
    first = 2 * lax.axis_index("expert")
    width = rows_a.shape[1]
    greet(plane_neighbours(place))
    own = pltpu.make_async_copy(x_ref, all_ref.at[place.block()], own_sem.at[0])
    own.start()
    steps = plane_gather_steps(place, x_ref, lambda at: all_ref.at[at], sems)
    next(steps)

    def loads_of(source, number, slot):
        dz, dy = GROUPS[number]
        return [
            pltpu.make_async_copy(
                source.at[pl.ds(at, 2)], tokens.at[slot, pl.ds(2 * i, 2)], load_sems.at[2 * slot + i]
            )
            for i, at in enumerate(group_blocks(place, dz, dy))
        ]

    saves = []

    def save(value_ref, target, number, slot):
        here = pl.ds(number * SLOTS, SLOTS)
        copy = pltpu.make_async_copy(value_ref.at[here], target.at[here], save_sems.at[slot])
        copy.start()
        saves.append(copy)

    def select(number, slot, is_grad):
        for load in loads_of(grads_ref if is_grad else all_ref, number, slot):
            load.wait()
        here = pl.ds(number * SLOTS, SLOTS)
        block = tokens[slot].reshape(512, width + 128)
        if is_grad:
            slots[number] = block[:, width:]
        rows = dot(chosen_rows(slots[number], first), block, TN)
        a, b = (grads_a, grads_b) if is_grad else (rows_a, rows_b)
        a[here] = rows[:SLOTS, :width].astype(BF16)
        b[here] = rows[SLOTS:, :width].astype(BF16)
        base = number * 2 + (16 if is_grad else 0)
        save(a, grad_a_ref if is_grad else row_a_ref, number, base)
        save(b, grad_b_ref if is_grad else row_b_ref, number, base + 1)
        if not is_grad:
            lane = lax.broadcasted_iota(jnp.int32, (SLOTS, 128), 1) % 64
            for j, (gates, target) in enumerate(((gates_a, gate_a_ref), (gates_b, gate_b_ref))):
                part = rows[j * SLOTS : (j + 1) * SLOTS, width:]
                gate = jnp.sum(jnp.where(lane == first + j, part, 0.0), axis=1, keepdims=True)
                gates[here] = jnp.broadcast_to(gate, (SLOTS, 128))
                save(gates, target, number, 32 + number * 2 + j)

    def start(is_grad, number, slot):
        for load in loads_of(grads_ref if is_grad else all_ref, number, slot):
            load.start()

    start(True, 0, 0)
    grad_turn = 0
    pieces = 0
    for stage in steps:
        if stage < 100:
            pieces += 1
            if pieces % 2 == 0 and grad_turn < 8:
                if grad_turn + 1 < 8:
                    start(True, grad_turn + 1, (grad_turn + 1) % 2)
                select(grad_turn, grad_turn % 2, True)
                grad_turn += 1
        elif stage == 101:
            assert grad_turn == 8
            own.wait()
            start(False, 0, 0)
            start(False, 1, 1)
            select(0, 0, False)
            select(1, 1, False)
        elif stage == 102:
            start(False, 2, 0)
            for number in range(2, 6):
                if number + 1 < 6:
                    start(False, number + 1, (number + 1) % 2)
                select(number, number % 2, False)
        elif stage == 103:
            start(False, 6, 0)
            start(False, 7, 1)
            select(6, 0, False)
            select(7, 1, False)
    for copy in saves:
        copy.wait()


def gather_select(x, grads, collective_id):
    count, full = x.shape
    width = full - 128
    total = len(GROUPS) * SLOTS
    rows = shape((total, width))
    gate = shape((total, 128), F32)
    return pl.pallas_call(
        gather_select_kernel,
        out_shape=(shape((32, count, full)), rows, rows, rows, rows, gate, gate),
        in_specs=[ANY, ANY],
        out_specs=(ANY,) * 7,
        scratch_shapes=[
            pltpu.VMEM((2, 4, count, full), BF16),
            pltpu.VMEM((8, 512, 128), BF16),
            *[pltpu.VMEM((total, width), BF16)] * 4,
            *[pltpu.VMEM((total, 128), F32)] * 2,
            *dma_sems(1, 4, 1, 48),
            *gather_sems(),
        ],
        compiler_params=pltpu.CompilerParams(
            collective_id=collective_id, has_side_effects=True, vmem_limit_bytes=60 * 2**20
        ),
        cost_estimate=pl.CostEstimate(flops=6 * 10**10, bytes_accessed=10**8, transcendentals=0),
        name="gather_select",
    )(x, grads)[1:]


def combine_scatter_kernel(
    back_a_ref, back_b_ref, out_a_ref, out_b_ref, slots_ref, gw_ref, sum_left_ref, sum_right_ref,
    grad_out_ref, hidden_ref, mixed_ref, state_ref, picks_ref, mlp_gain_ref, router_ref,
    shares_ref, from_right_ref, from_left_ref,
    grad_hidden_ref, grad_att_ref, grad_router_ref, gain_ref,
    rows, slots, blocks, out_rows, share, total, load_sems, row_sems, share_sems,
    line_send, line_recv, *scratch,
):
    place = Place()
    first = 2 * lax.axis_index("expert")
    count = hidden_ref.shape[0]
    width = hidden_ref.shape[1]
    for number, (dz, dy) in enumerate(GROUPS):
        for i, at in enumerate(group_blocks(place, dz, dy)):
            pltpu.make_async_copy(
                slots_ref.at[pl.ds(at, 2), :, pl.ds(width, 128)], slots.at[number, pl.ds(2 * i, 2)],
                load_sems.at[2 * number + i],
            ).start()
        for j, ref in enumerate((back_a_ref, back_b_ref)):
            pltpu.make_async_copy(
                ref.at[pl.ds(number * SLOTS, SLOTS)], rows.at[number, j],
                load_sems.at[16 + 2 * number + j],
            ).start()
    greet(plane_neighbours(place) + [place.on_line(1), place.on_line(-1)])
    line = second_sends(
        place, gw_ref, sum_left_ref, sum_right_ref, from_right_ref, from_left_ref, line_send,
        line_recv,
    )
    for copy in line:
        copy.start()
    made = set()

    def loaded(number):
        dz, dy = GROUPS[number]
        for i, at in enumerate(group_blocks(place, dz, dy)):
            pltpu.make_async_copy(
                slots_ref.at[pl.ds(at, 2), :, pl.ds(width, 128)], slots.at[number, pl.ds(2 * i, 2)],
                load_sems.at[2 * number + i],
            ).wait()
        for j, ref in enumerate((back_a_ref, back_b_ref)):
            pltpu.make_async_copy(
                ref.at[pl.ds(number * SLOTS, SLOTS)], rows.at[number, j],
                load_sems.at[16 + 2 * number + j],
            ).wait()

    def table_of(number):
        return chosen_rows(slots[number].reshape(512, 128), first)

    def make(dz, dy):
        number = GROUPS.index((dz, dy % 2))
        if number in made:
            return
        made.add(number)
        loaded(number)
        both = rows[number].reshape(2 * SLOTS, width + 128)
        sums = dot(table_of(number), both, NN).astype(BF16).reshape(2, 2, count, width + 128)
        low = dy % 2
        blocks[dz * 4 + low] = sums[0]
        blocks[dz * 4 + low + 2] = sums[1]

    def block(dz, dy, other):
        return blocks.at[dz * 4 + dy, (place.core + other) % 2]

    def finish(row, value):
        total[pl.ds(row, 16)] = value

    def out_loads(number):
        return [
            pltpu.make_async_copy(
                ref.at[pl.ds(number * SLOTS, SLOTS)], out_rows.at[number % 2, j],
                row_sems.at[2 * (number % 2) + j],
            )
            for j, ref in enumerate((out_a_ref, out_b_ref))
        ]

    def share_saves(number):
        dz, dy = GROUPS[number]
        return [
            pltpu.make_async_copy(
                share.at[number % 2, pl.ds(2 * i, 2)], shares_ref.at[pl.ds(at, 2)],
                share_sems.at[2 * (number % 2) + i],
            )
            for i, at in enumerate(group_blocks(place, dz, dy))
        ]

    def make_share(number):
        if number + 1 < len(GROUPS):
            for load in out_loads(number + 1):
                load.start()
        for load in out_loads(number):
            load.wait()
        if number >= 2:
            for save in share_saves(number - 2):
                save.wait()
        both = out_rows[number % 2].reshape(2 * SLOTS, width)
        sums = dot(table_of(number), both, NN).astype(BF16)
        share[number % 2] = sums.reshape(4, count, width)
        for save in share_saves(number):
            save.start()

    for load in out_loads(0):
        load.start()
    turn = 0
    for at, _ in enumerate(plane_scatter_steps(place, count, make, block, scratch, finish)):
        if at >= 5:
            for _ in range(2):
                if turn < len(GROUPS):
                    make_share(turn)
                    turn += 1
    while turn < len(GROUPS):
        make_share(turn)
        turn += 1

    experts = picks_ref.shape[1]
    probs, gates = state_ref[:, :experts], state_ref[:, experts : 2 * experts]
    picked_total = state_ref[:, 2 * experts : 2 * experts + 1]
    second_scale = state_ref[:, 2 * experts + 1 : 2 * experts + 2]
    tail = total[:, pl.ds(width, 128)]
    gate_grad = tail[:, :experts] + tail[:, experts:]
    mean = jnp.sum(gate_grad * gates, axis=1, keepdims=True)
    prob_grad = picks_ref[...] * (gate_grad - mean) / picked_total
    logit_grad = probs * (prob_grad - jnp.sum(prob_grad * probs, axis=1, keepdims=True))
    logit_grad = logit_grad.astype(BF16)
    grad_router_ref[...] = dot(logit_grad, mixed_ref[:, :width], TN)
    grad_mixed = total[:, :width] + dot(logit_grad, router_ref[...], NN)
    hidden = hidden_ref[...]
    gain_ref[...] = jnp.sum(grad_mixed * hidden * second_scale, axis=0, keepdims=True)
    grad_hidden = grad_out_ref[...].astype(F32) + norm_back(
        hidden, second_scale, mlp_gain_ref[...], grad_mixed
    )
    grad_hidden_ref[...] = grad_hidden
    grad_att_ref[...] = grad_hidden.astype(BF16)
    for number in (len(GROUPS) - 2, len(GROUPS) - 1):
        for save in share_saves(number):
            save.wait()
    for copy in line:
        copy.wait()


def combine_scatter(
    back, out, slots, line, grad_out, hidden, mixed, state, picks, mlp_gain, router_t, collective_id
):
    count, width = hidden.shape
    groups = len(GROUPS)
    return pl.pallas_call(
        combine_scatter_kernel,
        out_shape=(
            shape((32, count, width)),
            *[shape((3, line[0].shape[1] // 4, width))] * 2,
            shape((count, width), F32),
            shape((count, width)),
            shape(router_t.shape, F32),
            shape((1, width), F32),
        ),
        in_specs=[ANY] * 8 + [VMEM] * 7,
        out_specs=(ANY, ANY, ANY, VMEM, VMEM, VMEM, VMEM),
        scratch_shapes=[
            pltpu.VMEM((groups, 2, SLOTS, width + 128), BF16),
            pltpu.VMEM((groups, 4, count, 128), BF16),
            pltpu.VMEM((16, 2, count, width + 128), BF16),
            pltpu.VMEM((2, 2, SLOTS, width), BF16),
            pltpu.VMEM((2, 4, count, width), BF16),
            pltpu.VMEM((count, width + 128), F32),
            *dma_sems(32, 4, 4, 4, 4),
            *scatter_scratch(count, width + 128),
        ],
        compiler_params=pltpu.CompilerParams(
            collective_id=collective_id, has_side_effects=True, vmem_limit_bytes=62 * 2**20
        ),
        cost_estimate=pl.CostEstimate(flops=6 * 10**10, bytes_accessed=10**8, transcendentals=0),
        name="combine_scatter",
    )(*back, *out, slots, *line, grad_out, hidden, mixed, state, picks, mlp_gain, router_t)


def expert_kernel(
    expert_ref, own_ref, left_ref, right_ref, far0_ref, far1_ref, x_hbm, d_hbm, gate_hbm,
    *rest,
):
    expert_steps(
        None, expert_ref, (own_ref, left_ref, right_ref, far0_ref, far1_ref), x_hbm, d_hbm, gate_hbm,
        *rest,
    )


def expert_sending_kernel(
    expert_ref, own_ref, left_ref, right_ref, far0_ref, far1_ref, x_hbm, d_hbm, gate_hbm, other_hbm,
    p_hbm, rb_hbm, gw_hbm, sum_left_hbm, sum_right_hbm, *scratch,
):
    *scratch, come, mine, load_sems, send_sems, recv_sems, save_sems = scratch
    payload = first_sums_steps(
        Place(), other_hbm, sum_left_hbm, sum_right_hbm, come, mine, load_sems, send_sems,
        recv_sems, save_sems,
    )
    expert_steps(
        payload, expert_ref, (own_ref, left_ref, right_ref, far0_ref, far1_ref), x_hbm, d_hbm,
        gate_hbm, p_hbm, rb_hbm, gw_hbm, *scratch,
    )


def expert_steps(
    payload, expert_ref, parts, x_hbm, d_hbm, gate_hbm, p_hbm, rb_hbm, gw_hbm,
    w, x, d, gate, rg, middle, ggp, gup, p, rb, dots, turned, gw, in_sems, out_sems, gw_sems,
):
    f32, bf16 = jnp.float32, jnp.bfloat16
    rows, width = x.shape
    hidden = middle.shape[1]
    chunk = 256
    loads = [
        pltpu.make_async_copy(x_hbm, x, in_sems.at[0]),
        pltpu.make_async_copy(d_hbm, d, in_sems.at[1]),
        pltpu.make_async_copy(gate_hbm, gate, in_sems.at[2]),
    ]
    at = 0
    for i, ref in enumerate(parts):
        size = ref.shape[1]
        loads.append(pltpu.make_async_copy(ref, w.at[:, pl.ds(at, size)], in_sems.at[3 + i]))
        at += size
    for load in loads:
        load.start()
    if payload is not None:
        greet([Place().on_line(1), Place().on_line(-1)])
        next(payload)
    for load in loads:
        load.wait()

    @pl.loop(0, rows, step=16)
    def _(r):
        here = pl.ds(r, 16)
        scaled = d[here].astype(f32) * gate[here, 0:1]
        rg[here] = scaled.astype(bf16)

    for c in range(0, hidden, chunk):
        here = pl.ds(c, chunk)
        gate_pre = dot(x[...], w[0, here], NT)
        up_pre = dot(x[...], w[1, here], NT)
        grad_mid = dot(rg[...], w[2, here], NT)
        sig = 1.0 / (1.0 + jnp.exp(-gate_pre))
        act = gate_pre * sig
        middle[:, here] = (act * up_pre).astype(bf16)
        ggp[:, here] = (grad_mid * up_pre * sig * (1.0 + gate_pre * (1.0 - sig))).astype(bf16)
        gup[:, here] = (grad_mid * act).astype(bf16)

    dots[...] = jnp.zeros_like(dots)

    for n in range(0, width, chunk):
        here = pl.ds(n, chunk)
        out = dot(middle[...], w[2, :, here], NN).astype(bf16).astype(f32)
        p[:, here] = (out * gate[:, 0:1]).astype(bf16)
        along = out * d[:, here].astype(f32)
        dots[...] += along[:, :128] + along[:, 128:]
        back = dot(ggp[...], w[0, :, here], NN) + dot(gup[...], w[1, :, here], NN)
        rb[:, here] = back.astype(bf16)

    expert = expert_ref[0]
    total = jnp.sum(dots[...], axis=1, keepdims=True)
    high = total.astype(bf16).astype(f32)
    lane = lax.broadcasted_iota(jnp.int32, (rows, 128), 1)
    tail = jnp.where(lane == expert, high, jnp.where(lane == expert + 64, total - high, 0.0))
    rb[:, pl.ds(width, 128)] = tail.astype(bf16)
    outs = [
        pltpu.make_async_copy(rb, rb_hbm, out_sems.at[0]),
        pltpu.make_async_copy(p, p_hbm, out_sems.at[1]),
    ]
    for out in outs:
        out.start()

    for i, (left, right) in enumerate(((ggp, x), (gup, x), (middle, rg))):
        turned[...] = left[...].T

        for c in range(0, hidden, chunk):
            here = pl.ds(c, chunk)
            for n in range(0, width, 512):
                there = pl.ds(n, 512)
                gw[i, here, there] = dot(turned[here], right[:, there], NN).astype(bf16)

        save = pltpu.make_async_copy(gw.at[i], gw_hbm.at[i], gw_sems.at[i])
        save.start()
        outs.append(save)
    if payload is not None:
        run(payload)
    for out in outs:
        out.wait()


def first_sums_steps(
    place, gw_hbm, sum_left, sum_right, come, mine, load_sems, send_sems, recv_sems, save_sems
):
    shard = gw_hbm.shape[1] // 4
    half = shard // 2
    sends = [
        remote(gw_hbm.at[:, pl.ds(3 * shard + i * half, half)], come.at[i], send_sems.at[i],
               recv_sems.at[i], place.on_line(side))
        for i, side in ((0, -1), (1, 1))
    ]
    loads = [
        pltpu.make_async_copy(gw_hbm.at[:, pl.ds(at, half)], mine.at[i], load_sems.at[i])
        for i, at in ((0, shard), (1, 2 * shard + half))
    ]
    for copy in sends + loads:
        copy.start()
    yield
    saves = []
    for i, target in ((0, sum_left), (1, sum_right)):
        loads[i].wait()
        sends[i].wait()

        @pl.loop(0, half, step=16)
        def _(row):
            for j in range(3):
                here = (i, j, pl.ds(row, 16))
                mine[here] = (mine[here].astype(F32) + come[here].astype(F32)).astype(BF16)

        saves.append(pltpu.make_async_copy(mine.at[i], target, save_sems.at[i]))
        saves[i].start()
    for save in saves:
        save.wait()


def first_sums_scratch(half, width):
    return [
        pltpu.VMEM((2, 3, half, width), BF16),
        pltpu.VMEM((2, 3, half, width), BF16),
        *dma_sems(2, 2, 2, 2),
    ]


def second_sends(place, gw_hbm, sum_left, sum_right, from_right, from_left, send_sems, recv_sems):
    shard = gw_hbm.shape[1] // 4
    half = shard // 2
    low, high = pl.ds(0, half), pl.ds(half, half)
    plan = [
        (gw_hbm.at[:, pl.ds(shard + half, half)], from_right.at[:, high], -1),
        (gw_hbm.at[:, pl.ds(2 * shard, half)], from_left.at[:, low], 1),
        (sum_left, from_right.at[:, low], -1),
        (sum_right, from_left.at[:, high], 1),
    ]
    return [
        remote(source, target, send_sems.at[i], recv_sems.at[i], place.on_line(side))
        for i, (source, target, side) in enumerate(plan)
    ]


def expert_layer(expert, weights, x, d, gate, other=None, collective_id=None):
    bf16 = jnp.bfloat16
    rows, width = x.shape
    hidden = sum(part.shape[1] for part in weights)
    half = hidden // 8
    sending = other is not None
    more = [shape((3, half, width))] * 2 if sending else []
    extra = first_sums_scratch(half, width) if sending else []
    return pl.pallas_call(
        expert_sending_kernel if sending else expert_kernel,
        out_shape=(
            jax.ShapeDtypeStruct((rows, width), bf16),
            jax.ShapeDtypeStruct((rows, width + 128), bf16),
            jax.ShapeDtypeStruct((3, hidden, width), bf16),
            *more,
        ),
        in_specs=[SMEM] + [ANY] * (9 if sending else 8),
        out_specs=(ANY,) * (5 if sending else 3),
        scratch_shapes=[
            pltpu.VMEM((3, hidden, width), bf16),
            pltpu.VMEM((rows, width), bf16),
            pltpu.VMEM((rows, width), bf16),
            pltpu.VMEM((rows, 128), jnp.float32),
            pltpu.VMEM((rows, width), bf16),
            pltpu.VMEM((rows, hidden), bf16),
            pltpu.VMEM((rows, hidden), bf16),
            pltpu.VMEM((rows, hidden), bf16),
            pltpu.VMEM((rows, width), bf16),
            pltpu.VMEM((rows, width + 128), bf16),
            pltpu.VMEM((rows, 128), jnp.float32),
            pltpu.VMEM((hidden, rows), bf16),
            pltpu.VMEM((3, hidden, width), bf16),
            *dma_sems(8, 2, 3),
            *extra,
        ],
        compiler_params=pltpu.CompilerParams(
            vmem_limit_bytes=60 * 2**20, collective_id=collective_id, has_side_effects=sending
        ),
        cost_estimate=pl.CostEstimate(
            flops=18 * rows * hidden * width,
            bytes_accessed=12 * hidden * width + 10 * rows * width,
            transcendentals=rows * hidden,
        ),
        name="expert_sending" if sending else "expert_layer",
    )(expert, *weights, x, d, gate, *([other] if sending else []))


def rope_tables(length, head_size):
    position = jnp.arange(length, dtype=jnp.float32)[:, None]
    index_half = jnp.arange(head_size // 2, dtype=jnp.float32)[None, :]
    frequency = jnp.exp(index_half * (-2.0 / head_size) * jnp.log(ROPE_BASE))
    turned = position * frequency
    sine = jnp.sin(turned)
    return (
        jnp.concatenate([jnp.cos(turned)] * 2, axis=1),
        jnp.concatenate([-sine, sine], axis=1),
    )


def inverse_rms(values):
    return lax.rsqrt(jnp.mean(values * values, axis=-1, keepdims=True) + EPSILON)


def norm_back(values, scales, gain, grads):
    weighted = grads * gain
    return scales * weighted - values * scales * scales * scales * jnp.mean(
        weighted * values, axis=-1, keepdims=True
    )


def attend(seq, w_query, w_key, w_value, q_gain, k_gain, cosine, sine,
           query_rot, key_rot, values, query_unit, key_unit, stats, context):
    length = seq.shape[0]
    head = cosine.shape[1]
    heads = w_query.shape[1] // head
    scale = head ** (-0.5)
    cos, sin = cosine[...], sine[...]
    lane = lax.broadcasted_iota(jnp.int32, (length, head), 1)
    kept = jnp.zeros((length, head), F32)

    def unit_and_rot(raw, gain):
        scales = inverse_rms(raw)
        unit = raw * scales
        normed = unit * gain
        rot = normed * cos + pltpu.roll(normed, head // 2, 1) * sin
        return scales, unit, rot.astype(BF16)

    raw = dot(seq[...], w_key[...], NN)
    scales, unit, rot = unit_and_rot(raw, k_gain[...])
    key_unit[...] = unit
    key_rot[...] = rot
    kept = jnp.where(lane == 8, scales, kept)
    values[...] = dot(seq[...], w_value[...], NN).astype(BF16)
    half = length // 2
    for pair in range(0, heads, 2):
        raws = dot(seq[...], w_query[:, pl.ds(pair * head, 2 * head)], NN)
        for h in (pair, pair + 1):
            here = pl.ds(h * head, head)
            raw = raws[:, (h - pair) * head : (h - pair + 1) * head]
            scales, unit, rot = unit_and_rot(raw, q_gain[...])
            query_unit[:, here] = unit
            query_rot[:, here] = rot
            kept = jnp.where(lane == h, scales, kept)
            logs = []
            for part in range(2):
                until = (part + 1) * half
                scores = dot(rot[part * half : until], key_rot[:until], NT) * scale
                row = lax.broadcasted_iota(jnp.int32, scores.shape, 0) + part * half
                column = lax.broadcasted_iota(jnp.int32, scores.shape, 1)
                scores = jnp.where(row >= column, scores, MASK_VALUE)
                peak = jnp.max(scores, axis=1, keepdims=True)
                raised = jnp.exp(scores - peak)
                total = jnp.sum(raised, axis=1, keepdims=True)
                probs = (raised * (1.0 / total)).astype(BF16)
                mixed = dot(probs, values[:until], NN)
                context[pl.ds(part * half, half), here] = mixed.astype(BF16)
                logs.append(peak + jnp.log(total))
            kept = jnp.where(lane == 16 + h, jnp.concatenate(logs, axis=0), kept)
    stats[...] = kept


def attend_back(grad_rows, seq, w_query, w_key, w_value, w_out, q_gain, k_gain, cosine, sine,
                query_rot, key_rot, values, query_unit, key_unit, stats,
                grad_context, grad_qkv, gains):
    length = seq.shape[0]
    head = cosine.shape[1]
    heads = query_rot.shape[1] // head
    scale = head ** (-0.5)
    cos, sin = cosine[...], sine[...]
    half = length // 2

    def rotate_back(grads):
        return grads * cos - pltpu.roll(grads, head // 2, 1) * sin

    def unit_back(scales, unit, gain, grads):
        z = grads * gain
        return scales * (z - unit * jnp.mean(z * unit, axis=1, keepdims=True))

    for n in range(0, heads * head, 256):
        here = pl.ds(n, 256)
        grad_context[:, here] = dot(grad_rows[...], w_out[here], NT).astype(BF16)
    yield
    key_grads = [jnp.zeros((half, head), F32)] * 2
    value_grads = [jnp.zeros((half, head), F32)] * 2
    q_gain_grad = jnp.zeros((1, head), F32)
    for h in range(heads):
        here = pl.ds(h * head, head)
        query_grads = []
        for part in range(2):
            until = (part + 1) * half
            rows = pl.ds(part * half, half)
            rot = query_rot[rows, here]
            scores = dot(rot, key_rot[:until], NT) * scale
            row = lax.broadcasted_iota(jnp.int32, scores.shape, 0) + part * half
            column = lax.broadcasted_iota(jnp.int32, scores.shape, 1)
            scores = jnp.where(row >= column, scores, MASK_VALUE)
            probs = jnp.exp(scores - stats[rows, 16 + h : 17 + h])
            from_context = grad_context[rows, here]
            grad_probs = dot(from_context, values[:until], NT)
            low = probs.astype(BF16)
            value_part = dot(low, from_context, TN)
            mean = jnp.sum(grad_probs * probs, axis=1, keepdims=True)
            grad_scores = (probs * (grad_probs - mean)).astype(BF16)
            query_grads.append(dot(grad_scores, key_rot[:until], NN) * scale)
            key_part = dot(grad_scores, rot, TN) * scale
            for other in range(part + 1):
                cut = slice(other * half, (other + 1) * half)
                value_grads[other] = value_grads[other] + value_part[cut]
                key_grads[other] = key_grads[other] + key_part[cut]
        grads = rotate_back(jnp.concatenate(query_grads, axis=0))
        unit = query_unit[:, here]
        q_gain_grad = q_gain_grad + jnp.sum(grads * unit, axis=0, keepdims=True)
        grad_qkv[:, here] = unit_back(stats[:, h : h + 1], unit, q_gain[...], grads).astype(BF16)
        yield
    grads = rotate_back(jnp.concatenate(key_grads, axis=0))
    unit = key_unit[...]
    gains[0:1, :] = q_gain_grad
    gains[1:2, :] = jnp.sum(grads * unit, axis=0, keepdims=True)
    grad_qkv[:, pl.ds(heads * head, head)] = unit_back(
        stats[:, 8:9], unit, k_gain[...], grads
    ).astype(BF16)
    grad_qkv[:, pl.ds((heads + 1) * head, head)] = jnp.concatenate(value_grads, axis=0).astype(BF16)
    yield


def forward_kernel(
    inputs_ref, attn_gain_ref, q_gain_ref, k_gain_ref, cos_ref, sin_ref, mlp_gain_ref, router_ref,
    picks_ref, w_query_ref, w_key_ref, w_value_ref, w_out_ref,
    mixed_ref, hidden_ref, state_ref, seq_ref,
    query_rot_ref, key_rot_ref, values_ref, query_unit_ref, key_unit_ref, stats_ref, context_ref,
    seq, w_query, w_key, w_value, w_out, partial, query_rot, key_rot, values, query_unit, key_unit,
    stats, context, load_sems, save_sems, gather_send, gather_recv, *scratch,
):
    place = Place()
    count, width = inputs_ref.shape
    experts = picks_ref.shape[1]
    loads = [
        pltpu.make_async_copy(source, target, load_sems.at[i])
        for i, (source, target) in enumerate(
            (
                (w_key_ref, w_key), (w_value_ref, w_value),
                (w_query_ref, w_query), (w_out_ref, w_out),
            )
        )
    ]
    for load in loads:
        load.start()
    float_in = inputs_ref[...].astype(F32)
    first_scale = inverse_rms(float_in)
    own = pl.ds(place.x * count, count)
    seq[own] = (float_in * first_scale * attn_gain_ref[...]).astype(BF16)
    greet([place.on_line(1), place.on_line(-1)])
    run(line_gather_steps(place, seq, count, (gather_send, gather_recv)))
    for load in loads:
        load.wait()
    attend(seq, w_query, w_key, w_value, q_gain_ref, k_gain_ref, cos_ref, sin_ref,
           query_rot, key_rot, values, query_unit, key_unit, stats, context)
    for n in range(0, width, 512):
        here = pl.ds(n, 512)
        partial[:, here] = dot(context[...], w_out[:, here], NN).astype(BF16)
    steps = line_scatter_steps(place, partial, count, scratch)
    next(steps)
    saves = [
        pltpu.make_async_copy(source, target, save_sems.at[i])
        for i, (source, target) in enumerate(
            (
                (seq, seq_ref), (query_rot, query_rot_ref), (key_rot, key_rot_ref),
                (values, values_ref), (query_unit, query_unit_ref), (key_unit, key_unit_ref),
                (stats, stats_ref), (context, context_ref),
            )
        )
    ]
    for save in saves:
        save.start()
    run(steps)
    in_b = scratch[1]
    attended = partial[own].astype(F32) + in_b[0].astype(F32) + in_b[1].astype(F32)
    hidden = float_in + attended
    hidden_ref[...] = hidden
    second_scale = inverse_rms(hidden)
    mixed = (hidden * second_scale * mlp_gain_ref[...]).astype(BF16)
    mixed_ref[:, :width] = mixed
    logits = dot(mixed, router_ref[...], NT)
    raised = jnp.exp(logits - jnp.max(logits, axis=1, keepdims=True))
    probs = raised / jnp.sum(raised, axis=1, keepdims=True)
    picked = picks_ref[...] * probs
    picked_total = jnp.sum(picked, axis=1, keepdims=True)
    gates = picked / picked_total
    high = gates.astype(BF16)
    low = (gates - high.astype(F32)).astype(BF16)
    mixed_ref[:, width:] = jnp.concatenate([high, low], axis=1)
    state_ref[:, : 2 * experts] = jnp.concatenate([probs, gates], axis=1)
    lane = lax.broadcasted_iota(jnp.int32, (count, 2 * experts), 1)
    extra = jnp.where(lane == 0, picked_total, jnp.where(lane == 1, second_scale, first_scale))
    state_ref[:, 2 * experts :] = extra
    for save in saves:
        save.wait()


def forward(inputs, attn_gain, q_gain, k_gain, cosine, sine, mlp_gain, router_t, picks,
            w_query, w_key, w_value, w_out, collective_id):
    count, width = inputs.shape
    head = cosine.shape[1]
    length = 4 * count
    wide = w_query.shape[1]
    saved = [
        ((length, width), BF16), ((length, wide), BF16), ((length, head), BF16),
        ((length, head), BF16), ((length, wide), F32), ((length, head), F32),
        ((length, head), F32), ((length, wide), BF16),
    ]
    kept = [pltpu.VMEM(dims, dtype) for dims, dtype in saved]
    return pl.pallas_call(
        forward_kernel,
        out_shape=(
            shape((count, width + 128)),
            shape((count, width), F32),
            shape((count, 256), F32),
            *[shape(dims, dtype) for dims, dtype in saved],
        ),
        in_specs=[VMEM] * 9 + [ANY] * 4,
        out_specs=(VMEM, VMEM, VMEM, *[ANY] * 8),
        scratch_shapes=[
            kept[0],
            *[pltpu.VMEM(w.shape, BF16) for w in (w_query, w_key, w_value, w_out)],
            pltpu.VMEM((length, width), BF16),
            *kept[1:],
            *dma_sems(4, 8, 4, 4),
            *line_scatter_scratch(count, width),
        ],
        compiler_params=pltpu.CompilerParams(
            collective_id=collective_id, has_side_effects=True, vmem_limit_bytes=60 * 2**20
        ),
        cost_estimate=pl.CostEstimate(flops=7 * 10**10, bytes_accessed=10**8, transcendentals=0),
        name="forward",
    )(inputs, attn_gain, q_gain, k_gain, cosine, sine, mlp_gain, router_t, picks,
      w_query, w_key, w_value, w_out)


def backward_kernel(
    grad_att_ref, inputs_ref, attn_gain_ref, q_gain_ref, k_gain_ref, cos_ref, sin_ref, state_ref,
    grad_hidden_ref, router_grad_ref, mlp_grad_ref,
    gw_b_ref, seq_ref, w_query_ref, w_key_ref, w_value_ref, w_out_ref,
    query_rot_ref, key_rot_ref, values_ref, query_unit_ref, key_unit_ref, stats_ref, context_ref,
    grad_inputs_ref, router_out_ref, gains_out_ref, all_w_ref, right_b_ref, left_b_ref,
    sum_left_ref, sum_right_ref,
    grad_rows, seq, w_query, w_key, w_value, w_out,
    query_rot, key_rot, values, query_unit, key_unit, stats, context,
    grad_context, grad_qkv, summed, out_w, qkv_w, gains,
    late, late_in, router_all, both_sum, load_sems, line_send, line_recv, second_send, second_recv,
    *scratch,
):
    place = Place()
    count, width = inputs_ref.shape
    experts = router_grad_ref.shape[0]
    head = cos_ref.shape[1]
    pairs = (
        (context_ref, context), (w_out_ref, w_out), (query_rot_ref, query_rot),
        (key_rot_ref, key_rot), (values_ref, values), (stats_ref, stats),
        (query_unit_ref, query_unit), (key_unit_ref, key_unit), (w_query_ref, w_query),
        (w_key_ref, w_key), (w_value_ref, w_value), (seq_ref, seq),
    )
    loads = [
        pltpu.make_async_copy(source, target, load_sems.at[i])
        for i, (source, target) in enumerate(pairs)
    ]
    for load in loads:
        load.start()
    own = pl.ds(place.x * count, count)
    grad_rows[own] = grad_att_ref[...]
    far = {
        "x": [place.on_line(step) for step in (1, -1, 2)],
        "z": [place.device("z", step) for step in (1, -1, 2)],
        "y": [place.device("y", step) for step in (1, -1, 2)],
        "core": [place.device(other=1)],
    }
    greet([device for axis in ("x", "z", "y", "core") for device in far[axis]])
    line = line_gather_steps(place, grad_rows, count, (line_send, line_recv))
    next(line)

    run(line)

    half = width // 2
    for load in loads[:2]:
        load.wait()
    for n in range(0, width, 512):
        where = (pl.ds((n // half) * context.shape[1], context.shape[1]), pl.ds(n % half, 512))
        out_w[where] = dot(context[...], grad_rows[:, pl.ds(n, 512)], TN).astype(BF16)

    def scattered(weights, columns, scratch):
        rows = weights.shape[0] // 32

        def block(dz, dy, other):
            return weights.at[pl.ds(place.block("z", dz, dy, other) * rows, rows)]

        def finish(row, value):
            both_sum[pl.ds(row, 16), columns] = value.astype(BF16)

        return plane_scatter_steps(place, rows, lambda dz, dy: None, block, scratch, finish)

    out_width = out_w.shape[1]
    scatter_out, scratch = scratch[:9], scratch[9:]
    scatter_qkv, scratch = scratch[:9], scratch[9:]
    gather_both, scratch = scratch[:4], scratch[4:]
    late_send, late_recv, keep_sem, *scratch = scratch
    sums_scratch, scratch = scratch[:6], scratch[6:]

    def out_total():
        return scattered(out_w, pl.ds(0, out_width), scatter_out)

    outs = out_total()
    next(outs)
    sums = first_sums_steps(place, gw_b_ref, sum_left_ref, sum_right_ref, *sums_scratch)
    next(sums)
    for load in loads[2:]:
        load.wait()
    back = attend_back(grad_rows, seq, w_query, w_key, w_value, w_out, q_gain_ref, k_gain_ref,
                       cos_ref, sin_ref, query_rot, key_rot, values, query_unit, key_unit, stats,
                       grad_context, grad_qkv, gains)
    gains[...] = jnp.zeros_like(gains)
    for _ in back:
        next(outs, None)
    heads = query_rot.shape[1]
    block_rows = summed.shape[0] // 4
    part = experts // 4
    for i in range(4):
        router = router_grad_ref[pl.ds(i * part, part)]
        high = router.astype(BF16)
        summed[pl.ds(i * block_rows + count, part)] = high
        summed[pl.ds(i * block_rows + count + part, part)] = (router - high.astype(F32)).astype(BF16)
    for n in range(0, width, 512):
        here = pl.ds(n, 512)
        value = dot(grad_qkv[:, :heads], w_query[here], NT)
        value = value + dot(grad_qkv[:, heads : heads + head], w_key[here], NT)
        value = value + dot(grad_qkv[:, heads + head :], w_value[here], NT)
        for i in range(4):
            summed[pl.ds(i * block_rows, count), here] = value[i * count : (i + 1) * count].astype(BF16)
    line_scatter = scratch
    line = line_scatter_steps(place, summed, block_rows, line_scatter)
    next(line)
    for n in range(0, grad_qkv.shape[1], 256):
        here = pl.ds(n, 256)
        qkv_w[:, here] = dot(seq[...], grad_qkv[:, here], TN).astype(BF16)

    rows = both_sum.shape[0]

    def qkv_total():
        yield from scattered(qkv_w, pl.ds(out_width, qkv_w.shape[1]), scatter_qkv)
        for _ in outs:
            pass
        keep = pltpu.make_async_copy(
            both_sum, all_w_ref.at[pl.ds(place.block() * rows, rows)], keep_sem.at[0]
        )
        keep.start()
        yield from plane_gather_steps(
            place, both_sum, lambda at: all_w_ref.at[pl.ds(at * rows, rows)], gather_both
        )
        keep.wait()

    second = second_sends(
        place, gw_b_ref, sum_left_ref, sum_right_ref, right_b_ref, left_b_ref, second_send, second_recv
    )
    for copy in second[:2]:
        copy.start()
    run(sums)
    for copy in second[2:]:
        copy.start()
    qkvs = qkv_total()
    next(qkvs)
    next(line)
    for _ in range(4):
        next(qkvs, None)
    run(line)
    in_b = line_scatter[1]

    def line_total(start, size):
        here = pl.ds(start, size)
        total = summed[pl.ds(place.x * block_rows + start, size)].astype(F32)
        return total + in_b[0, here].astype(F32) + in_b[1, here].astype(F32)

    grad_normed = line_total(0, count)
    late[...] = jnp.zeros_like(late)
    late[:part] = line_total(count, part) + line_total(count + part, part)
    float_in = inputs_ref[...].astype(F32)
    first_scale = state_ref[:, 2 * experts + 2 : 2 * experts + 3]
    grad_inputs_ref[...] = (
        grad_hidden_ref[...] + norm_back(float_in, first_scale, attn_gain_ref[...], grad_normed)
    ).astype(BF16)
    late[part : part + 1, :] = jnp.sum(grad_normed * float_in * first_scale, axis=0, keepdims=True)
    late[part + 1 : part + 2, :head] = gains[0:1, :]
    late[part + 1 : part + 2, head : 2 * head] = gains[1:2, :]
    late[part + 2 : part + 3, :] = mlp_grad_ref[...]

    def late_total():
        base = 0
        for axis in ("x", "z", "y", "core"):
            peers = far[axis]
            span = pl.ds(part, 8) if axis == "x" else pl.ds(0, part + 8)
            copies = [
                remote(late.at[span], late_in.at[base + i, span], late_send.at[base + i],
                       late_recv.at[base + i], device)
                for i, device in enumerate(peers)
            ]
            for copy in copies:
                copy.start()
            yield
            for copy in copies:
                copy.wait()
            total = late[span]
            for i in range(len(peers)):
                total = total + late_in[base + i, span]
            late[span] = total
            base += len(peers)
        router_all[place.x] = late[:part]
        mine = router_all.at[place.x]
        copies = [
            remote(mine, mine, late_send.at[base + i], late_recv.at[base + i], device)
            for i, device in enumerate(far["x"])
        ]
        for copy in copies:
            copy.start()
        yield
        for copy in copies:
            copy.wait_send()
        for i, step in enumerate((-1, 1, 2)):
            there = router_all.at[(place.x + step) % 4]
            remote(
                there, there, late_send.at[base + i], late_recv.at[base + i], far["x"][0]
            ).wait_recv()

    lates = late_total()
    running = [qkvs, lates]
    while running:
        for steps in list(running):
            if next(steps, "end") == "end":
                running.remove(steps)
    gains_out_ref[...] = late[part : part + 8]
    for i in range(4):
        router_out_ref[i * part : (i + 1) * part] = router_all[i]
    for copy in second:
        copy.wait()


def backward(grad_att, inputs, attn_gain, q_gain, k_gain, cosine, sine, state, grad_hidden,
             router_grad, mlp_grad, gw_b, weights, saved, collective_id):
    count, width = inputs.shape
    length = 4 * count
    head = cosine.shape[1]
    seq, query_rot, key_rot, values, query_unit, key_unit, stats, context = saved
    w_query, w_key, w_value, w_out = weights
    wide = w_query.shape[1]
    total = wide + 2 * head
    experts = router_grad.shape[0]
    part = experts // 4
    block_rows = count + 2 * part
    rows = width // 32
    shard = gw_b.shape[1] // 4
    like = lambda array: pltpu.VMEM(array.shape, array.dtype)
    return pl.pallas_call(
        backward_kernel,
        out_shape=(
            shape((count, width)),
            shape((experts, width), F32),
            shape((8, width), F32),
            shape((width, width // 2 + total)),
            *[shape((3, shard, width))] * 2,
            *[shape((3, shard // 2, width))] * 2,
        ),
        in_specs=[VMEM] * 11 + [ANY] * 13,
        out_specs=(VMEM, VMEM, VMEM) + (ANY,) * 5,
        scratch_shapes=[
            pltpu.VMEM((length, width), BF16),
            *[like(a) for a in (seq, w_query, w_key, w_value, w_out)],
            *[like(a) for a in saved[1:]],
            pltpu.VMEM((length, wide), BF16),
            pltpu.VMEM((length, total), BF16),
            pltpu.VMEM((4 * block_rows, width), BF16),
            pltpu.VMEM((2 * wide, width // 2), BF16),
            pltpu.VMEM((width, total), BF16),
            pltpu.VMEM((8, head), F32),
            pltpu.VMEM((part + 8, width), F32),
            pltpu.VMEM((10, part + 8, width), F32),
            pltpu.VMEM((4, part, width), F32),
            pltpu.VMEM((rows, width // 2 + total), BF16),
            *dma_sems(12, 4, 4, 4, 4),
            *scatter_scratch(2 * wide // 32, width // 2),
            *scatter_scratch(rows, total),
            *gather_sems(),
            *dma_sems(13, 13, 1),
            *first_sums_scratch(shard // 2, width),
            *line_scatter_scratch(block_rows, width),
        ],
        compiler_params=pltpu.CompilerParams(
            collective_id=collective_id, has_side_effects=True, vmem_limit_bytes=62 * 2**20
        ),
        cost_estimate=pl.CostEstimate(flops=10**11, bytes_accessed=10**8, transcendentals=0),
        name="backward",
    )(grad_att, inputs, attn_gain, q_gain, k_gain, cosine, sine, state, grad_hidden, router_grad,
      mlp_grad, gw_b, seq, w_query, w_key, w_value, w_out, *saved[1:])


def along_line(value, step):
    return lax.ppermute(value, "tensor", [(i, (i + step) % 4) for i in range(4)])


def per_device(
    inputs,
    attn_gain,
    w_query,
    w_key,
    w_value,
    q_gain,
    k_gain,
    w_out,
    mlp_gain,
    w_router,
    w_gate,
    w_up,
    w_down,
    routes,
    grad_out,
):
    row_count, model_width = inputs.shape
    head_size = q_gain.shape[0]
    expert_count = w_router.shape[1]
    place = lax.axis_index("expert")
    first = (2 * place).astype(jnp.int32).reshape(1)

    chosen = routes[:, :, None] == jnp.arange(expert_count, dtype=jnp.int32)[None, None, :]
    picks = jnp.sum(chosen.astype(F32), axis=1)
    before = (jnp.arange(row_count)[:, None] > jnp.arange(row_count)[None, :]).astype(BF16)
    rank = jnp.dot(before, picks.astype(BF16), preferred_element_type=F32)
    base = 20 * ((place // 4) % 2 * 2 + place % 2)
    slots = jnp.where(picks > 0.0, rank + base.astype(F32), -1.0)
    slots = jnp.concatenate([slots, jnp.full_like(slots, -1.0)], axis=1).astype(BF16)
    dout_all = lax.all_gather(jnp.concatenate([grad_out, slots], axis=1), "expert", axis=0)

    gate_t = jnp.swapaxes(w_gate, 1, 2)
    up_t = jnp.swapaxes(w_up, 1, 2)
    own = [jnp.stack([gate_t[j], up_t[j], w_down[j]]) for j in range(2)]
    half = own[0].shape[1] // 2
    cosine, sine = rope_tables(4 * row_count, head_size)
    router_t = w_router.T
    q_gain, k_gain = q_gain[None], k_gain[None]
    attn_gain, mlp_gain = attn_gain[None], mlp_gain[None]
    left_a, right_a = along_line(own[0], 1), along_line(own[0], -1)
    mixed, hidden, state, *saved = forward(
        inputs, attn_gain, q_gain, k_gain, cosine, sine, mlp_gain, router_t, picks,
        w_query, w_key, w_value, w_out, 0,
    )

    mixed, left_a, right_a, own[1] = lax.optimization_barrier((mixed, left_a, right_a, own[1]))
    low_a, high_a = along_line(left_a[:, :half], 1), along_line(right_a[:, half:], -1)
    left_b, right_b = along_line(own[1], 1), along_line(own[1], -1)
    grad_a, grad_b, rows_a, rows_b, gate_a, gate_b = gather_select(mixed, dout_all, 1)
    rows_a, left_b, right_b, low_a, high_a = lax.optimization_barrier(
        (rows_a, left_b, right_b, low_a, high_a)
    )
    low_b, high_b = along_line(left_b[:, :half], 1), along_line(right_b[:, half:], -1)
    out_a, back_a, gw_a = expert_layer(
        first, (own[0], left_a, right_a, low_a, high_a), rows_a, grad_a, gate_a
    )
    rows_b, back_a = lax.optimization_barrier((rows_b, back_a))
    out_b, back_b, gw_b, sum_left_a, sum_right_a = expert_layer(
        first + 1, (own[1], left_b, right_b, low_b, high_b), rows_b, grad_b, gate_b, gw_a, 4
    )
    shares, right_a, left_a, grad_hidden, grad_att, router_grad, mlp_grad = combine_scatter(
        (back_a, back_b), (out_a, out_b), dout_all, (gw_a, sum_left_a, sum_right_a), grad_out,
        hidden, mixed, state, picks, mlp_gain, router_t, 2,
    )
    expert_mix = lax.psum_scatter(
        shares.reshape(-1, model_width), "expert", scatter_dimension=0, tiled=True
    )
    output = (hidden + expert_mix.astype(F32)).astype(BF16)

    results = backward(
        grad_att, inputs, attn_gain, q_gain, k_gain, cosine, sine, state, grad_hidden,
        router_grad, mlp_grad, gw_b, (w_query, w_key, w_value, w_out), saved, 3,
    )
    grad_inputs, router_grad, gains, all_w, right_b, left_b, _, _ = results
    wide, narrow = w_query.shape[1], w_key.shape[1]
    start = model_width // 2
    out_w = jnp.concatenate([all_w[:wide, :start], all_w[wide:, :start]], axis=1).astype(F32)
    query_w = all_w[:, start : start + wide].astype(F32)
    key_w = all_w[:, start + wide : start + wide + narrow].astype(F32)
    value_w = all_w[:, start + wide + narrow :].astype(F32)

    def line_total(i):
        shard = w_down.shape[1]
        return jnp.stack([
            gw[i, :shard].astype(F32) + right[i].astype(F32) + left[i].astype(F32)
            for gw, right, left in ((gw_a, right_a, left_a), (gw_b, right_b, left_b))
        ])

    return (
        output,
        grad_inputs,
        gains[0],
        query_w,
        key_w,
        value_w,
        gains[1, :head_size],
        gains[1, head_size : 2 * head_size],
        out_w,
        gains[2],
        router_grad.T,
        jnp.swapaxes(line_total(0), 1, 2),
        jnp.swapaxes(line_total(1), 1, 2),
        line_total(2),
    )


def solution(mesh):
    placed = (
        P(("expert", "tensor"), None),
        P(),
        P(None, "tensor"),
        P(None, "tensor"),
        P(None, "tensor"),
        P(),
        P(),
        P("tensor", None),
        P(),
        P(),
        P("expert", None, "tensor"),
        P("expert", None, "tensor"),
        P("expert", "tensor", None),
        P(("expert", "tensor"), None),
        P(("expert", "tensor"), None),
    )
    return jax.shard_map(
        per_device,
        mesh=mesh,
        in_specs=placed,
        out_specs=(
            P(("expert", "tensor"), None),
            P(("expert", "tensor"), None),
            P(),
            P(None, "tensor"),
            P(None, "tensor"),
            P(None, "tensor"),
            P(),
            P(),
            P("tensor", None),
            P(),
            P(),
            P("expert", None, "tensor"),
            P("expert", None, "tensor"),
            P("expert", "tensor", None),
        ),
        check_vma=False,
    )
```

```python
import functools

import jax
import jax.numpy as jnp
from jax import lax
from jax.experimental import pallas as pl
from jax.experimental.pallas import tpu as pltpu
from jax.sharding import PartitionSpec as P

MESH = pl.DeviceIdType.MESH
F32 = jnp.float32
BF16 = jnp.bfloat16
EPSILON = 1e-06
ROPE_BASE = 1000000.0
MASK_VALUE = -1e30
NT = (((1,), (1,)), ((), ()))
TN = (((0,), (0,)), ((), ()))
NN = (((1,), (0,)), ((), ()))
OTHER = {"z": "y", "y": "z"}
ANY = pl.BlockSpec(memory_space=pl.ANY)
VMEM = pl.BlockSpec(memory_space=pltpu.VMEM)
SMEM = pl.BlockSpec(memory_space=pltpu.SMEM)


def dot(left, right, dims):
    return lax.dot_general(left, right, dims, preferred_element_type=F32)


def shape(dims, dtype=BF16):
    return jax.ShapeDtypeStruct(tuple(dims), dtype)


def dma_sems(*counts):
    return [pltpu.SemaphoreType.DMA((count,)) for count in counts]


class Place:
    def __init__(self):
        e = lax.axis_index("expert")
        self.x = lax.axis_index("tensor")
        self.z = e // 8
        self.y = (e // 2) % 4
        self.core = e % 2

    def block(self, axis="z", a=0, b=0, other=0):
        dz, dy = (a, b) if axis == "z" else (b, a)
        core = (self.core + other) % 2
        return ((self.z + dz) % 4) * 8 + ((self.y + dy) % 4) * 2 + core

    def device(self, axis="z", a=0, b=0, other=0):
        return (self.block(axis, a, b, other), self.x)

    def on_line(self, step):
        return (self.block(), (self.x + step) % 4)


def greet(devices):
    barrier = pltpu.get_barrier_semaphore()
    for device in devices:
        pl.semaphore_signal(barrier, inc=1, device_id=device, device_id_type=MESH)
    pl.semaphore_wait(barrier, len(devices))


def plane_neighbours(place):
    return [
        place.device("z", 1),
        place.device("z", -1),
        place.device("y", 1),
        place.device("y", -1),
        place.device(other=1),
    ]


def run(steps):
    for _ in steps:
        pass


def remote(source, target, send_sem, recv_sem, device):
    return pltpu.make_async_remote_copy(
        src_ref=source, dst_ref=target, send_sem=send_sem, recv_sem=recv_sem,
        device_id=device, device_id_type=MESH,
    )


def gather_plan():
    stages = [[], [], [], []]
    for half, first in ((0, "y"), (1, "z")):
        for side in (-1, 1):
            stages[0].append((first, half, side, 0, None, ("f", side)))
            stages[0].append((first, half, 0, side, None, ("s", side)))
    for half, first in ((0, "y"), (1, "z")):
        for quarter, side in ((0, -1), (1, 1)):
            stages[1].append((first, half, 2, 0, quarter, ("f", side)))
        for f in (-1, 1):
            for side in (-1, 1):
                stages[1].append((first, half, f, side, None, ("s", side)))
        for quarter, side in ((0, -1), (1, 1)):
            stages[1].append((first, half, 0, 2, quarter, ("s", side)))
    for half, first in ((0, "y"), (1, "z")):
        for quarter in (0, 1):
            for side in (-1, 1):
                stages[2].append((first, half, 2, side, quarter, ("s", side)))
        for f in (-1, 1):
            for quarter, side in ((0, -1), (1, 1)):
                stages[2].append((first, half, f, 2, quarter, ("s", side)))
    for half, first in ((0, "y"), (1, "z")):
        for quarter, side in ((0, -1), (1, 1)):
            stages[3].append((first, half, 2, 2, quarter, ("s", side)))
    return stages


STAGES = gather_plan()
PIECES = [piece for stage in STAGES for piece in stage]
PIECE_AT = {piece: at for at, piece in enumerate(PIECES)}


def onward(piece):
    first, half, f, s, quarter, (leg, side) = piece
    found = []
    for target in PIECES:
        _, t_half, t_f, t_s, t_quarter, (t_leg, t_side) = target
        if t_half != half or (quarter is not None and t_quarter != quarter):
            continue
        if t_leg == "f":
            take = t_f == 2 and leg == "f" and f == t_side and s == 0
        elif t_s == 2:
            take = leg == "s" and s == t_side and f == t_f
        else:
            take = leg == "f" and s == 0 and f == t_f
        if take:
            found.append(target)
    return found


def plane_gather_steps(place, x_ref, blocks, sems):
    send_sems, recv_sems, core_send, core_recv = sems
    rows = x_ref.shape[0]
    sibling = place.device(other=1)

    def span(half, quarter):
        if quarter is None:
            return pl.ds(half * (rows // 2), rows // 2)
        return pl.ds(half * (rows // 2) + quarter * (rows // 4), rows // 4)

    def send(target, source, f, s):
        first, half, _, _, quarter, (leg, side) = target
        at = PIECE_AT[target]
        copy = remote(
            source.at[span(half, quarter)],
            blocks(place.block(first, f, s)).at[span(half, quarter)],
            send_sems.at[at], recv_sems.at[at],
            place.device(first if leg == "f" else OTHER[first], -side),
        )
        copy.start()
        return copy

    started = [send(piece, x_ref, 0, 0) for piece in STAGES[0]]
    last = len(PIECES)
    core_copies = [
        remote(x_ref, blocks(place.block()), core_send.at[last], core_recv.at[last], sibling)
    ]
    core_copies[0].start()
    yield -1
    for number, stage in enumerate(STAGES):
        for piece in stage:
            first, half, f, s, quarter, _ = piece
            at = PIECE_AT[piece]
            block = blocks(place.block(first, f, s))
            view = block.at[span(half, quarter)]
            remote(view, view, send_sems.at[at], recv_sems.at[at], sibling).wait_recv()
            for target in onward(piece):
                started.append(send(target, block, f, s))
            copy = remote(view, view, core_send.at[at], core_recv.at[at], sibling)
            copy.start()
            core_copies.append(copy)
            yield number
        if number == 0:
            other = blocks(place.block(other=1))
            remote(other, other, core_send.at[last], core_recv.at[last], sibling).wait_recv()
        for piece in stage:
            first, half, f, s, quarter, _ = piece
            at = PIECE_AT[piece]
            view = blocks(place.block(first, f, s, 1)).at[span(half, quarter)]
            remote(view, view, core_send.at[at], core_recv.at[at], sibling).wait_recv()
        yield number + 100
    for copy in started + core_copies:
        copy.wait_send()


def gather_sems():
    count = len(PIECES)
    return dma_sems(count, count, count + 1, count + 1)


def scatter_scratch(rows, width):
    return [
        pltpu.VMEM((16, rows, width), BF16),
        pltpu.VMEM((2, 4, 2, rows // 4, width), BF16),
        pltpu.VMEM((2, 4, 2, rows // 2, width), BF16),
        pltpu.VMEM((2, 2, rows // 4, width), BF16),
        pltpu.VMEM((2, 2, rows // 2, width), BF16),
        *dma_sems(16, 16, 40, 40),
    ]


def plane_scatter_steps(place, rows, make, block, scratch, finish):
    other, in_a, in_b, in_c, in_d, core_send, core_recv, send_sems, recv_sems = scratch
    half_rows, quarter_rows = rows // 2, rows // 4
    exchanged, ready, sent = {}, set(), []

    def exchange(dz, dy):
        at = dz * 4 + dy
        if at in exchanged:
            return
        make(dz, dy)
        exchanged[at] = remote(
            block(dz, dy, 1), other.at[at], core_send.at[at], core_recv.at[at],
            place.device(other=1),
        )
        exchanged[at].start()

    def add_rows(into, start, count, source):
        @pl.loop(0, count, step=16)
        def _(row):
            here = pl.ds(start + row, 16)
            total = into[here].astype(F32) + source[pl.ds(row, 16)].astype(F32)
            into[here] = total.astype(BF16)

    def where(axis, a, b):
        dz, dy = (a, b) if axis == "z" else (b, a)
        return dz % 4, dy % 4

    def ready_block(axis, a, b):
        dz, dy = where(axis, a, b)
        at = dz * 4 + dy
        if at not in ready:
            ready.add(at)
            exchange(dz, dy)
            exchanged[at].wait_recv()
            add_rows(block(dz, dy, 0), 0, rows, other.at[at])
        return block(dz, dy, 0)

    def send(source, target, number, device):
        copy = remote(source, target, send_sems.at[number], recv_sems.at[number], device)
        copy.start()
        sent.append(copy)

    def arrive(target, number):
        remote(
            target, target, send_sems.at[number], recv_sems.at[number], place.device("z", 1)
        ).wait_recv()

    axes = (("z", "y"), ("y", "z"))
    sides = ((0, 1), (1, -1))
    lines = (2, 1, 3, 0)
    first_needs = []
    for line in lines:
        for first, _ in axes:
            if where(first, 2, line) not in first_needs:
                first_needs.append(where(first, 2, line))
    for dz, dy in first_needs[:4]:
        exchange(dz, dy)
    yield
    for line in lines:
        for half, (first, second) in enumerate(axes):
            for dz, dy in first_needs:
                if (dz, dy) not in [where(first, 2, line)] and dz * 4 + dy not in exchanged:
                    exchange(dz, dy)
                    break
            held = ready_block(first, 2, line)
            for quarter, side in sides:
                rows_here = pl.ds(half * half_rows + quarter * quarter_rows, quarter_rows)
                send(held.at[rows_here], in_a.at[half, line, quarter],
                     (half * 4 + line) * 2 + quarter, place.device(first, side))
        yield
    for dz in (1, 3, 0, 2):
        for dy in (1, 3, 0, 2):
            exchange(dz, dy)
    yield
    for line in lines:
        for half, (first, second) in enumerate(axes):
            for quarter, side in sides:
                held = ready_block(first, side, line)
                number = (half * 4 + line) * 2 + quarter
                arrive(in_a.at[half, line, quarter], number)
                add_rows(held, half * half_rows + quarter * quarter_rows, quarter_rows,
                         in_a.at[half, line, quarter])
                send(held.at[pl.ds(half * half_rows, half_rows)],
                     in_b.at[half, line, quarter], 16 + number, place.device(first, side))
        yield
    for line in lines:
        for half, (first, second) in enumerate(axes):
            held = ready_block(first, 0, line)
            for quarter in (0, 1):
                number = (half * 4 + line) * 2 + quarter
                arrive(in_b.at[half, line, quarter], 16 + number)
                add_rows(held, half * half_rows, half_rows, in_b.at[half, line, quarter])
            if line == 2:
                for quarter, side in sides:
                    rows_here = pl.ds(half * half_rows + quarter * quarter_rows, quarter_rows)
                    send(held.at[rows_here], in_c.at[half, quarter],
                         32 + half * 2 + quarter, place.device(second, side))
            if line in (1, 3):
                quarter, side = sides[0] if line == 1 else sides[1]
                number = 32 + half * 2 + quarter
                arrive(in_c.at[half, quarter], number)
                add_rows(held, half * half_rows + quarter * quarter_rows, quarter_rows,
                         in_c.at[half, quarter])
                send(held.at[pl.ds(half * half_rows, half_rows)], in_d.at[half, quarter],
                     36 + half * 2 + quarter, place.device(second, side))
        yield
    held = block(0, 0, 0)
    for half in (0, 1):
        for quarter in (0, 1):
            arrive(in_d.at[half, quarter], 36 + half * 2 + quarter)

        @pl.loop(0, half_rows, step=16)
        def _(row):
            here = pl.ds(half * half_rows + row, 16)
            total = held[here].astype(F32)
            for quarter in (0, 1):
                total = total + in_d[half, quarter, pl.ds(row, 16)].astype(F32)
            finish(half * half_rows + row, total)

    for copy in sent:
        copy.wait_send()
    for at in exchanged:
        exchanged[at].wait_send()


def line_gather_steps(place, out_ref, rows, sems):
    send_sems, recv_sems = sems
    half = rows // 2

    def part(step, start, count):
        return out_ref.at[pl.ds(((place.x + step) % 4) * rows + start, count)]

    def copy(view, number, side):
        return remote(view, view, send_sems.at[number], recv_sems.at[number], place.on_line(side))

    copies = [copy(part(0, 0, rows), 0, 1), copy(part(0, 0, rows), 1, -1)]
    for c in copies:
        c.start()
    yield
    copy(part(-1, 0, rows), 0, 1).wait_recv()
    copies.append(copy(part(-1, 0, half), 2, 1))
    copies[2].start()
    copy(part(1, 0, rows), 1, -1).wait_recv()
    copies.append(copy(part(1, half, half), 3, -1))
    copies[3].start()
    yield
    copy(part(2, 0, half), 2, 1).wait_recv()
    copy(part(2, half, half), 3, -1).wait_recv()
    for c in copies:
        c.wait_send()


def line_scatter_scratch(rows, width):
    return [
        pltpu.VMEM((2, rows // 2, width), BF16),
        pltpu.VMEM((2, rows, width), BF16),
        *dma_sems(4, 4),
    ]


def line_scatter_steps(place, c_ref, rows, scratch):
    in_a, in_b, send_sems, recv_sems = scratch
    half = rows // 2

    def part(step, start, count):
        return c_ref.at[pl.ds(((place.x + step) % 4) * rows + start, count)]

    def copy(source, target, number, side):
        return remote(
            source, target, send_sems.at[number], recv_sems.at[number], place.on_line(side)
        )

    copies = [
        copy(part(2, 0, half), in_a.at[0], 0, 1),
        copy(part(2, half, half), in_a.at[1], 1, -1),
    ]
    for c in copies:
        c.start()
    yield

    def add(view, source):
        @pl.loop(0, half, step=16)
        def _(row):
            here = pl.ds(row, 16)
            view[here] = (view[here].astype(F32) + source[here].astype(F32)).astype(BF16)

    copies[0].wait_recv()
    add(part(1, 0, half), in_a.at[0])
    copies.append(copy(part(1, 0, rows), in_b.at[0], 2, 1))
    copies[2].start()
    copies[1].wait_recv()
    add(part(-1, half, half), in_a.at[1])
    copies.append(copy(part(-1, 0, rows), in_b.at[1], 3, -1))
    copies[3].start()
    yield
    copies[2].wait_recv()
    copies[3].wait_recv()
    for c in copies:
        c.wait_send()


SLOTS = 80
GROUPS = [(dz, dy) for dz in (0, 1, 3, 2) for dy in (0, 1)]


def chosen_rows(slots, first):
    value = slots.astype(F32)
    lane = lax.broadcasted_iota(jnp.int32, value.shape, 1)
    slot = lax.broadcasted_iota(jnp.int32, (value.shape[0], 2 * SLOTS), 1).astype(F32)
    found = []
    for j in range(2):
        mine = jnp.sum(jnp.where(lane == first + j, value, 0.0), axis=1, keepdims=True)
        found.append(jnp.where(mine >= 0.0, mine + float(j * SLOTS), -1.0))
    return jnp.where((slot == found[0]) | (slot == found[1]), 1.0, 0.0).astype(BF16)


def group_blocks(place, dz, dy):
    z = (place.z + dz) % 4
    return [z * 8 + ((place.y + dy + two) % 4) * 2 for two in (0, 2)]


def gather_select_kernel(
    x_ref, grads_ref, gate_w_ref, up_w_ref, down_w_ref, left_gate_ref, right_gate_ref,
    left_two_ref, right_two_ref, low_ref, high_ref, left_next_ref, right_next_ref,
    all_ref, grad_a_ref, grad_b_ref, row_a_ref, row_b_ref, gate_a_ref, gate_b_ref,
    tokens, slots, rows_a, rows_b, grads_a, grads_b, gates_a, gates_b,
    own_sem, load_sems, save_sems, line_send, line_recv, *sems,
):
    place = Place()
    first = 2 * lax.axis_index("expert")
    width = rows_a.shape[1]
    greet(plane_neighbours(place) + [place.on_line(1), place.on_line(-1)])
    line = line_weights_steps(
        place, gate_w_ref, up_w_ref, down_w_ref, left_gate_ref, right_gate_ref, left_two_ref,
        right_two_ref, low_ref, high_ref, left_next_ref, right_next_ref, line_send, line_recv,
    )
    next(line)
    own = pltpu.make_async_copy(x_ref, all_ref.at[place.block()], own_sem.at[0])
    own.start()
    steps = plane_gather_steps(place, x_ref, lambda at: all_ref.at[at], sems)
    next(steps)

    def loads_of(source, number, slot):
        dz, dy = GROUPS[number]
        return [
            pltpu.make_async_copy(
                source.at[pl.ds(at, 2)], tokens.at[slot, pl.ds(2 * i, 2)], load_sems.at[2 * slot + i]
            )
            for i, at in enumerate(group_blocks(place, dz, dy))
        ]

    saves = []

    def save(value_ref, target, number, slot):
        here = pl.ds(number * SLOTS, SLOTS)
        copy = pltpu.make_async_copy(value_ref.at[here], target.at[here], save_sems.at[slot])
        copy.start()
        saves.append(copy)

    def select(number, slot, is_grad):
        for load in loads_of(grads_ref if is_grad else all_ref, number, slot):
            load.wait()
        here = pl.ds(number * SLOTS, SLOTS)
        block = tokens[slot].reshape(512, width + 128)
        if is_grad:
            slots[number] = block[:, width:]
        rows = dot(chosen_rows(slots[number], first), block, TN)
        a, b = (grads_a, grads_b) if is_grad else (rows_a, rows_b)
        a[here] = rows[:SLOTS, :width].astype(BF16)
        b[here] = rows[SLOTS:, :width].astype(BF16)
        base = number * 2 + (16 if is_grad else 0)
        save(a, grad_a_ref if is_grad else row_a_ref, number, base)
        save(b, grad_b_ref if is_grad else row_b_ref, number, base + 1)
        if not is_grad:
            lane = lax.broadcasted_iota(jnp.int32, (SLOTS, 128), 1) % 64
            for j, (gates, target) in enumerate(((gates_a, gate_a_ref), (gates_b, gate_b_ref))):
                part = rows[j * SLOTS : (j + 1) * SLOTS, width:]
                gate = jnp.sum(jnp.where(lane == first + j, part, 0.0), axis=1, keepdims=True)
                gates[here] = jnp.broadcast_to(gate, (SLOTS, 128))
                save(gates, target, number, 32 + number * 2 + j)

    def start(is_grad, number, slot):
        for load in loads_of(grads_ref if is_grad else all_ref, number, slot):
            load.start()

    start(True, 0, 0)
    grad_turn = 0
    pieces = 0
    for stage in steps:
        if stage < 100:
            pieces += 1
            if pieces % 2 == 0 and grad_turn < 8:
                if grad_turn + 1 < 8:
                    start(True, grad_turn + 1, (grad_turn + 1) % 2)
                select(grad_turn, grad_turn % 2, True)
                grad_turn += 1
        elif stage == 101:
            assert grad_turn == 8
            next(line)
            own.wait()
            start(False, 0, 0)
            start(False, 1, 1)
            select(0, 0, False)
            select(1, 1, False)
        elif stage == 102:
            start(False, 2, 0)
            next(line)
            for number in range(2, 6):
                if number + 1 < 6:
                    start(False, number + 1, (number + 1) % 2)
                select(number, number % 2, False)
        elif stage == 103:
            start(False, 6, 0)
            start(False, 7, 1)
            select(6, 0, False)
            select(7, 1, False)
    run(line)
    for copy in saves:
        copy.wait()


def line_weights_steps(
    place, gate_w, up_w, down_w, left_gate, right_gate, left_two, right_two, low, high,
    left_next, right_next, send_sems, recv_sems,
):
    half = gate_w.shape[1] // 2
    first, second = pl.ds(0, half), pl.ds(half, half)
    numbers = iter(range(12))
    started = []

    def send(source, target, side):
        number = next(numbers)
        copy = remote(
            source, target, send_sems.at[number], recv_sems.at[number], place.on_line(side)
        )
        copy.start()
        started.append(copy)
        return copy

    def onward(left, right, matrix):
        send(left.at[first], low.at[matrix], 1)
        send(right.at[second], high.at[matrix], -1)

    near = []
    for i, w in enumerate((up_w, down_w)):
        near.append((send(w.at[0], left_two.at[i], 1), send(w.at[0], right_two.at[i], -1)))
        if i == 0:
            onward(left_gate, right_gate, 0)
    send(gate_w.at[1], left_next, 1)
    send(gate_w.at[1], right_next, -1)
    yield
    for i in range(2):
        for copy in near[i]:
            copy.wait_recv()
        onward(left_two.at[i], right_two.at[i], i + 1)
        yield
    come = [id(copy) for pair in near for copy in pair]
    for copy in started:
        copy.wait_send()
        if id(copy) not in come:
            copy.wait_recv()


def gather_select(x, grads, gate_w, up_w, down_w, left_gate, right_gate, collective_id):
    count, full = x.shape
    width = full - 128
    total = len(GROUPS) * SLOTS
    rows = shape((total, width))
    gate = shape((total, 128), F32)
    shard = gate_w.shape[1]
    two = shape((2, shard, width))
    far = shape((3, shard // 2, width))
    one = shape((shard, width))
    return pl.pallas_call(
        gather_select_kernel,
        out_shape=(
            two, two, far, far, one, one, shape((32, count, full)), rows, rows, rows, rows, gate, gate
        ),
        in_specs=[ANY] * 7,
        out_specs=(ANY,) * 13,
        scratch_shapes=[
            pltpu.VMEM((2, 4, count, full), BF16),
            pltpu.VMEM((8, 512, 128), BF16),
            *[pltpu.VMEM((total, width), BF16)] * 4,
            *[pltpu.VMEM((total, 128), F32)] * 2,
            *dma_sems(1, 4, 48, 12, 12),
            *gather_sems(),
        ],
        compiler_params=pltpu.CompilerParams(
            collective_id=collective_id, has_side_effects=True, vmem_limit_bytes=60 * 2**20
        ),
        cost_estimate=pl.CostEstimate(flops=6 * 10**10, bytes_accessed=10**8, transcendentals=0),
        name="gather_select",
    )(x, grads, gate_w, up_w, down_w, left_gate, right_gate)


def combine_scatter_kernel(
    back_a_ref, back_b_ref, out_a_ref, out_b_ref, slots_ref, gw_ref,
    grad_out_ref, hidden_ref, mixed_ref, state_ref, picks_ref, mlp_gain_ref, router_ref,
    shares_ref, from_right_ref, from_left_ref, sum_left_ref, sum_right_ref,
    grad_hidden_ref, grad_att_ref, grad_router_ref, gain_ref,
    rows, slots, blocks, out_rows, share, total, load_sems, row_sems, share_sems,
    line_send, line_recv, *scratch,
):
    place = Place()
    first = 2 * lax.axis_index("expert")
    count = hidden_ref.shape[0]
    width = hidden_ref.shape[1]
    for number, (dz, dy) in enumerate(GROUPS):
        for i, at in enumerate(group_blocks(place, dz, dy)):
            pltpu.make_async_copy(
                slots_ref.at[pl.ds(at, 2), :, pl.ds(width, 128)], slots.at[number, pl.ds(2 * i, 2)],
                load_sems.at[2 * number + i],
            ).start()
        for j, ref in enumerate((back_a_ref, back_b_ref)):
            pltpu.make_async_copy(
                ref.at[pl.ds(number * SLOTS, SLOTS)], rows.at[number, j],
                load_sems.at[16 + 2 * number + j],
            ).start()
    greet(plane_neighbours(place) + [place.on_line(1), place.on_line(-1)])
    line = second_sends(
        place, gw_ref, sum_left_ref, sum_right_ref, from_right_ref, from_left_ref, line_send,
        line_recv,
    )
    sums = first_sums_steps(place, gw_ref, sum_left_ref, sum_right_ref, *scratch[:6])
    scratch = scratch[6:]
    next(sums)
    for copy in line[:2]:
        copy.start()
    made = set()

    def loaded(number):
        dz, dy = GROUPS[number]
        for i, at in enumerate(group_blocks(place, dz, dy)):
            pltpu.make_async_copy(
                slots_ref.at[pl.ds(at, 2), :, pl.ds(width, 128)], slots.at[number, pl.ds(2 * i, 2)],
                load_sems.at[2 * number + i],
            ).wait()
        for j, ref in enumerate((back_a_ref, back_b_ref)):
            pltpu.make_async_copy(
                ref.at[pl.ds(number * SLOTS, SLOTS)], rows.at[number, j],
                load_sems.at[16 + 2 * number + j],
            ).wait()

    def table_of(number):
        return chosen_rows(slots[number].reshape(512, 128), first)

    def make(dz, dy):
        number = GROUPS.index((dz, dy % 2))
        if number in made:
            return
        made.add(number)
        loaded(number)
        both = rows[number].reshape(2 * SLOTS, width + 128)
        sums = dot(table_of(number), both, NN).astype(BF16).reshape(2, 2, count, width + 128)
        low = dy % 2
        blocks[dz * 4 + low] = sums[0]
        blocks[dz * 4 + low + 2] = sums[1]

    def block(dz, dy, other):
        return blocks.at[dz * 4 + dy, (place.core + other) % 2]

    def finish(row, value):
        total[pl.ds(row, 16)] = value

    def out_loads(number):
        return [
            pltpu.make_async_copy(
                ref.at[pl.ds(number * SLOTS, SLOTS)], out_rows.at[number % 2, j],
                row_sems.at[2 * (number % 2) + j],
            )
            for j, ref in enumerate((out_a_ref, out_b_ref))
        ]

    def share_saves(number):
        dz, dy = GROUPS[number]
        return [
            pltpu.make_async_copy(
                share.at[number % 2, pl.ds(2 * i, 2)], shares_ref.at[pl.ds(at, 2)],
                share_sems.at[2 * (number % 2) + i],
            )
            for i, at in enumerate(group_blocks(place, dz, dy))
        ]

    def make_share(number):
        if number + 1 < len(GROUPS):
            for load in out_loads(number + 1):
                load.start()
        for load in out_loads(number):
            load.wait()
        if number >= 2:
            for save in share_saves(number - 2):
                save.wait()
        both = out_rows[number % 2].reshape(2 * SLOTS, width)
        sums = dot(table_of(number), both, NN).astype(BF16)
        share[number % 2] = sums.reshape(4, count, width)
        for save in share_saves(number):
            save.start()

    for load in out_loads(0):
        load.start()
    turn = 0
    for at, _ in enumerate(plane_scatter_steps(place, count, make, block, scratch, finish)):
        if at == 6:
            run(sums)
            for copy in line[2:]:
                copy.start()
        if at >= 5:
            for _ in range(2):
                if turn < len(GROUPS):
                    make_share(turn)
                    turn += 1
    while turn < len(GROUPS):
        make_share(turn)
        turn += 1

    experts = picks_ref.shape[1]
    probs, gates = state_ref[:, :experts], state_ref[:, experts : 2 * experts]
    picked_total = state_ref[:, 2 * experts : 2 * experts + 1]
    second_scale = state_ref[:, 2 * experts + 1 : 2 * experts + 2]
    tail = total[:, pl.ds(width, 128)]
    gate_grad = tail[:, :experts] + tail[:, experts:]
    mean = jnp.sum(gate_grad * gates, axis=1, keepdims=True)
    prob_grad = picks_ref[...] * (gate_grad - mean) / picked_total
    logit_grad = probs * (prob_grad - jnp.sum(prob_grad * probs, axis=1, keepdims=True))
    logit_grad = logit_grad.astype(BF16)
    grad_router_ref[...] = dot(logit_grad, mixed_ref[:, :width], TN)
    grad_mixed = total[:, :width] + dot(logit_grad, router_ref[...], NN)
    hidden = hidden_ref[...]
    gain_ref[...] = jnp.sum(grad_mixed * hidden * second_scale, axis=0, keepdims=True)
    grad_hidden = grad_out_ref[...].astype(F32) + norm_back(
        hidden, second_scale, mlp_gain_ref[...], grad_mixed
    )
    grad_hidden_ref[...] = grad_hidden
    grad_att_ref[...] = grad_hidden.astype(BF16)
    for number in (len(GROUPS) - 2, len(GROUPS) - 1):
        for save in share_saves(number):
            save.wait()
    for copy in line:
        copy.wait()


def combine_scatter(
    back, out, slots, gw, grad_out, hidden, mixed, state, picks, mlp_gain, router_t, collective_id
):
    count, width = hidden.shape
    groups = len(GROUPS)
    return pl.pallas_call(
        combine_scatter_kernel,
        out_shape=(
            shape((32, count, width)),
            *[shape((3, gw.shape[1] // 4, width))] * 2,
            *[shape((3, gw.shape[1] // 8, width))] * 2,
            shape((count, width), F32),
            shape((count, width)),
            shape(router_t.shape, F32),
            shape((1, width), F32),
        ),
        in_specs=[ANY] * 6 + [VMEM] * 7,
        out_specs=(ANY, ANY, ANY, ANY, ANY, VMEM, VMEM, VMEM, VMEM),
        scratch_shapes=[
            pltpu.VMEM((groups, 2, SLOTS, width + 128), BF16),
            pltpu.VMEM((groups, 4, count, 128), BF16),
            pltpu.VMEM((16, 2, count, width + 128), BF16),
            pltpu.VMEM((2, 2, SLOTS, width), BF16),
            pltpu.VMEM((2, 4, count, width), BF16),
            pltpu.VMEM((count, width + 128), F32),
            *dma_sems(32, 4, 4, 4, 4),
            *first_sums_scratch(gw.shape[1] // 8, width),
            *scatter_scratch(count, width + 128),
        ],
        compiler_params=pltpu.CompilerParams(
            collective_id=collective_id, has_side_effects=True, vmem_limit_bytes=62 * 2**20
        ),
        cost_estimate=pl.CostEstimate(flops=6 * 10**10, bytes_accessed=10**8, transcendentals=0),
        name="combine_scatter",
    )(*back, *out, slots, gw, grad_out, hidden, mixed, state, picks, mlp_gain, router_t)


def expert_steps(
    expert_ref, parts, receive, x_hbm, d_hbm, gate_hbm, p_hbm, rb_hbm, gw_hbm,
    w, x, d, gate, rg, middle, ggp, gup, p, rb, dots, gw, in_sems, out_sems, gw_sems,
):
    f32, bf16 = jnp.float32, jnp.bfloat16
    rows, width = x.shape
    hidden = middle.shape[1]
    chunk = 256
    loads = [
        pltpu.make_async_copy(x_hbm, x, in_sems.at[0]),
        pltpu.make_async_copy(d_hbm, d, in_sems.at[1]),
        pltpu.make_async_copy(gate_hbm, gate, in_sems.at[2]),
    ]
    for i, (ref, where) in enumerate(parts):
        loads.append(pltpu.make_async_copy(ref, w.at[where], in_sems.at[3 + i]))
    for load in loads:
        load.start()
    if receive is not None:
        next(receive)
    for load in loads:
        load.wait()

    @pl.loop(0, rows, step=16)
    def _(r):
        here = pl.ds(r, 16)
        scaled = d[here].astype(f32) * gate[here, 0:1]
        rg[here] = scaled.astype(bf16)

    def hidden_chunk(c):
        here = pl.ds(c, chunk)
        gate_pre = dot(x[...], w[0, here], NT)
        up_pre = dot(x[...], w[1, here], NT)
        grad_mid = dot(rg[...], w[2, here], NT)
        sig = 1.0 / (1.0 + jnp.exp(-gate_pre))
        act = gate_pre * sig
        middle[:, here] = (act * up_pre).astype(bf16)
        ggp[:, here] = (grad_mid * up_pre * sig * (1.0 + gate_pre * (1.0 - sig))).astype(bf16)
        gup[:, here] = (grad_mid * act).astype(bf16)

    outs = []

    def weight_chunk(c):
        here = pl.ds(c, chunk)
        for i, (left, right) in enumerate(((ggp, x), (gup, x), (middle, rg))):
            turned = left[:, here].T
            for n in range(0, width, 512):
                there = pl.ds(n, 512)
                gw[i, here, there] = dot(turned, right[:, there], NN).astype(bf16)
            save = pltpu.make_async_copy(
                gw.at[i, here], gw_hbm.at[i, here], gw_sems.at[c // chunk * 3 + i]
            )
            save.start()
            outs.append(save)

    chunks = list(range(0, hidden, chunk))
    for c in chunks[:-1]:
        hidden_chunk(c)
    if receive is not None:
        for c in chunks[:-1]:
            weight_chunk(c)
        run(receive)
    hidden_chunk(chunks[-1])
    dots[...] = jnp.zeros_like(dots)

    for n in range(0, width, chunk):
        here = pl.ds(n, chunk)
        out = dot(middle[...], w[2, :, here], NN).astype(bf16).astype(f32)
        p[:, here] = (out * gate[:, 0:1]).astype(bf16)
        along = out * d[:, here].astype(f32)
        dots[...] += along[:, :128] + along[:, 128:]
        back = dot(ggp[...], w[0, :, here], NN) + dot(gup[...], w[1, :, here], NN)
        rb[:, here] = back.astype(bf16)

    expert = expert_ref[0]
    total = jnp.sum(dots[...], axis=1, keepdims=True)
    high = total.astype(bf16).astype(f32)
    lane = lax.broadcasted_iota(jnp.int32, (rows, 128), 1)
    tail = jnp.where(lane == expert, high, jnp.where(lane == expert + 64, total - high, 0.0))
    rb[:, pl.ds(width, 128)] = tail.astype(bf16)
    outs.append(pltpu.make_async_copy(rb, rb_hbm, out_sems.at[0]))
    outs.append(pltpu.make_async_copy(p, p_hbm, out_sems.at[1]))
    outs[-2].start()
    outs[-1].start()
    for c in chunks[-1:] if receive is not None else chunks:
        weight_chunk(c)
    for out in outs:
        out.wait()


def near_parts(number, gate_ref, up_ref, down_ref, left_gate, left_two, right_gate, right_two):
    shard = gate_ref.shape[1]
    own, left, right = pl.ds(0, shard), pl.ds(shard, shard), pl.ds(2 * shard, shard)
    return [
        (gate_ref.at[number], (0, own)), (up_ref.at[number], (1, own)),
        (down_ref.at[number], (2, own)), (left_gate, (0, left)),
        (left_two, (pl.ds(1, 2), left)), (right_gate, (0, right)), (right_two, (pl.ds(1, 2), right)),
    ]


def first_expert_kernel(expert_ref, x, d, gate, *refs):
    weights, low, high, rest = refs[:7], refs[7], refs[8], refs[9:]
    half = low.shape[1]
    parts = near_parts(0, *weights)
    for i, ref in enumerate((low, high)):
        parts.append((ref, (slice(None), pl.ds((6 + i) * half, half))))
    expert_steps(expert_ref, parts, None, x, d, gate, *rest)


def second_expert_kernel(expert_ref, x, d, gate, *refs):
    weights, rest = refs[:7], refs[7:]
    *rest, send_sems, recv_sems = rest
    w = rest[3]
    shard = weights[0].shape[1]
    half = shard // 2
    _, _, _, left_gate, left_two, right_gate, right_two = weights
    place = Place()

    def receive():
        greet([place.on_line(1), place.on_line(-1)])
        copies = []
        for i, (one, two, side) in enumerate(
            ((left_gate, left_two, 1), (right_gate, right_two, -1))
        ):
            cut = pl.ds(i * half, half)
            there = pl.ds((6 + i) * half, half)
            copies.append(
                remote(one.at[cut], w.at[0, there], send_sems.at[2 * i], recv_sems.at[2 * i],
                       place.on_line(side))
            )
            copies.append(
                remote(two.at[:, cut], w.at[pl.ds(1, 2), there], send_sems.at[2 * i + 1],
                       recv_sems.at[2 * i + 1], place.on_line(side))
            )
        for copy in copies:
            copy.start()
        yield
        for copy in copies:
            copy.wait()

    expert_steps(expert_ref, near_parts(1, *weights), receive(), x, d, gate, *rest)


def first_sums_steps(
    place, gw_hbm, sum_left, sum_right, come, mine, load_sems, send_sems, recv_sems, save_sems
):
    shard = gw_hbm.shape[1] // 4
    half = shard // 2
    sends = [
        remote(gw_hbm.at[:, pl.ds(3 * shard + i * half, half)], come.at[i], send_sems.at[i],
               recv_sems.at[i], place.on_line(side))
        for i, side in ((0, -1), (1, 1))
    ]
    loads = [
        pltpu.make_async_copy(gw_hbm.at[:, pl.ds(at, half)], mine.at[i], load_sems.at[i])
        for i, at in ((0, shard), (1, 2 * shard + half))
    ]
    for copy in sends + loads:
        copy.start()
    yield
    saves = []
    for i, target in ((0, sum_left), (1, sum_right)):
        loads[i].wait()
        sends[i].wait()

        @pl.loop(0, half, step=16)
        def _(row):
            for j in range(3):
                here = (i, j, pl.ds(row, 16))
                mine[here] = (mine[here].astype(F32) + come[here].astype(F32)).astype(BF16)

        saves.append(pltpu.make_async_copy(mine.at[i], target, save_sems.at[i]))
        saves[i].start()
    for save in saves:
        save.wait()


def first_sums_scratch(half, width):
    return [
        pltpu.VMEM((2, 3, half, width), BF16),
        pltpu.VMEM((2, 3, half, width), BF16),
        *dma_sems(2, 2, 2, 2),
    ]


def second_sends(place, gw_hbm, sum_left, sum_right, from_right, from_left, send_sems, recv_sems):
    shard = gw_hbm.shape[1] // 4
    half = shard // 2
    low, high = pl.ds(0, half), pl.ds(half, half)
    plan = [
        (gw_hbm.at[:, pl.ds(shard + half, half)], from_right.at[:, high], -1),
        (gw_hbm.at[:, pl.ds(2 * shard, half)], from_left.at[:, low], 1),
        (sum_left, from_right.at[:, low], -1),
        (sum_right, from_left.at[:, high], 1),
    ]
    return [
        remote(source, target, send_sems.at[i], recv_sems.at[i], place.on_line(side))
        for i, (source, target, side) in enumerate(plan)
    ]


def expert_layer(expert, weights, x, d, gate, collective_id=None):
    bf16 = jnp.bfloat16
    rows, width = x.shape
    hidden = 4 * weights[0].shape[1]
    second = collective_id is not None
    extra = dma_sems(4, 4) if second else []
    return pl.pallas_call(
        second_expert_kernel if second else first_expert_kernel,
        out_shape=(
            shape((rows, width)),
            shape((rows, width + 128)),
            shape((3, hidden, width)),
        ),
        in_specs=[SMEM] + [ANY] * (3 + len(weights)),
        out_specs=(ANY,) * 3,
        scratch_shapes=[
            pltpu.VMEM((3, hidden, width), bf16),
            pltpu.VMEM((rows, width), bf16),
            pltpu.VMEM((rows, width), bf16),
            pltpu.VMEM((rows, 128), jnp.float32),
            pltpu.VMEM((rows, width), bf16),
            pltpu.VMEM((rows, hidden), bf16),
            pltpu.VMEM((rows, hidden), bf16),
            pltpu.VMEM((rows, hidden), bf16),
            pltpu.VMEM((rows, width), bf16),
            pltpu.VMEM((rows, width + 128), bf16),
            pltpu.VMEM((rows, 128), jnp.float32),
            pltpu.VMEM((3, hidden, width), bf16),
            *dma_sems(12, 2, 9),
            *extra,
        ],
        compiler_params=pltpu.CompilerParams(
            vmem_limit_bytes=60 * 2**20, collective_id=collective_id, has_side_effects=second
        ),
        cost_estimate=pl.CostEstimate(
            flops=18 * rows * hidden * width,
            bytes_accessed=12 * hidden * width + 10 * rows * width,
            transcendentals=rows * hidden,
        ),
        name="second_expert" if second else "first_expert",
    )(expert, x, d, gate, *weights)


def rope_tables(length, head_size):
    position = jnp.arange(length, dtype=jnp.float32)[:, None]
    index_half = jnp.arange(head_size // 2, dtype=jnp.float32)[None, :]
    frequency = jnp.exp(index_half * (-2.0 / head_size) * jnp.log(ROPE_BASE))
    turned = position * frequency
    sine = jnp.sin(turned)
    return (
        jnp.concatenate([jnp.cos(turned)] * 2, axis=1),
        jnp.concatenate([-sine, sine], axis=1),
    )


def inverse_rms(values):
    return lax.rsqrt(jnp.mean(values * values, axis=-1, keepdims=True) + EPSILON)


def norm_back(values, scales, gain, grads):
    weighted = grads * gain
    return scales * weighted - values * scales * scales * scales * jnp.mean(
        weighted * values, axis=-1, keepdims=True
    )


def attend(seq, w_query, w_key, w_value, q_gain, k_gain, cosine, sine,
           query_rot, key_rot, values, query_unit, key_unit, stats, context):
    length = seq.shape[0]
    head = cosine.shape[1]
    heads = w_query.shape[1] // head
    scale = head ** (-0.5)
    cos, sin = cosine[...], sine[...]
    lane = lax.broadcasted_iota(jnp.int32, (length, head), 1)
    kept = jnp.zeros((length, head), F32)

    def unit_and_rot(raw, gain):
        scales = inverse_rms(raw)
        unit = raw * scales
        normed = unit * gain
        rot = normed * cos + pltpu.roll(normed, head // 2, 1) * sin
        return scales, unit, rot.astype(BF16)

    raw = dot(seq[...], w_key[...], NN)
    scales, unit, rot = unit_and_rot(raw, k_gain[...])
    key_unit[...] = unit
    key_rot[...] = rot
    kept = jnp.where(lane == 8, scales, kept)
    values[...] = dot(seq[...], w_value[...], NN).astype(BF16)
    half = length // 2
    for pair in range(0, heads, 2):
        raws = dot(seq[...], w_query[:, pl.ds(pair * head, 2 * head)], NN)
        for h in (pair, pair + 1):
            here = pl.ds(h * head, head)
            raw = raws[:, (h - pair) * head : (h - pair + 1) * head]
            scales, unit, rot = unit_and_rot(raw, q_gain[...])
            query_unit[:, here] = unit
            query_rot[:, here] = rot
            kept = jnp.where(lane == h, scales, kept)
            logs = []
            for part in range(2):
                until = (part + 1) * half
                scores = dot(rot[part * half : until], key_rot[:until], NT) * scale
                row = lax.broadcasted_iota(jnp.int32, scores.shape, 0) + part * half
                column = lax.broadcasted_iota(jnp.int32, scores.shape, 1)
                scores = jnp.where(row >= column, scores, MASK_VALUE)
                peak = jnp.max(scores, axis=1, keepdims=True)
                raised = jnp.exp(scores - peak)
                total = jnp.sum(raised, axis=1, keepdims=True)
                probs = (raised * (1.0 / total)).astype(BF16)
                mixed = dot(probs, values[:until], NN)
                context[pl.ds(part * half, half), here] = mixed.astype(BF16)
                logs.append(peak + jnp.log(total))
            kept = jnp.where(lane == 16 + h, jnp.concatenate(logs, axis=0), kept)
        yield
    stats[...] = kept


def attend_back(grad_rows, seq, w_query, w_key, w_value, w_out, q_gain, k_gain, cosine, sine,
                query_rot, key_rot, values, query_unit, key_unit, stats,
                grad_context, grad_qkv, gains):
    length = seq.shape[0]
    head = cosine.shape[1]
    heads = query_rot.shape[1] // head
    scale = head ** (-0.5)
    cos, sin = cosine[...], sine[...]
    half = length // 2

    def rotate_back(grads):
        return grads * cos - pltpu.roll(grads, head // 2, 1) * sin

    def unit_back(scales, unit, gain, grads):
        z = grads * gain
        return scales * (z - unit * jnp.mean(z * unit, axis=1, keepdims=True))

    for n in range(0, heads * head, 256):
        here = pl.ds(n, 256)
        grad_context[:, here] = dot(grad_rows[...], w_out[here], NT).astype(BF16)
    yield
    key_grads = [jnp.zeros((half, head), F32)] * 2
    value_grads = [jnp.zeros((half, head), F32)] * 2
    q_gain_grad = jnp.zeros((1, head), F32)
    for h in range(heads):
        here = pl.ds(h * head, head)
        query_grads = []
        for part in range(2):
            until = (part + 1) * half
            rows = pl.ds(part * half, half)
            rot = query_rot[rows, here]
            scores = dot(rot, key_rot[:until], NT) * scale
            row = lax.broadcasted_iota(jnp.int32, scores.shape, 0) + part * half
            column = lax.broadcasted_iota(jnp.int32, scores.shape, 1)
            scores = jnp.where(row >= column, scores, MASK_VALUE)
            probs = jnp.exp(scores - stats[rows, 16 + h : 17 + h])
            from_context = grad_context[rows, here]
            grad_probs = dot(from_context, values[:until], NT)
            low = probs.astype(BF16)
            value_part = dot(low, from_context, TN)
            mean = jnp.sum(grad_probs * probs, axis=1, keepdims=True)
            grad_scores = (probs * (grad_probs - mean)).astype(BF16)
            query_grads.append(dot(grad_scores, key_rot[:until], NN) * scale)
            key_part = dot(grad_scores, rot, TN) * scale
            for other in range(part + 1):
                cut = slice(other * half, (other + 1) * half)
                value_grads[other] = value_grads[other] + value_part[cut]
                key_grads[other] = key_grads[other] + key_part[cut]
        grads = rotate_back(jnp.concatenate(query_grads, axis=0))
        unit = query_unit[:, here]
        q_gain_grad = q_gain_grad + jnp.sum(grads * unit, axis=0, keepdims=True)
        grad_qkv[:, here] = unit_back(stats[:, h : h + 1], unit, q_gain[...], grads).astype(BF16)
        yield
    grads = rotate_back(jnp.concatenate(key_grads, axis=0))
    unit = key_unit[...]
    gains[0:1, :] = q_gain_grad
    gains[1:2, :] = jnp.sum(grads * unit, axis=0, keepdims=True)
    grad_qkv[:, pl.ds(heads * head, head)] = unit_back(
        stats[:, 8:9], unit, k_gain[...], grads
    ).astype(BF16)
    grad_qkv[:, pl.ds((heads + 1) * head, head)] = jnp.concatenate(value_grads, axis=0).astype(BF16)
    yield


def forward_kernel(
    inputs_ref, attn_gain_ref, q_gain_ref, k_gain_ref, cos_ref, sin_ref, mlp_gain_ref, router_ref,
    picks_ref, w_query_ref, w_key_ref, w_value_ref, w_out_ref, gate_w_ref, dout_ref,
    mixed_ref, hidden_ref, state_ref, left_gate_ref, right_gate_ref, dout_all_ref, seq_ref,
    query_rot_ref, key_rot_ref, values_ref, query_unit_ref, key_unit_ref, stats_ref, context_ref,
    seq, w_query, w_key, w_value, w_out, partial, query_rot, key_rot, values, query_unit, key_unit,
    stats, context, load_sems, save_sems, gather_send, gather_recv, gate_send, gate_recv, dout_sem,
    *scratch,
):
    place = Place()
    count, width = inputs_ref.shape
    experts = picks_ref.shape[1]
    loads = [
        pltpu.make_async_copy(source, target, load_sems.at[i])
        for i, (source, target) in enumerate(
            (
                (w_key_ref, w_key), (w_value_ref, w_value),
                (w_query_ref, w_query), (w_out_ref, w_out),
            )
        )
    ]
    for load in loads:
        load.start()
    float_in = inputs_ref[...].astype(F32)
    first_scale = inverse_rms(float_in)
    own = pl.ds(place.x * count, count)
    seq[own] = (float_in * first_scale * attn_gain_ref[...]).astype(BF16)
    greet(plane_neighbours(place) + [place.on_line(1), place.on_line(-1)])
    scratch, dout_sems = scratch[:4], scratch[4:]
    keep = pltpu.make_async_copy(dout_ref, dout_all_ref.at[place.block()], dout_sem.at[0])
    douts = plane_gather_steps(place, dout_ref, lambda at: dout_all_ref.at[at], dout_sems)

    def gather_until(last):
        for stage in douts:
            if stage == last:
                break

    line = line_gather_steps(place, seq, count, (gather_send, gather_recv))
    next(line)
    keep.start()
    for _ in range(9):
        next(douts)
    run(line)
    gates_sent = [
        remote(gate_w_ref.at[0], target, gate_send.at[i], gate_recv.at[i], place.on_line(side))
        for i, (target, side) in enumerate(((left_gate_ref, 1), (right_gate_ref, -1)))
    ]
    for copy in gates_sent:
        copy.start()
    for load in loads:
        load.wait()
    heads_done = attend(
        seq, w_query, w_key, w_value, q_gain_ref, k_gain_ref, cos_ref, sin_ref,
        query_rot, key_rot, values, query_unit, key_unit, stats, context,
    )
    next(heads_done)
    next(heads_done)
    gather_until(101)
    run(heads_done)
    for n in range(0, width, 512):
        here = pl.ds(n, 512)
        partial[:, here] = dot(context[...], w_out[:, here], NN).astype(BF16)
    steps = line_scatter_steps(place, partial, count, scratch)
    next(steps)
    gather_until(102)
    saves = [
        pltpu.make_async_copy(source, target, save_sems.at[i])
        for i, (source, target) in enumerate(
            (
                (seq, seq_ref), (query_rot, query_rot_ref), (key_rot, key_rot_ref),
                (values, values_ref), (query_unit, query_unit_ref), (key_unit, key_unit_ref),
                (stats, stats_ref), (context, context_ref),
            )
        )
    ]
    for save in saves:
        save.start()
    next(steps)
    run(douts)
    run(steps)
    in_b = scratch[1]
    attended = partial[own].astype(F32) + in_b[0].astype(F32) + in_b[1].astype(F32)
    hidden = float_in + attended
    hidden_ref[...] = hidden
    second_scale = inverse_rms(hidden)
    mixed = (hidden * second_scale * mlp_gain_ref[...]).astype(BF16)
    mixed_ref[:, :width] = mixed
    logits = dot(mixed, router_ref[...], NT)
    raised = jnp.exp(logits - jnp.max(logits, axis=1, keepdims=True))
    probs = raised / jnp.sum(raised, axis=1, keepdims=True)
    picked = picks_ref[...] * probs
    picked_total = jnp.sum(picked, axis=1, keepdims=True)
    gates = picked / picked_total
    high = gates.astype(BF16)
    low = (gates - high.astype(F32)).astype(BF16)
    mixed_ref[:, width:] = jnp.concatenate([high, low], axis=1)
    state_ref[:, : 2 * experts] = jnp.concatenate([probs, gates], axis=1)
    lane = lax.broadcasted_iota(jnp.int32, (count, 2 * experts), 1)
    extra = jnp.where(lane == 0, picked_total, jnp.where(lane == 1, second_scale, first_scale))
    state_ref[:, 2 * experts :] = extra
    for copy in saves + gates_sent + [keep]:
        copy.wait()


def forward(inputs, attn_gain, q_gain, k_gain, cosine, sine, mlp_gain, router_t, picks,
            w_query, w_key, w_value, w_out, gate_w, dout, collective_id):
    count, width = inputs.shape
    head = cosine.shape[1]
    length = 4 * count
    wide = w_query.shape[1]
    saved = [
        ((length, width), BF16), ((length, wide), BF16), ((length, head), BF16),
        ((length, head), BF16), ((length, wide), F32), ((length, head), F32),
        ((length, head), F32), ((length, wide), BF16),
    ]
    kept = [pltpu.VMEM(dims, dtype) for dims, dtype in saved]
    return pl.pallas_call(
        forward_kernel,
        out_shape=(
            shape((count, width + 128)),
            shape((count, width), F32),
            shape((count, 256), F32),
            *[shape(gate_w.shape[1:])] * 2,
            shape((32, *dout.shape)),
            *[shape(dims, dtype) for dims, dtype in saved],
        ),
        in_specs=[VMEM] * 9 + [ANY] * 6,
        out_specs=(VMEM, VMEM, VMEM, *[ANY] * 11),
        scratch_shapes=[
            kept[0],
            *[pltpu.VMEM(w.shape, BF16) for w in (w_query, w_key, w_value, w_out)],
            pltpu.VMEM((length, width), BF16),
            *kept[1:],
            *dma_sems(4, 8, 4, 4, 2, 2, 1),
            *line_scatter_scratch(count, width),
            *gather_sems(),
        ],
        compiler_params=pltpu.CompilerParams(
            collective_id=collective_id, has_side_effects=True, vmem_limit_bytes=60 * 2**20
        ),
        cost_estimate=pl.CostEstimate(flops=7 * 10**10, bytes_accessed=10**8, transcendentals=0),
        name="forward",
    )(inputs, attn_gain, q_gain, k_gain, cosine, sine, mlp_gain, router_t, picks,
      w_query, w_key, w_value, w_out, gate_w, dout)


LATE_EVERY = 12


def exchange_steps(buffer, inbox, peers, sems):
    send_sems, recv_sems, base = sems
    copies = [
        remote(buffer, inbox.at[base + i], send_sems.at[base + i], recv_sems.at[base + i], device)
        for i, device in enumerate(peers)
    ]
    for copy in copies:
        copy.start()
    yield
    for copy in copies:
        copy.wait()


def backward_kernel(
    grad_att_ref, inputs_ref, attn_gain_ref, q_gain_ref, k_gain_ref, cos_ref, sin_ref, state_ref,
    grad_hidden_ref, router_grad_ref, mlp_grad_ref,
    gw_b_ref, seq_ref, w_query_ref, w_key_ref, w_value_ref, w_out_ref,
    query_rot_ref, key_rot_ref, values_ref, query_unit_ref, key_unit_ref, stats_ref, context_ref,
    grad_inputs_ref, router_out_ref, gains_out_ref, all_w_ref, right_b_ref, left_b_ref,
    sum_left_ref, sum_right_ref,
    grad_rows, seq, w_query, w_key, w_value, w_out,
    query_rot, key_rot, values, query_unit, key_unit, stats, context,
    grad_context, grad_qkv, summed, out_w, qkv_w, gains,
    small, small_in, small_out, late, late_in, both_sum, load_sems, line_send, line_recv, small_send,
    small_recv, second_send, second_recv, *scratch,
):
    place = Place()
    count, width = inputs_ref.shape
    experts = router_grad_ref.shape[0]
    head = cos_ref.shape[1]
    pairs = (
        (context_ref, context), (w_out_ref, w_out), (query_rot_ref, query_rot),
        (key_rot_ref, key_rot), (values_ref, values), (stats_ref, stats),
        (query_unit_ref, query_unit), (key_unit_ref, key_unit), (w_query_ref, w_query),
        (w_key_ref, w_key), (w_value_ref, w_value), (seq_ref, seq),
    )
    loads = [
        pltpu.make_async_copy(source, target, load_sems.at[i])
        for i, (source, target) in enumerate(pairs)
    ]
    for load in loads:
        load.start()
    own = pl.ds(place.x * count, count)
    grad_rows[own] = grad_att_ref[...]
    far = {
        "x": [place.on_line(step) for step in (1, -1, 2)],
        "z": [place.device("z", step) for step in (1, -1, 2)],
        "y": [place.device("y", step) for step in (1, -1, 2)],
        "core": [place.device(other=1)],
    }
    greet([device for axis in ("x", "z", "y", "core") for device in far[axis]])
    line = line_gather_steps(place, grad_rows, count, (line_send, line_recv))
    next(line)

    part = small.shape[1]
    small[...] = jnp.zeros_like(small)
    for i in range(4):
        used = min(part, experts + 1 - i * part)
        from_router = min(used, experts - i * part)
        if from_router > 0:
            small[i, :from_router] = router_grad_ref[i * part : i * part + from_router]
    at_gain = experts // part
    small[at_gain, experts - at_gain * part : experts - at_gain * part + 1] = mlp_grad_ref[...]

    def small_total():
        def send(step, number):
            return remote(
                small.at[(place.x + step) % 4], small_in.at[number], small_send.at[number],
                small_recv.at[number], place.on_line(step),
            )

        copies = [send(step, i) for i, step in enumerate((1, -1, 2))]
        for copy in copies:
            copy.start()
        yield
        for copy in copies:
            copy.wait()
        mine = small.at[place.x]
        mine[...] = mine[...] + small_in[0] + small_in[1] + small_in[2]
        base = 3
        for axis in ("z", "y", "core"):
            peers = far[axis]
            yield from exchange_steps(mine, small_in, peers, (small_send, small_recv, base))
            total = mine[...]
            for i in range(len(peers)):
                total = total + small_in[base + i]
            mine[...] = total
            base += len(peers)
        done = small_out.at[place.x]
        done[...] = mine[...]
        copies = [
            remote(done, done, small_send.at[base + i], small_recv.at[base + i], device)
            for i, device in enumerate(far["x"])
        ]
        for copy in copies:
            copy.start()
        yield
        for i, step in enumerate((-1, 1, 2)):
            copies[i].wait_send()
            there = small_out.at[(place.x + step) % 4]
            remote(
                there, there, small_send.at[base + i], small_recv.at[base + i], far["x"][0]
            ).wait_recv()

    smalls = small_total()
    next(smalls)
    run(line)

    half = width // 2
    for load in loads[:2]:
        load.wait()
    for n in range(0, width, 512):
        where = (pl.ds((n // half) * context.shape[1], context.shape[1]), pl.ds(n % half, 512))
        out_w[where] = dot(context[...], grad_rows[:, pl.ds(n, 512)], TN).astype(BF16)

    def scattered(weights, columns, scratch):
        rows = weights.shape[0] // 32

        def block(dz, dy, other):
            return weights.at[pl.ds(place.block("z", dz, dy, other) * rows, rows)]

        def finish(row, value):
            both_sum[pl.ds(row, 16), columns] = value.astype(BF16)

        return plane_scatter_steps(place, rows, lambda dz, dy: None, block, scratch, finish)

    out_width = out_w.shape[1]
    scatter_out, scratch = scratch[:9], scratch[9:]
    scatter_qkv, scratch = scratch[:9], scratch[9:]
    gather_both, scratch = scratch[:4], scratch[4:]
    late_send, late_recv, keep_sem, *scratch = scratch
    sums_scratch, scratch = scratch[:6], scratch[6:]

    def out_total():
        return scattered(out_w, pl.ds(0, out_width), scatter_out)

    outs = out_total()
    next(outs)
    sums = first_sums_steps(place, gw_b_ref, sum_left_ref, sum_right_ref, *sums_scratch)
    next(sums)
    next(smalls)
    second = second_sends(
        place, gw_b_ref, sum_left_ref, sum_right_ref, right_b_ref, left_b_ref, second_send, second_recv
    )
    for load in loads[2:]:
        load.wait()
    back = attend_back(grad_rows, seq, w_query, w_key, w_value, w_out, q_gain_ref, k_gain_ref,
                       cos_ref, sin_ref, query_rot, key_rot, values, query_unit, key_unit, stats,
                       grad_context, grad_qkv, gains)
    gains[...] = jnp.zeros_like(gains)
    for at, _ in enumerate(back):
        next(outs, None)
        if at in (4, 9):
            next(smalls)
    heads = query_rot.shape[1]
    for n in range(0, width, 512):
        here = pl.ds(n, 512)
        value = dot(grad_qkv[:, :heads], w_query[here], NT)
        value = value + dot(grad_qkv[:, heads : heads + head], w_key[here], NT)
        value = value + dot(grad_qkv[:, heads + head :], w_value[here], NT)
        summed[:, here] = value.astype(BF16)
    line_scatter = scratch
    line = line_scatter_steps(place, summed, count, line_scatter)
    next(line)
    for n in range(0, grad_qkv.shape[1], 256):
        here = pl.ds(n, 256)
        qkv_w[:, here] = dot(seq[...], grad_qkv[:, here], TN).astype(BF16)

    rows = both_sum.shape[0]

    def qkv_total():
        yield from scattered(qkv_w, pl.ds(out_width, qkv_w.shape[1]), scatter_qkv)
        for _ in outs:
            pass
        keep = pltpu.make_async_copy(
            both_sum, all_w_ref.at[pl.ds(place.block() * rows, rows)], keep_sem.at[0]
        )
        keep.start()
        yield from plane_gather_steps(
            place, both_sum, lambda at: all_w_ref.at[pl.ds(at * rows, rows)], gather_both
        )
        keep.wait()

    qkvs = qkv_total()
    for step in range(15):
        next(qkvs)
        if step == 2:
            next(line)
        if step == 6:
            run(sums)
        if step == 10:
            next(smalls)
    run(line)
    in_b = line_scatter[1]
    grad_normed = summed[own].astype(F32) + in_b[0].astype(F32) + in_b[1].astype(F32)
    float_in = inputs_ref[...].astype(F32)
    first_scale = state_ref[:, 2 * experts + 2 : 2 * experts + 3]
    grad_inputs_ref[...] = (
        grad_hidden_ref[...] + norm_back(float_in, first_scale, attn_gain_ref[...], grad_normed)
    ).astype(BF16)
    late[...] = jnp.zeros_like(late)
    late[0:1, :] = jnp.sum(grad_normed * float_in * first_scale, axis=0, keepdims=True)
    late[1:2, :head] = gains[0:1, :]
    late[1:2, head : 2 * head] = gains[1:2, :]

    def late_total():
        base = 0
        for axis in ("x", "z", "y", "core"):
            peers = far[axis]
            yield from exchange_steps(late, late_in, peers, (late_send, late_recv, base))
            total = late[...]
            for i in range(len(peers)):
                total = total + late_in[base + i]
            late[...] = total
            base += len(peers)

    lates = late_total()
    next(lates)
    for _ in range(4):
        next(qkvs)
    next(lates)
    for copy in second:
        copy.start()
    steps_done = 0
    for _ in qkvs:
        steps_done += 1
        if steps_done % LATE_EVERY == 0:
            next(lates, None)
    run(lates)
    run(smalls)
    gains_out_ref[0:2] = late[0:2]
    at_row = experts - at_gain * part
    gains_out_ref[2:3] = small_out[at_gain, at_row : at_row + 1]
    for i in range(4):
        from_router = min(part, experts - i * part)
        if from_router > 0:
            router_out_ref[i * part : i * part + from_router] = small_out[i, :from_router]
    for copy in second:
        copy.wait()


def backward(grad_att, inputs, attn_gain, q_gain, k_gain, cosine, sine, state, grad_hidden,
             router_grad, mlp_grad, gw_b, weights, saved, collective_id):
    count, width = inputs.shape
    length = 4 * count
    head = cosine.shape[1]
    seq, query_rot, key_rot, values, query_unit, key_unit, stats, context = saved
    w_query, w_key, w_value, w_out = weights
    wide = w_query.shape[1]
    total = wide + 2 * head
    experts = router_grad.shape[0]
    part = -(-(experts + 1) // 32) * 8
    rows = width // 32
    shard = gw_b.shape[1] // 4
    like = lambda array: pltpu.VMEM(array.shape, array.dtype)
    return pl.pallas_call(
        backward_kernel,
        out_shape=(
            shape((count, width)),
            shape((experts, width), F32),
            shape((8, width), F32),
            shape((width, width // 2 + total)),
            *[shape((3, shard, width))] * 2,
            *[shape((3, shard // 2, width))] * 2,
        ),
        in_specs=[VMEM] * 11 + [ANY] * 13,
        out_specs=(VMEM, VMEM, VMEM) + (ANY,) * 5,
        scratch_shapes=[
            pltpu.VMEM((length, width), BF16),
            *[like(a) for a in (seq, w_query, w_key, w_value, w_out)],
            *[like(a) for a in saved[1:]],
            pltpu.VMEM((length, wide), BF16),
            pltpu.VMEM((length, total), BF16),
            pltpu.VMEM((length, width), BF16),
            pltpu.VMEM((2 * wide, width // 2), BF16),
            pltpu.VMEM((width, total), BF16),
            pltpu.VMEM((8, head), F32),
            pltpu.VMEM((4, part, width), F32),
            pltpu.VMEM((10, part, width), F32),
            pltpu.VMEM((4, part, width), F32),
            pltpu.VMEM((8, width), F32),
            pltpu.VMEM((10, 8, width), F32),
            pltpu.VMEM((rows, width // 2 + total), BF16),
            *dma_sems(12, 4, 4, 13, 13, 4, 4),
            *scatter_scratch(2 * wide // 32, width // 2),
            *scatter_scratch(rows, total),
            *gather_sems(),
            *dma_sems(10, 10, 1),
            *first_sums_scratch(shard // 2, width),
            *line_scatter_scratch(count, width),
        ],
        compiler_params=pltpu.CompilerParams(
            collective_id=collective_id, has_side_effects=True, vmem_limit_bytes=62 * 2**20
        ),
        cost_estimate=pl.CostEstimate(flops=10**11, bytes_accessed=10**8, transcendentals=0),
        name="backward",
    )(grad_att, inputs, attn_gain, q_gain, k_gain, cosine, sine, state, grad_hidden, router_grad,
      mlp_grad, gw_b, seq, w_query, w_key, w_value, w_out, *saved[1:])


def attention_grads_kernel(all_ref, out_ref, query_ref, key_ref, value_ref):
    value = all_ref[...].astype(F32)
    at = 0
    for ref in (out_ref, query_ref, key_ref, value_ref):
        ref[...] = value[:, at : at + ref.shape[1]]
        at += ref.shape[1]


def attention_grads(total, wide, narrow):
    rows, full = total.shape
    half = full - wide - 2 * narrow
    step = 128
    steps = rows // step
    cut = wide // step
    return pl.pallas_call(
        attention_grads_kernel,
        grid=(steps,),
        out_shape=(
            shape((wide, half * steps // cut), F32), shape((rows, wide), F32),
            shape((rows, narrow), F32), shape((rows, narrow), F32),
        ),
        in_specs=[pl.BlockSpec((step, full), lambda i: (i, 0))],
        out_specs=(
            pl.BlockSpec((step, half), lambda i: (i % cut, i // cut)),
            pl.BlockSpec((step, wide), lambda i: (i, 0)),
            pl.BlockSpec((step, narrow), lambda i: (i, 0)),
            pl.BlockSpec((step, narrow), lambda i: (i, 0)),
        ),
        compiler_params=pltpu.CompilerParams(vmem_limit_bytes=32 * 2**20),
        name="attention_grads",
    )(total)


def expert_grads_kernel(own_a, right_a, left_a, own_b, right_b, left_b, *outs):
    step = pl.program_id(0)

    def add(own, right, left):
        for i, out in enumerate(outs):
            value = own[i].astype(F32) + right[i].astype(F32)
            out[0] = value + left[i].astype(F32)

    @pl.when(step < 2)
    def _():
        add(own_a, right_a, left_a)

    @pl.when(step >= 2)
    def _():
        add(own_b, right_b, left_b)


def expert_grads(first, second):
    _, shard, width = first[1].shape
    half = shard // 2
    early = pl.BlockSpec((3, half, width), lambda i: (0, jnp.minimum(i, 1), 0))
    late = pl.BlockSpec((3, half, width), lambda i: (0, jnp.maximum(i - 2, 0), 0))
    return pl.pallas_call(
        expert_grads_kernel,
        grid=(4,),
        out_shape=(shape((2, shard, width), F32),) * 3,
        in_specs=[early] * 3 + [late] * 3,
        out_specs=(pl.BlockSpec((1, half, width), lambda i: (i // 2, i % 2, 0)),) * 3,
        compiler_params=pltpu.CompilerParams(vmem_limit_bytes=48 * 2**20),
        name="expert_grads",
    )(*first, *second)


def along_line(value, step):
    return lax.ppermute(value, "tensor", [(i, (i + step) % 4) for i in range(4)])


def per_device(
    inputs,
    attn_gain,
    w_query,
    w_key,
    w_value,
    q_gain,
    k_gain,
    w_out,
    mlp_gain,
    w_router,
    w_gate,
    w_up,
    w_down,
    routes,
    grad_out,
):
    row_count, model_width = inputs.shape
    head_size = q_gain.shape[0]
    expert_count = w_router.shape[1]
    place = lax.axis_index("expert")
    first = (2 * place).astype(jnp.int32).reshape(1)

    chosen = routes[:, :, None] == jnp.arange(expert_count, dtype=jnp.int32)[None, None, :]
    picks = jnp.sum(chosen.astype(F32), axis=1)
    before = (jnp.arange(row_count)[:, None] > jnp.arange(row_count)[None, :]).astype(BF16)
    rank = jnp.dot(before, picks.astype(BF16), preferred_element_type=F32)
    base = 20 * ((place // 4) % 2 * 2 + place % 2)
    slots = jnp.where(picks > 0.0, rank + base.astype(F32), -1.0)
    slots = jnp.concatenate([slots, jnp.full_like(slots, -1.0)], axis=1).astype(BF16)
    dout = jnp.concatenate([grad_out, slots], axis=1)

    gate_t = jnp.swapaxes(w_gate, 1, 2)
    up_t = jnp.swapaxes(w_up, 1, 2)
    cosine, sine = rope_tables(4 * row_count, head_size)
    router_t = w_router.T
    q_gain, k_gain = q_gain[None], k_gain[None]
    attn_gain, mlp_gain = attn_gain[None], mlp_gain[None]
    mixed, hidden, state, left_a, right_a, dout_all, *saved = forward(
        inputs, attn_gain, q_gain, k_gain, cosine, sine, mlp_gain, router_t, picks,
        w_query, w_key, w_value, w_out, gate_t, dout, 0,
    )

    left_two_a, right_two_a, low_a, high_a, left_b, right_b, _, *rows = gather_select(
        mixed, dout_all, gate_t, up_t, w_down, left_a, right_a, 1
    )
    grad_a, grad_b, rows_a, rows_b, gate_a, gate_b = rows
    own_two, rows_a = lax.optimization_barrier((jnp.stack([up_t[1], w_down[1]]), rows_a))
    left_two_b, right_two_b = along_line(own_two, 1), along_line(own_two, -1)
    shards = (gate_t, up_t, w_down)
    out_a, back_a, gw_a = expert_layer(
        first, (*shards, left_a, left_two_a, right_a, right_two_a, low_a, high_a),
        rows_a, grad_a, gate_a,
    )
    rows_b, back_a, left_two_b, right_two_b = lax.optimization_barrier(
        (rows_b, back_a, left_two_b, right_two_b)
    )
    out_b, back_b, gw_b = expert_layer(
        first + 1, (*shards, left_b, left_two_b, right_b, right_two_b), rows_b, grad_b, gate_b, 4
    )
    shares, right_a, left_a, _, _, grad_hidden, grad_att, router_grad, mlp_grad = combine_scatter(
        (back_a, back_b), (out_a, out_b), dout_all, gw_a, grad_out, hidden, mixed, state, picks,
        mlp_gain, router_t, 2,
    )
    expert_mix = lax.psum_scatter(
        shares.reshape(-1, model_width), "expert", scatter_dimension=0, tiled=True
    )
    output = (hidden + expert_mix.astype(F32)).astype(BF16)

    results = backward(
        grad_att, inputs, attn_gain, q_gain, k_gain, cosine, sine, state, grad_hidden,
        router_grad, mlp_grad, gw_b, (w_query, w_key, w_value, w_out), saved, 3,
    )
    grad_inputs, router_grad, gains, all_w, right_b, left_b, _, _ = results
    out_w, query_w, key_w, value_w = attention_grads(all_w, w_query.shape[1], w_key.shape[1])
    gate_w, up_w, down_w = expert_grads((gw_a, right_a, left_a), (gw_b, right_b, left_b))
    return (
        output,
        grad_inputs,
        gains[0],
        query_w,
        key_w,
        value_w,
        gains[1, :head_size],
        gains[1, head_size : 2 * head_size],
        out_w,
        gains[2],
        router_grad.T,
        jnp.swapaxes(gate_w, 1, 2),
        jnp.swapaxes(up_w, 1, 2),
        down_w,
    )


def solution(mesh):
    placed = (
        P(("expert", "tensor"), None),
        P(),
        P(None, "tensor"),
        P(None, "tensor"),
        P(None, "tensor"),
        P(),
        P(),
        P("tensor", None),
        P(),
        P(),
        P("expert", None, "tensor"),
        P("expert", None, "tensor"),
        P("expert", "tensor", None),
        P(("expert", "tensor"), None),
        P(("expert", "tensor"), None),
    )
    return jax.shard_map(
        per_device,
        mesh=mesh,
        in_specs=placed,
        out_specs=(
            P(("expert", "tensor"), None),
            P(("expert", "tensor"), None),
            P(),
            P(None, "tensor"),
            P(None, "tensor"),
            P(None, "tensor"),
            P(),
            P(),
            P("tensor", None),
            P(),
            P(),
            P("expert", None, "tensor"),
            P("expert", None, "tensor"),
            P("expert", "tensor", None),
        ),
        check_vma=False,
    )
```

```python
import functools

import jax
import jax.numpy as jnp
from jax import lax
from jax.experimental import pallas as pl
from jax.experimental.pallas import tpu as pltpu
from jax.sharding import PartitionSpec as P

MESH = pl.DeviceIdType.MESH
F32 = jnp.float32
BF16 = jnp.bfloat16
EPSILON = 1e-06
ROPE_BASE = 1000000.0
MASK_VALUE = -1e30
NT = (((1,), (1,)), ((), ()))
TN = (((0,), (0,)), ((), ()))
NN = (((1,), (0,)), ((), ()))
OTHER = {"z": "y", "y": "z"}
ANY = pl.BlockSpec(memory_space=pl.ANY)
VMEM = pl.BlockSpec(memory_space=pltpu.VMEM)
SMEM = pl.BlockSpec(memory_space=pltpu.SMEM)


def dot(left, right, dims):
    return lax.dot_general(left, right, dims, preferred_element_type=F32)


def shape(dims, dtype=BF16):
    return jax.ShapeDtypeStruct(tuple(dims), dtype)


def dma_sems(*counts):
    return [pltpu.SemaphoreType.DMA((count,)) for count in counts]


class Place:
    def __init__(self):
        e = lax.axis_index("expert")
        self.x = lax.axis_index("tensor")
        self.z = e // 8
        self.y = (e // 2) % 4
        self.core = e % 2

    def block(self, axis="z", a=0, b=0, other=0):
        dz, dy = (a, b) if axis == "z" else (b, a)
        core = (self.core + other) % 2
        return ((self.z + dz) % 4) * 8 + ((self.y + dy) % 4) * 2 + core

    def device(self, axis="z", a=0, b=0, other=0):
        return (self.block(axis, a, b, other), self.x)

    def on_line(self, step):
        return (self.block(), (self.x + step) % 4)


def greet(devices):
    barrier = pltpu.get_barrier_semaphore()
    for device in devices:
        pl.semaphore_signal(barrier, inc=1, device_id=device, device_id_type=MESH)
    pl.semaphore_wait(barrier, len(devices))


def plane_neighbours(place):
    return [
        place.device("z", 1),
        place.device("z", -1),
        place.device("y", 1),
        place.device("y", -1),
        place.device(other=1),
    ]


def run(steps):
    for _ in steps:
        pass


def remote(source, target, send_sem, recv_sem, device):
    return pltpu.make_async_remote_copy(
        src_ref=source, dst_ref=target, send_sem=send_sem, recv_sem=recv_sem,
        device_id=device, device_id_type=MESH,
    )


def gather_plan():
    stages = [[], [], [], []]
    for half, first in ((0, "y"), (1, "z")):
        for side in (-1, 1):
            stages[0].append((first, half, side, 0, None, ("f", side)))
            stages[0].append((first, half, 0, side, None, ("s", side)))
    for half, first in ((0, "y"), (1, "z")):
        for quarter, side in ((0, -1), (1, 1)):
            stages[1].append((first, half, 2, 0, quarter, ("f", side)))
        for f in (-1, 1):
            for side in (-1, 1):
                stages[1].append((first, half, f, side, None, ("s", side)))
        for quarter, side in ((0, -1), (1, 1)):
            stages[1].append((first, half, 0, 2, quarter, ("s", side)))
    for half, first in ((0, "y"), (1, "z")):
        for quarter in (0, 1):
            for side in (-1, 1):
                stages[2].append((first, half, 2, side, quarter, ("s", side)))
        for f in (-1, 1):
            for quarter, side in ((0, -1), (1, 1)):
                stages[2].append((first, half, f, 2, quarter, ("s", side)))
    for half, first in ((0, "y"), (1, "z")):
        for quarter, side in ((0, -1), (1, 1)):
            stages[3].append((first, half, 2, 2, quarter, ("s", side)))
    return stages


STAGES = gather_plan()
PIECES = [piece for stage in STAGES for piece in stage]
PIECE_AT = {piece: at for at, piece in enumerate(PIECES)}


def onward(piece):
    first, half, f, s, quarter, (leg, side) = piece
    found = []
    for target in PIECES:
        _, t_half, t_f, t_s, t_quarter, (t_leg, t_side) = target
        if t_half != half or (quarter is not None and t_quarter != quarter):
            continue
        if t_leg == "f":
            take = t_f == 2 and leg == "f" and f == t_side and s == 0
        elif t_s == 2:
            take = leg == "s" and s == t_side and f == t_f
        else:
            take = leg == "f" and s == 0 and f == t_f
        if take:
            found.append(target)
    return found


def plane_gather_steps(place, x_ref, blocks, sems):
    send_sems, recv_sems, core_send, core_recv = sems
    rows = x_ref.shape[0]
    sibling = place.device(other=1)

    def span(half, quarter):
        if quarter is None:
            return pl.ds(half * (rows // 2), rows // 2)
        return pl.ds(half * (rows // 2) + quarter * (rows // 4), rows // 4)

    def send(target, source, f, s):
        first, half, _, _, quarter, (leg, side) = target
        at = PIECE_AT[target]
        copy = remote(
            source.at[span(half, quarter)],
            blocks(place.block(first, f, s)).at[span(half, quarter)],
            send_sems.at[at], recv_sems.at[at],
            place.device(first if leg == "f" else OTHER[first], -side),
        )
        copy.start()
        return copy

    started = [send(piece, x_ref, 0, 0) for piece in STAGES[0]]
    last = len(PIECES)
    core_copies = [
        remote(x_ref, blocks(place.block()), core_send.at[last], core_recv.at[last], sibling)
    ]
    core_copies[0].start()
    yield -1
    for number, stage in enumerate(STAGES):
        for piece in stage:
            first, half, f, s, quarter, _ = piece
            at = PIECE_AT[piece]
            block = blocks(place.block(first, f, s))
            view = block.at[span(half, quarter)]
            remote(view, view, send_sems.at[at], recv_sems.at[at], sibling).wait_recv()
            for target in onward(piece):
                started.append(send(target, block, f, s))
            copy = remote(view, view, core_send.at[at], core_recv.at[at], sibling)
            copy.start()
            core_copies.append(copy)
            yield number
        if number == 0:
            other = blocks(place.block(other=1))
            remote(other, other, core_send.at[last], core_recv.at[last], sibling).wait_recv()
        for piece in stage:
            first, half, f, s, quarter, _ = piece
            at = PIECE_AT[piece]
            view = blocks(place.block(first, f, s, 1)).at[span(half, quarter)]
            remote(view, view, core_send.at[at], core_recv.at[at], sibling).wait_recv()
        yield number + 100
    for copy in started + core_copies:
        copy.wait_send()


def gather_sems():
    count = len(PIECES)
    return dma_sems(count, count, count + 1, count + 1)


def scatter_scratch(rows, width):
    return [
        pltpu.VMEM((16, rows, width), BF16),
        pltpu.VMEM((2, 4, 2, rows // 4, width), BF16),
        pltpu.VMEM((2, 4, 2, rows // 2, width), BF16),
        pltpu.VMEM((2, 2, rows // 4, width), BF16),
        pltpu.VMEM((2, 2, rows // 2, width), BF16),
        *dma_sems(16, 16, 40, 40),
    ]


def plane_scatter_steps(place, rows, make, block, scratch, finish):
    other, in_a, in_b, in_c, in_d, core_send, core_recv, send_sems, recv_sems = scratch
    half_rows, quarter_rows = rows // 2, rows // 4
    exchanged, ready, sent = {}, set(), []

    def exchange(dz, dy):
        at = dz * 4 + dy
        if at in exchanged:
            return
        make(dz, dy)
        exchanged[at] = remote(
            block(dz, dy, 1), other.at[at], core_send.at[at], core_recv.at[at],
            place.device(other=1),
        )
        exchanged[at].start()

    def add_rows(into, start, count, source):
        @pl.loop(0, count, step=16)
        def _(row):
            here = pl.ds(start + row, 16)
            total = into[here].astype(F32) + source[pl.ds(row, 16)].astype(F32)
            into[here] = total.astype(BF16)

    def where(axis, a, b):
        dz, dy = (a, b) if axis == "z" else (b, a)
        return dz % 4, dy % 4

    def ready_block(axis, a, b):
        dz, dy = where(axis, a, b)
        at = dz * 4 + dy
        if at not in ready:
            ready.add(at)
            exchange(dz, dy)
            exchanged[at].wait_recv()
            add_rows(block(dz, dy, 0), 0, rows, other.at[at])
        return block(dz, dy, 0)

    def send(source, target, number, device):
        copy = remote(source, target, send_sems.at[number], recv_sems.at[number], device)
        copy.start()
        sent.append(copy)

    def arrive(target, number):
        remote(
            target, target, send_sems.at[number], recv_sems.at[number], place.device("z", 1)
        ).wait_recv()

    axes = (("z", "y"), ("y", "z"))
    sides = ((0, 1), (1, -1))
    lines = (2, 1, 3, 0)
    first_needs = []
    for line in lines:
        for first, _ in axes:
            if where(first, 2, line) not in first_needs:
                first_needs.append(where(first, 2, line))
    for dz, dy in first_needs[:4]:
        exchange(dz, dy)
    yield
    for line in lines:
        for half, (first, second) in enumerate(axes):
            for dz, dy in first_needs:
                if (dz, dy) not in [where(first, 2, line)] and dz * 4 + dy not in exchanged:
                    exchange(dz, dy)
                    break
            held = ready_block(first, 2, line)
            for quarter, side in sides:
                rows_here = pl.ds(half * half_rows + quarter * quarter_rows, quarter_rows)
                send(held.at[rows_here], in_a.at[half, line, quarter],
                     (half * 4 + line) * 2 + quarter, place.device(first, side))
        yield
    for dz in (1, 3, 0, 2):
        for dy in (1, 3, 0, 2):
            exchange(dz, dy)
    yield
    for line in lines:
        for half, (first, second) in enumerate(axes):
            for quarter, side in sides:
                held = ready_block(first, side, line)
                number = (half * 4 + line) * 2 + quarter
                arrive(in_a.at[half, line, quarter], number)
                add_rows(held, half * half_rows + quarter * quarter_rows, quarter_rows,
                         in_a.at[half, line, quarter])
                send(held.at[pl.ds(half * half_rows, half_rows)],
                     in_b.at[half, line, quarter], 16 + number, place.device(first, side))
        yield
    for line in lines:
        for half, (first, second) in enumerate(axes):
            held = ready_block(first, 0, line)
            for quarter in (0, 1):
                number = (half * 4 + line) * 2 + quarter
                arrive(in_b.at[half, line, quarter], 16 + number)
                add_rows(held, half * half_rows, half_rows, in_b.at[half, line, quarter])
            if line == 2:
                for quarter, side in sides:
                    rows_here = pl.ds(half * half_rows + quarter * quarter_rows, quarter_rows)
                    send(held.at[rows_here], in_c.at[half, quarter],
                         32 + half * 2 + quarter, place.device(second, side))
            if line in (1, 3):
                quarter, side = sides[0] if line == 1 else sides[1]
                number = 32 + half * 2 + quarter
                arrive(in_c.at[half, quarter], number)
                add_rows(held, half * half_rows + quarter * quarter_rows, quarter_rows,
                         in_c.at[half, quarter])
                send(held.at[pl.ds(half * half_rows, half_rows)], in_d.at[half, quarter],
                     36 + half * 2 + quarter, place.device(second, side))
        yield
    held = block(0, 0, 0)
    for half in (0, 1):
        for quarter in (0, 1):
            arrive(in_d.at[half, quarter], 36 + half * 2 + quarter)

        @pl.loop(0, half_rows, step=16)
        def _(row):
            here = pl.ds(half * half_rows + row, 16)
            total = held[here].astype(F32)
            for quarter in (0, 1):
                total = total + in_d[half, quarter, pl.ds(row, 16)].astype(F32)
            finish(half * half_rows + row, total)

    for copy in sent:
        copy.wait_send()
    for at in exchanged:
        exchanged[at].wait_send()


def line_gather_steps(place, out_ref, rows, sems):
    send_sems, recv_sems = sems
    half = rows // 2

    def part(step, start, count):
        return out_ref.at[pl.ds(((place.x + step) % 4) * rows + start, count)]

    def copy(view, number, side):
        return remote(view, view, send_sems.at[number], recv_sems.at[number], place.on_line(side))

    copies = [copy(part(0, 0, rows), 0, 1), copy(part(0, 0, rows), 1, -1)]
    for c in copies:
        c.start()
    yield
    copy(part(-1, 0, rows), 0, 1).wait_recv()
    copies.append(copy(part(-1, 0, half), 2, 1))
    copies[2].start()
    copy(part(1, 0, rows), 1, -1).wait_recv()
    copies.append(copy(part(1, half, half), 3, -1))
    copies[3].start()
    yield
    copy(part(2, 0, half), 2, 1).wait_recv()
    copy(part(2, half, half), 3, -1).wait_recv()
    for c in copies:
        c.wait_send()


def line_scatter_scratch(rows, width):
    return [
        pltpu.VMEM((2, rows // 2, width), BF16),
        pltpu.VMEM((2, rows, width), BF16),
        *dma_sems(4, 4),
    ]


def line_scatter_steps(place, c_ref, rows, scratch):
    in_a, in_b, send_sems, recv_sems = scratch
    half = rows // 2

    def part(step, start, count):
        return c_ref.at[pl.ds(((place.x + step) % 4) * rows + start, count)]

    def copy(source, target, number, side):
        return remote(
            source, target, send_sems.at[number], recv_sems.at[number], place.on_line(side)
        )

    copies = [
        copy(part(2, 0, half), in_a.at[0], 0, 1),
        copy(part(2, half, half), in_a.at[1], 1, -1),
    ]
    for c in copies:
        c.start()
    yield

    def add(view, source):
        @pl.loop(0, half, step=16)
        def _(row):
            here = pl.ds(row, 16)
            view[here] = (view[here].astype(F32) + source[here].astype(F32)).astype(BF16)

    copies[0].wait_recv()
    add(part(1, 0, half), in_a.at[0])
    copies.append(copy(part(1, 0, rows), in_b.at[0], 2, 1))
    copies[2].start()
    copies[1].wait_recv()
    add(part(-1, half, half), in_a.at[1])
    copies.append(copy(part(-1, 0, rows), in_b.at[1], 3, -1))
    copies[3].start()
    yield
    copies[2].wait_recv()
    copies[3].wait_recv()
    for c in copies:
        c.wait_send()


SLOTS = 80
GROUPS = [(dz, dy) for dz in (0, 1, 3, 2) for dy in (0, 1)]


def chosen_rows(slots, first):
    value = slots.astype(F32)
    lane = lax.broadcasted_iota(jnp.int32, value.shape, 1)
    slot = lax.broadcasted_iota(jnp.int32, (value.shape[0], 2 * SLOTS), 1).astype(F32)
    found = []
    for j in range(2):
        mine = jnp.sum(jnp.where(lane == first + j, value, 0.0), axis=1, keepdims=True)
        found.append(jnp.where(mine >= 0.0, mine + float(j * SLOTS), -1.0))
    return jnp.where((slot == found[0]) | (slot == found[1]), 1.0, 0.0).astype(BF16)


def group_blocks(place, dz, dy):
    z = (place.z + dz) % 4
    return [z * 8 + ((place.y + dy + two) % 4) * 2 for two in (0, 2)]


def gather_select_kernel(
    x_ref, grads_ref, gate_w_ref, up_w_ref, down_w_ref, left_gate_ref, right_gate_ref,
    left_two_ref, right_two_ref, low_ref, high_ref, left_next_ref, right_next_ref,
    all_ref, grad_a_ref, grad_b_ref, row_a_ref, row_b_ref, gate_a_ref, gate_b_ref,
    tokens, slots, rows_a, rows_b, grads_a, grads_b, gates_a, gates_b,
    own_sem, load_sems, save_sems, line_send, line_recv, *sems,
):
    place = Place()
    first = 2 * lax.axis_index("expert")
    width = rows_a.shape[1]
    greet(plane_neighbours(place) + [place.on_line(1), place.on_line(-1)])
    line = line_weights_steps(
        place, gate_w_ref, up_w_ref, down_w_ref, left_gate_ref, right_gate_ref, left_two_ref,
        right_two_ref, low_ref, high_ref, left_next_ref, right_next_ref, line_send, line_recv,
    )
    next(line)
    own = pltpu.make_async_copy(x_ref, all_ref.at[place.block()], own_sem.at[0])
    own.start()
    steps = plane_gather_steps(place, x_ref, lambda at: all_ref.at[at], sems)
    next(steps)

    def loads_of(source, number, slot):
        dz, dy = GROUPS[number]
        return [
            pltpu.make_async_copy(
                source.at[pl.ds(at, 2)], tokens.at[slot, pl.ds(2 * i, 2)], load_sems.at[2 * slot + i]
            )
            for i, at in enumerate(group_blocks(place, dz, dy))
        ]

    saves = []

    def save(value_ref, target, number, slot):
        here = pl.ds(number * SLOTS, SLOTS)
        copy = pltpu.make_async_copy(value_ref.at[here], target.at[here], save_sems.at[slot])
        copy.start()
        saves.append(copy)

    def select(number, slot, is_grad):
        for load in loads_of(grads_ref if is_grad else all_ref, number, slot):
            load.wait()
        here = pl.ds(number * SLOTS, SLOTS)
        block = tokens[slot].reshape(512, width + 128)
        if is_grad:
            slots[number] = block[:, width:]
        rows = dot(chosen_rows(slots[number], first), block, TN)
        a, b = (grads_a, grads_b) if is_grad else (rows_a, rows_b)
        a[here] = rows[:SLOTS, :width].astype(BF16)
        b[here] = rows[SLOTS:, :width].astype(BF16)
        base = number * 2 + (16 if is_grad else 0)
        save(a, grad_a_ref if is_grad else row_a_ref, number, base)
        save(b, grad_b_ref if is_grad else row_b_ref, number, base + 1)
        if not is_grad:
            lane = lax.broadcasted_iota(jnp.int32, (SLOTS, 128), 1) % 64
            for j, (gates, target) in enumerate(((gates_a, gate_a_ref), (gates_b, gate_b_ref))):
                part = rows[j * SLOTS : (j + 1) * SLOTS, width:]
                gate = jnp.sum(jnp.where(lane == first + j, part, 0.0), axis=1, keepdims=True)
                gates[here] = jnp.broadcast_to(gate, (SLOTS, 128))
                save(gates, target, number, 32 + number * 2 + j)

    def start(is_grad, number, slot):
        for load in loads_of(grads_ref if is_grad else all_ref, number, slot):
            load.start()

    start(True, 0, 0)
    grad_turn = 0
    pieces = 0
    for stage in steps:
        if stage < 100:
            pieces += 1
            if pieces % 2 == 0 and grad_turn < 8:
                if grad_turn + 1 < 8:
                    start(True, grad_turn + 1, (grad_turn + 1) % 2)
                select(grad_turn, grad_turn % 2, True)
                grad_turn += 1
        elif stage == 101:
            assert grad_turn == 8
            next(line)
            own.wait()
            start(False, 0, 0)
            start(False, 1, 1)
            select(0, 0, False)
            select(1, 1, False)
        elif stage == 102:
            start(False, 2, 0)
            next(line)
            for number in range(2, 6):
                if number + 1 < 6:
                    start(False, number + 1, (number + 1) % 2)
                select(number, number % 2, False)
        elif stage == 103:
            start(False, 6, 0)
            start(False, 7, 1)
            select(6, 0, False)
            select(7, 1, False)
    run(line)
    for copy in saves:
        copy.wait()


def line_weights_steps(
    place, gate_w, up_w, down_w, left_gate, right_gate, left_two, right_two, low, high,
    left_next, right_next, send_sems, recv_sems,
):
    half = gate_w.shape[1] // 2
    first, second = pl.ds(0, half), pl.ds(half, half)
    numbers = iter(range(12))
    started = []

    def send(source, target, side):
        number = next(numbers)
        copy = remote(
            source, target, send_sems.at[number], recv_sems.at[number], place.on_line(side)
        )
        copy.start()
        started.append(copy)
        return copy

    def onward(left, right, matrix):
        send(left.at[first], low.at[matrix], 1)
        send(right.at[second], high.at[matrix], -1)

    near = []
    for i, w in enumerate((up_w, down_w)):
        near.append((send(w.at[0], left_two.at[i], 1), send(w.at[0], right_two.at[i], -1)))
        if i == 0:
            onward(left_gate, right_gate, 0)
    send(gate_w.at[1], left_next, 1)
    send(gate_w.at[1], right_next, -1)
    yield
    for i in range(2):
        for copy in near[i]:
            copy.wait_recv()
        onward(left_two.at[i], right_two.at[i], i + 1)
        yield
    come = [id(copy) for pair in near for copy in pair]
    for copy in started:
        copy.wait_send()
        if id(copy) not in come:
            copy.wait_recv()


def gather_select(x, grads, gate_w, up_w, down_w, left_gate, right_gate, collective_id):
    count, full = x.shape
    width = full - 128
    total = len(GROUPS) * SLOTS
    rows = shape((total, width))
    gate = shape((total, 128), F32)
    shard = gate_w.shape[1]
    two = shape((2, shard, width))
    far = shape((3, shard // 2, width))
    one = shape((shard, width))
    return pl.pallas_call(
        gather_select_kernel,
        out_shape=(
            two, two, far, far, one, one, shape((32, count, full)), rows, rows, rows, rows, gate, gate
        ),
        in_specs=[ANY] * 7,
        out_specs=(ANY,) * 13,
        scratch_shapes=[
            pltpu.VMEM((2, 4, count, full), BF16),
            pltpu.VMEM((8, 512, 128), BF16),
            *[pltpu.VMEM((total, width), BF16)] * 4,
            *[pltpu.VMEM((total, 128), F32)] * 2,
            *dma_sems(1, 4, 48, 12, 12),
            *gather_sems(),
        ],
        compiler_params=pltpu.CompilerParams(
            collective_id=collective_id, has_side_effects=True, vmem_limit_bytes=60 * 2**20
        ),
        cost_estimate=pl.CostEstimate(flops=6 * 10**10, bytes_accessed=10**8, transcendentals=0),
        name="gather_select",
    )(x, grads, gate_w, up_w, down_w, left_gate, right_gate)


def combine_scatter_kernel(
    back_a_ref, back_b_ref, out_a_ref, out_b_ref, slots_ref, gw_ref,
    grad_out_ref, hidden_ref, mixed_ref, state_ref, picks_ref, mlp_gain_ref, router_ref,
    shares_ref, right_low_ref, left_high_ref, right_last_ref, left_last_ref, sum_left_ref,
    sum_right_ref,
    grad_hidden_ref, grad_att_ref, grad_router_ref, gain_ref,
    rows, slots, blocks, out_rows, share, total, load_sems, row_sems, share_sems,
    line_send, line_recv, *scratch,
):
    place = Place()
    first = 2 * lax.axis_index("expert")
    count = hidden_ref.shape[0]
    width = hidden_ref.shape[1]
    for number, (dz, dy) in enumerate(GROUPS):
        for i, at in enumerate(group_blocks(place, dz, dy)):
            pltpu.make_async_copy(
                slots_ref.at[pl.ds(at, 2), :, pl.ds(width, 128)], slots.at[number, pl.ds(2 * i, 2)],
                load_sems.at[2 * number + i],
            ).start()
        for j, ref in enumerate((back_a_ref, back_b_ref)):
            pltpu.make_async_copy(
                ref.at[pl.ds(number * SLOTS, SLOTS)], rows.at[number, j],
                load_sems.at[16 + 2 * number + j],
            ).start()
    greet(plane_neighbours(place) + [place.on_line(1), place.on_line(-1)])
    line = raw_sends(
        place, gw_ref, pl.ds(2, 1), right_last_ref, left_last_ref,
        [line_send.at[0], line_send.at[1]], [line_recv.at[0], line_recv.at[1]],
    )
    for i, (source, target, side) in enumerate(
        ((sum_left_ref, right_low_ref, -1), (sum_right_ref, left_high_ref, 1))
    ):
        line.append(
            remote(source, target, line_send.at[2 + i], line_recv.at[2 + i], place.on_line(side))
        )
    sums = first_sums_steps(place, gw_ref, sum_left_ref, sum_right_ref, *scratch[:6])
    scratch = scratch[6:]
    next(sums)
    for copy in line[:2]:
        copy.start()
    made = set()

    def loaded(number):
        dz, dy = GROUPS[number]
        for i, at in enumerate(group_blocks(place, dz, dy)):
            pltpu.make_async_copy(
                slots_ref.at[pl.ds(at, 2), :, pl.ds(width, 128)], slots.at[number, pl.ds(2 * i, 2)],
                load_sems.at[2 * number + i],
            ).wait()
        for j, ref in enumerate((back_a_ref, back_b_ref)):
            pltpu.make_async_copy(
                ref.at[pl.ds(number * SLOTS, SLOTS)], rows.at[number, j],
                load_sems.at[16 + 2 * number + j],
            ).wait()

    def table_of(number):
        return chosen_rows(slots[number].reshape(512, 128), first)

    def make(dz, dy):
        number = GROUPS.index((dz, dy % 2))
        if number in made:
            return
        made.add(number)
        loaded(number)
        both = rows[number].reshape(2 * SLOTS, width + 128)
        sums = dot(table_of(number), both, NN).astype(BF16).reshape(2, 2, count, width + 128)
        low = dy % 2
        blocks[dz * 4 + low] = sums[0]
        blocks[dz * 4 + low + 2] = sums[1]

    def block(dz, dy, other):
        return blocks.at[dz * 4 + dy, (place.core + other) % 2]

    def finish(row, value):
        total[pl.ds(row, 16)] = value

    def out_loads(number):
        return [
            pltpu.make_async_copy(
                ref.at[pl.ds(number * SLOTS, SLOTS)], out_rows.at[number % 2, j],
                row_sems.at[2 * (number % 2) + j],
            )
            for j, ref in enumerate((out_a_ref, out_b_ref))
        ]

    def share_saves(number):
        dz, dy = GROUPS[number]
        return [
            pltpu.make_async_copy(
                share.at[number % 2, pl.ds(2 * i, 2)], shares_ref.at[pl.ds(at, 2)],
                share_sems.at[2 * (number % 2) + i],
            )
            for i, at in enumerate(group_blocks(place, dz, dy))
        ]

    def make_share(number):
        if number + 1 < len(GROUPS):
            for load in out_loads(number + 1):
                load.start()
        for load in out_loads(number):
            load.wait()
        if number >= 2:
            for save in share_saves(number - 2):
                save.wait()
        both = out_rows[number % 2].reshape(2 * SLOTS, width)
        sums = dot(table_of(number), both, NN).astype(BF16)
        share[number % 2] = sums.reshape(4, count, width)
        for save in share_saves(number):
            save.start()

    for load in out_loads(0):
        load.start()
    turn = 0
    for at, _ in enumerate(plane_scatter_steps(place, count, make, block, scratch, finish)):
        if at == 6:
            run(sums)
            for copy in line[2:]:
                copy.start()
        if at >= 5:
            for _ in range(2):
                if turn < len(GROUPS):
                    make_share(turn)
                    turn += 1
    while turn < len(GROUPS):
        make_share(turn)
        turn += 1

    experts = picks_ref.shape[1]
    probs, gates = state_ref[:, :experts], state_ref[:, experts : 2 * experts]
    picked_total = state_ref[:, 2 * experts : 2 * experts + 1]
    second_scale = state_ref[:, 2 * experts + 1 : 2 * experts + 2]
    tail = total[:, pl.ds(width, 128)]
    gate_grad = tail[:, :experts] + tail[:, experts:]
    mean = jnp.sum(gate_grad * gates, axis=1, keepdims=True)
    prob_grad = picks_ref[...] * (gate_grad - mean) / picked_total
    logit_grad = probs * (prob_grad - jnp.sum(prob_grad * probs, axis=1, keepdims=True))
    logit_grad = logit_grad.astype(BF16)
    grad_router_ref[...] = dot(logit_grad, mixed_ref[:, :width], TN)
    grad_mixed = total[:, :width] + dot(logit_grad, router_ref[...], NN)
    hidden = hidden_ref[...]
    gain_ref[...] = jnp.sum(grad_mixed * hidden * second_scale, axis=0, keepdims=True)
    grad_hidden = grad_out_ref[...].astype(F32) + norm_back(
        hidden, second_scale, mlp_gain_ref[...], grad_mixed
    )
    grad_hidden_ref[...] = grad_hidden
    grad_att_ref[...] = grad_hidden.astype(BF16)
    for number in (len(GROUPS) - 2, len(GROUPS) - 1):
        for save in share_saves(number):
            save.wait()
    for copy in line:
        copy.wait()


def combine_scatter(
    back, out, slots, gw, grad_out, hidden, mixed, state, picks, mlp_gain, router_t, collective_id
):
    count, width = hidden.shape
    groups = len(GROUPS)
    return pl.pallas_call(
        combine_scatter_kernel,
        out_shape=(
            shape((32, count, width)),
            *[shape((3, gw.shape[1] // 8, width))] * 2,
            *[shape((1, gw.shape[1] // 8, width))] * 2,
            *[shape((3, gw.shape[1] // 8, width))] * 2,
            shape((count, width), F32),
            shape((count, width)),
            shape(router_t.shape, F32),
            shape((1, width), F32),
        ),
        in_specs=[ANY] * 6 + [VMEM] * 7,
        out_specs=(ANY, ANY, ANY, ANY, ANY, ANY, ANY, VMEM, VMEM, VMEM, VMEM),
        scratch_shapes=[
            pltpu.VMEM((groups, 2, SLOTS, width + 128), BF16),
            pltpu.VMEM((groups, 4, count, 128), BF16),
            pltpu.VMEM((16, 2, count, width + 128), BF16),
            pltpu.VMEM((2, 2, SLOTS, width), BF16),
            pltpu.VMEM((2, 4, count, width), BF16),
            pltpu.VMEM((count, width + 128), F32),
            *dma_sems(32, 4, 4, 4, 4),
            *first_sums_scratch(gw.shape[1] // 8, width),
            *scatter_scratch(count, width + 128),
        ],
        compiler_params=pltpu.CompilerParams(
            collective_id=collective_id, has_side_effects=True, vmem_limit_bytes=62 * 2**20
        ),
        cost_estimate=pl.CostEstimate(flops=6 * 10**10, bytes_accessed=10**8, transcendentals=0),
        name="combine_scatter",
    )(*back, *out, slots, gw, grad_out, hidden, mixed, state, picks, mlp_gain, router_t)


def expert_steps(
    expert_ref, parts, receive, x_hbm, d_hbm, gate_hbm, p_hbm, rb_hbm, gw_hbm,
    w, x, d, gate, rg, middle, ggp, gup, p, rb, dots, gw, in_sems, out_sems, gw_sems,
):
    f32, bf16 = jnp.float32, jnp.bfloat16
    rows, width = x.shape
    hidden = middle.shape[1]
    chunk = 256
    loads = [
        pltpu.make_async_copy(x_hbm, x, in_sems.at[0]),
        pltpu.make_async_copy(d_hbm, d, in_sems.at[1]),
        pltpu.make_async_copy(gate_hbm, gate, in_sems.at[2]),
    ]
    for i, (ref, where) in enumerate(parts):
        loads.append(pltpu.make_async_copy(ref, w.at[where], in_sems.at[3 + i]))
    for load in loads:
        load.start()
    if receive is not None:
        next(receive)
    for load in loads:
        load.wait()

    @pl.loop(0, rows, step=16)
    def _(r):
        here = pl.ds(r, 16)
        scaled = d[here].astype(f32) * gate[here, 0:1]
        rg[here] = scaled.astype(bf16)

    def hidden_chunk(c):
        here = pl.ds(c, chunk)
        gate_pre = dot(x[...], w[0, here], NT)
        up_pre = dot(x[...], w[1, here], NT)
        grad_mid = dot(rg[...], w[2, here], NT)
        sig = 1.0 / (1.0 + jnp.exp(-gate_pre))
        act = gate_pre * sig
        middle[:, here] = (act * up_pre).astype(bf16)
        ggp[:, here] = (grad_mid * up_pre * sig * (1.0 + gate_pre * (1.0 - sig))).astype(bf16)
        gup[:, here] = (grad_mid * act).astype(bf16)

    outs = []

    def weight_chunk(c):
        here = pl.ds(c, chunk)
        for i, (left, right) in enumerate(((ggp, x), (gup, x), (middle, rg))):
            turned = left[:, here].T
            for n in range(0, width, 512):
                there = pl.ds(n, 512)
                gw[i, here, there] = dot(turned, right[:, there], NN).astype(bf16)
            save = pltpu.make_async_copy(
                gw.at[i, here], gw_hbm.at[i, here], gw_sems.at[c // chunk * 3 + i]
            )
            save.start()
            outs.append(save)

    chunks = list(range(0, hidden, chunk))
    for c in chunks[:-1]:
        hidden_chunk(c)
    if receive is not None:
        for c in chunks[:-1]:
            weight_chunk(c)
        next(receive)
    hidden_chunk(chunks[-1])
    dots[...] = jnp.zeros_like(dots)

    for n in range(0, width, chunk):
        here = pl.ds(n, chunk)
        out = dot(middle[...], w[2, :, here], NN).astype(bf16).astype(f32)
        p[:, here] = (out * gate[:, 0:1]).astype(bf16)
        along = out * d[:, here].astype(f32)
        dots[...] += along[:, :128] + along[:, 128:]
        back = dot(ggp[...], w[0, :, here], NN) + dot(gup[...], w[1, :, here], NN)
        rb[:, here] = back.astype(bf16)

    expert = expert_ref[0]
    total = jnp.sum(dots[...], axis=1, keepdims=True)
    high = total.astype(bf16).astype(f32)
    lane = lax.broadcasted_iota(jnp.int32, (rows, 128), 1)
    tail = jnp.where(lane == expert, high, jnp.where(lane == expert + 64, total - high, 0.0))
    rb[:, pl.ds(width, 128)] = tail.astype(bf16)
    outs.append(pltpu.make_async_copy(rb, rb_hbm, out_sems.at[0]))
    outs.append(pltpu.make_async_copy(p, p_hbm, out_sems.at[1]))
    outs[-2].start()
    outs[-1].start()
    for c in chunks[-1:] if receive is not None else chunks:
        weight_chunk(c)
    if receive is not None:
        run(receive)
    for out in outs:
        out.wait()


def near_parts(number, gate_ref, up_ref, down_ref, left_gate, left_two, right_gate, right_two):
    shard = gate_ref.shape[1]
    own, left, right = pl.ds(0, shard), pl.ds(shard, shard), pl.ds(2 * shard, shard)
    return [
        (gate_ref.at[number], (0, own)), (up_ref.at[number], (1, own)),
        (down_ref.at[number], (2, own)), (left_gate, (0, left)),
        (left_two, (pl.ds(1, 2), left)), (right_gate, (0, right)), (right_two, (pl.ds(1, 2), right)),
    ]


def first_expert_kernel(expert_ref, x, d, gate, *refs):
    weights, low, high, rest = refs[:7], refs[7], refs[8], refs[9:]
    half = low.shape[1]
    parts = near_parts(0, *weights)
    for i, ref in enumerate((low, high)):
        parts.append((ref, (slice(None), pl.ds((6 + i) * half, half))))
    expert_steps(expert_ref, parts, None, x, d, gate, *rest)


def second_expert_kernel(expert_ref, x, d, gate, *refs):
    weights, other, rest = refs[:7], refs[7], refs[8:]
    *rest, send_sems, recv_sems = rest
    raw_right, raw_left = rest[3:5]
    rest = rest[:3] + rest[5:]
    w = rest[3]
    shard = weights[0].shape[1]
    half = shard // 2
    _, _, _, left_gate, left_two, right_gate, right_two = weights
    place = Place()

    def receive():
        greet([place.on_line(1), place.on_line(-1)])
        copies = []
        for i, (one, two, side) in enumerate(
            ((left_gate, left_two, 1), (right_gate, right_two, -1))
        ):
            cut = pl.ds(i * half, half)
            there = pl.ds((6 + i) * half, half)
            copies.append(
                remote(one.at[cut], w.at[0, there], send_sems.at[2 * i], recv_sems.at[2 * i],
                       place.on_line(side))
            )
            copies.append(
                remote(two.at[:, cut], w.at[pl.ds(1, 2), there], send_sems.at[2 * i + 1],
                       recv_sems.at[2 * i + 1], place.on_line(side))
            )
        for copy in copies:
            copy.start()
        yield
        for copy in copies:
            copy.wait()
        sends = raw_sends(
            place, other, pl.ds(0, 2), raw_right, raw_left,
            [send_sems.at[4], send_sems.at[5]], [recv_sems.at[4], recv_sems.at[5]],
        )
        for copy in sends:
            copy.start()
        yield
        for copy in sends:
            copy.wait()

    expert_steps(expert_ref, near_parts(1, *weights), receive(), x, d, gate, *rest)


def first_sums_steps(
    place, gw_hbm, sum_left, sum_right, come, mine, load_sems, send_sems, recv_sems, save_sems
):
    shard = gw_hbm.shape[1] // 4
    half = shard // 2
    sends = [
        remote(gw_hbm.at[:, pl.ds(3 * shard + i * half, half)], come.at[i], send_sems.at[i],
               recv_sems.at[i], place.on_line(side))
        for i, side in ((0, -1), (1, 1))
    ]
    loads = [
        pltpu.make_async_copy(gw_hbm.at[:, pl.ds(at, half)], mine.at[i], load_sems.at[i])
        for i, at in ((0, shard), (1, 2 * shard + half))
    ]
    for copy in sends + loads:
        copy.start()
    yield
    saves = []
    for i, target in ((0, sum_left), (1, sum_right)):
        loads[i].wait()
        sends[i].wait()

        @pl.loop(0, half, step=16)
        def _(row):
            for j in range(3):
                here = (i, j, pl.ds(row, 16))
                mine[here] = (mine[here].astype(F32) + come[here].astype(F32)).astype(BF16)

        saves.append(pltpu.make_async_copy(mine.at[i], target, save_sems.at[i]))
        saves[i].start()
    for save in saves:
        save.wait()


def first_sums_scratch(half, width):
    return [
        pltpu.VMEM((2, 3, half, width), BF16),
        pltpu.VMEM((2, 3, half, width), BF16),
        *dma_sems(2, 2, 2, 2),
    ]


def raw_sends(place, gw_hbm, which, raw_right, raw_left, send_sems, recv_sems):
    shard = gw_hbm.shape[1] // 4
    half = shard // 2
    return [
        remote(gw_hbm.at[which, pl.ds(start, half)], target, send_sems[i], recv_sems[i],
               place.on_line(side))
        for i, (start, target, side) in enumerate(
            ((shard + half, raw_right, -1), (2 * shard, raw_left, 1))
        )
    ]


def second_sends(place, gw_hbm, sum_left, sum_right, from_right, from_left, send_sems, recv_sems):
    shard = gw_hbm.shape[1] // 4
    half = shard // 2
    low, high = pl.ds(0, half), pl.ds(half, half)
    plan = [
        (gw_hbm.at[:, pl.ds(shard + half, half)], from_right.at[:, high], -1),
        (gw_hbm.at[:, pl.ds(2 * shard, half)], from_left.at[:, low], 1),
        (sum_left, from_right.at[:, low], -1),
        (sum_right, from_left.at[:, high], 1),
    ]
    return [
        remote(source, target, send_sems.at[i], recv_sems.at[i], place.on_line(side))
        for i, (source, target, side) in enumerate(plan)
    ]


def expert_layer(expert, weights, x, d, gate, other=None, collective_id=None):
    bf16 = jnp.bfloat16
    rows, width = x.shape
    hidden = 4 * weights[0].shape[1]
    second = collective_id is not None
    extra = dma_sems(6, 6) if second else []
    raw = [shape((2, hidden // 8, width))] * 2 if second else []
    more = [other] if second else []
    return pl.pallas_call(
        second_expert_kernel if second else first_expert_kernel,
        out_shape=(
            shape((rows, width)),
            shape((rows, width + 128)),
            shape((3, hidden, width)),
            *raw,
        ),
        in_specs=[SMEM] + [ANY] * (3 + len(weights) + len(more)),
        out_specs=(ANY,) * (3 + len(raw)),
        scratch_shapes=[
            pltpu.VMEM((3, hidden, width), bf16),
            pltpu.VMEM((rows, width), bf16),
            pltpu.VMEM((rows, width), bf16),
            pltpu.VMEM((rows, 128), jnp.float32),
            pltpu.VMEM((rows, width), bf16),
            pltpu.VMEM((rows, hidden), bf16),
            pltpu.VMEM((rows, hidden), bf16),
            pltpu.VMEM((rows, hidden), bf16),
            pltpu.VMEM((rows, width), bf16),
            pltpu.VMEM((rows, width + 128), bf16),
            pltpu.VMEM((rows, 128), jnp.float32),
            pltpu.VMEM((3, hidden, width), bf16),
            *dma_sems(12, 2, 9),
            *extra,
        ],
        compiler_params=pltpu.CompilerParams(
            vmem_limit_bytes=60 * 2**20, collective_id=collective_id, has_side_effects=second
        ),
        cost_estimate=pl.CostEstimate(
            flops=18 * rows * hidden * width,
            bytes_accessed=12 * hidden * width + 10 * rows * width,
            transcendentals=rows * hidden,
        ),
        name="second_expert" if second else "first_expert",
    )(expert, x, d, gate, *weights, *more)


def rope_tables(length, head_size):
    position = jnp.arange(length, dtype=jnp.float32)[:, None]
    index_half = jnp.arange(head_size // 2, dtype=jnp.float32)[None, :]
    frequency = jnp.exp(index_half * (-2.0 / head_size) * jnp.log(ROPE_BASE))
    turned = position * frequency
    sine = jnp.sin(turned)
    return (
        jnp.concatenate([jnp.cos(turned)] * 2, axis=1),
        jnp.concatenate([-sine, sine], axis=1),
    )


def inverse_rms(values):
    return lax.rsqrt(jnp.mean(values * values, axis=-1, keepdims=True) + EPSILON)


def norm_back(values, scales, gain, grads):
    weighted = grads * gain
    return scales * weighted - values * scales * scales * scales * jnp.mean(
        weighted * values, axis=-1, keepdims=True
    )


def attend(seq, w_query, w_key, w_value, q_gain, k_gain, cosine, sine,
           query_rot, key_rot, values, query_unit, key_unit, stats, context):
    length = seq.shape[0]
    head = cosine.shape[1]
    heads = w_query.shape[1] // head
    scale = head ** (-0.5)
    cos, sin = cosine[...], sine[...]
    lane = lax.broadcasted_iota(jnp.int32, (length, head), 1)
    kept = jnp.zeros((length, head), F32)

    def unit_and_rot(raw, gain):
        scales = inverse_rms(raw)
        unit = raw * scales
        normed = unit * gain
        rot = normed * cos + pltpu.roll(normed, head // 2, 1) * sin
        return scales, unit, rot.astype(BF16)

    raw = dot(seq[...], w_key[...], NN)
    scales, unit, rot = unit_and_rot(raw, k_gain[...])
    key_unit[...] = unit
    key_rot[...] = rot
    kept = jnp.where(lane == 8, scales, kept)
    values[...] = dot(seq[...], w_value[...], NN).astype(BF16)
    half = length // 2
    for pair in range(0, heads, 2):
        raws = dot(seq[...], w_query[:, pl.ds(pair * head, 2 * head)], NN)
        for h in (pair, pair + 1):
            here = pl.ds(h * head, head)
            raw = raws[:, (h - pair) * head : (h - pair + 1) * head]
            scales, unit, rot = unit_and_rot(raw, q_gain[...])
            query_unit[:, here] = unit
            query_rot[:, here] = rot
            kept = jnp.where(lane == h, scales, kept)
            logs = []
            for part in range(2):
                until = (part + 1) * half
                scores = dot(rot[part * half : until], key_rot[:until], NT) * scale
                row = lax.broadcasted_iota(jnp.int32, scores.shape, 0) + part * half
                column = lax.broadcasted_iota(jnp.int32, scores.shape, 1)
                scores = jnp.where(row >= column, scores, MASK_VALUE)
                peak = jnp.max(scores, axis=1, keepdims=True)
                raised = jnp.exp(scores - peak)
                total = jnp.sum(raised, axis=1, keepdims=True)
                probs = (raised * (1.0 / total)).astype(BF16)
                mixed = dot(probs, values[:until], NN)
                context[pl.ds(part * half, half), here] = mixed.astype(BF16)
                logs.append(peak + jnp.log(total))
            kept = jnp.where(lane == 16 + h, jnp.concatenate(logs, axis=0), kept)
        yield
    stats[...] = kept


def attend_back(grad_rows, seq, w_query, w_key, w_value, w_out, q_gain, k_gain, cosine, sine,
                query_rot, key_rot, values, query_unit, key_unit, stats,
                grad_context, grad_qkv, gains):
    length = seq.shape[0]
    head = cosine.shape[1]
    heads = query_rot.shape[1] // head
    scale = head ** (-0.5)
    cos, sin = cosine[...], sine[...]
    half = length // 2

    def rotate_back(grads):
        return grads * cos - pltpu.roll(grads, head // 2, 1) * sin

    def unit_back(scales, unit, gain, grads):
        z = grads * gain
        return scales * (z - unit * jnp.mean(z * unit, axis=1, keepdims=True))

    for n in range(0, heads * head, 256):
        here = pl.ds(n, 256)
        grad_context[:, here] = dot(grad_rows[...], w_out[here], NT).astype(BF16)
    yield
    key_grads = [jnp.zeros((half, head), F32)] * 2
    value_grads = [jnp.zeros((half, head), F32)] * 2
    q_gain_grad = jnp.zeros((1, head), F32)
    for h in range(heads):
        here = pl.ds(h * head, head)
        query_grads = []
        for part in range(2):
            until = (part + 1) * half
            rows = pl.ds(part * half, half)
            rot = query_rot[rows, here]
            scores = dot(rot, key_rot[:until], NT) * scale
            row = lax.broadcasted_iota(jnp.int32, scores.shape, 0) + part * half
            column = lax.broadcasted_iota(jnp.int32, scores.shape, 1)
            scores = jnp.where(row >= column, scores, MASK_VALUE)
            probs = jnp.exp(scores - stats[rows, 16 + h : 17 + h])
            from_context = grad_context[rows, here]
            grad_probs = dot(from_context, values[:until], NT)
            low = probs.astype(BF16)
            value_part = dot(low, from_context, TN)
            mean = jnp.sum(grad_probs * probs, axis=1, keepdims=True)
            grad_scores = (probs * (grad_probs - mean)).astype(BF16)
            query_grads.append(dot(grad_scores, key_rot[:until], NN) * scale)
            key_part = dot(grad_scores, rot, TN) * scale
            for other in range(part + 1):
                cut = slice(other * half, (other + 1) * half)
                value_grads[other] = value_grads[other] + value_part[cut]
                key_grads[other] = key_grads[other] + key_part[cut]
        grads = rotate_back(jnp.concatenate(query_grads, axis=0))
        unit = query_unit[:, here]
        q_gain_grad = q_gain_grad + jnp.sum(grads * unit, axis=0, keepdims=True)
        grad_qkv[:, here] = unit_back(stats[:, h : h + 1], unit, q_gain[...], grads).astype(BF16)
        yield
    grads = rotate_back(jnp.concatenate(key_grads, axis=0))
    unit = key_unit[...]
    gains[0:1, :] = q_gain_grad
    gains[1:2, :] = jnp.sum(grads * unit, axis=0, keepdims=True)
    grad_qkv[:, pl.ds(heads * head, head)] = unit_back(
        stats[:, 8:9], unit, k_gain[...], grads
    ).astype(BF16)
    grad_qkv[:, pl.ds((heads + 1) * head, head)] = jnp.concatenate(value_grads, axis=0).astype(BF16)
    yield


def forward_kernel(
    inputs_ref, attn_gain_ref, q_gain_ref, k_gain_ref, cos_ref, sin_ref, mlp_gain_ref, router_ref,
    picks_ref, w_query_ref, w_key_ref, w_value_ref, w_out_ref, gate_w_ref, dout_ref,
    mixed_ref, hidden_ref, state_ref, left_gate_ref, right_gate_ref, dout_all_ref, seq_ref,
    query_rot_ref, key_rot_ref, values_ref, query_unit_ref, key_unit_ref, stats_ref, context_ref,
    seq, w_query, w_key, w_value, w_out, partial, query_rot, key_rot, values, query_unit, key_unit,
    stats, context, load_sems, save_sems, gather_send, gather_recv, gate_send, gate_recv, dout_sem,
    *scratch,
):
    place = Place()
    count, width = inputs_ref.shape
    experts = picks_ref.shape[1]
    loads = [
        pltpu.make_async_copy(source, target, load_sems.at[i])
        for i, (source, target) in enumerate(
            (
                (w_key_ref, w_key), (w_value_ref, w_value),
                (w_query_ref, w_query), (w_out_ref, w_out),
            )
        )
    ]
    for load in loads:
        load.start()
    float_in = inputs_ref[...].astype(F32)
    first_scale = inverse_rms(float_in)
    own = pl.ds(place.x * count, count)
    seq[own] = (float_in * first_scale * attn_gain_ref[...]).astype(BF16)
    greet(plane_neighbours(place) + [place.on_line(1), place.on_line(-1)])
    scratch, dout_sems = scratch[:4], scratch[4:]
    keep = pltpu.make_async_copy(dout_ref, dout_all_ref.at[place.block()], dout_sem.at[0])
    douts = plane_gather_steps(place, dout_ref, lambda at: dout_all_ref.at[at], dout_sems)

    def gather_until(last):
        for stage in douts:
            if stage == last:
                break

    line = line_gather_steps(place, seq, count, (gather_send, gather_recv))
    next(line)
    keep.start()
    for _ in range(9):
        next(douts)
    run(line)
    gates_sent = [
        remote(gate_w_ref.at[0], target, gate_send.at[i], gate_recv.at[i], place.on_line(side))
        for i, (target, side) in enumerate(((left_gate_ref, 1), (right_gate_ref, -1)))
    ]
    for copy in gates_sent:
        copy.start()
    for load in loads:
        load.wait()
    heads_done = attend(
        seq, w_query, w_key, w_value, q_gain_ref, k_gain_ref, cos_ref, sin_ref,
        query_rot, key_rot, values, query_unit, key_unit, stats, context,
    )
    next(heads_done)
    next(heads_done)
    gather_until(101)
    run(heads_done)
    for n in range(0, width, 512):
        here = pl.ds(n, 512)
        partial[:, here] = dot(context[...], w_out[:, here], NN).astype(BF16)
    steps = line_scatter_steps(place, partial, count, scratch)
    next(steps)
    gather_until(102)
    saves = [
        pltpu.make_async_copy(source, target, save_sems.at[i])
        for i, (source, target) in enumerate(
            (
                (seq, seq_ref), (query_rot, query_rot_ref), (key_rot, key_rot_ref),
                (values, values_ref), (query_unit, query_unit_ref), (key_unit, key_unit_ref),
                (stats, stats_ref), (context, context_ref),
            )
        )
    ]
    for save in saves:
        save.start()
    next(steps)
    run(douts)
    run(steps)
    in_b = scratch[1]
    attended = partial[own].astype(F32) + in_b[0].astype(F32) + in_b[1].astype(F32)
    hidden = float_in + attended
    hidden_ref[...] = hidden
    second_scale = inverse_rms(hidden)
    mixed = (hidden * second_scale * mlp_gain_ref[...]).astype(BF16)
    mixed_ref[:, :width] = mixed
    logits = dot(mixed, router_ref[...], NT)
    raised = jnp.exp(logits - jnp.max(logits, axis=1, keepdims=True))
    probs = raised / jnp.sum(raised, axis=1, keepdims=True)
    picked = picks_ref[...] * probs
    picked_total = jnp.sum(picked, axis=1, keepdims=True)
    gates = picked / picked_total
    high = gates.astype(BF16)
    low = (gates - high.astype(F32)).astype(BF16)
    mixed_ref[:, width:] = jnp.concatenate([high, low], axis=1)
    state_ref[:, : 2 * experts] = jnp.concatenate([probs, gates], axis=1)
    lane = lax.broadcasted_iota(jnp.int32, (count, 2 * experts), 1)
    extra = jnp.where(lane == 0, picked_total, jnp.where(lane == 1, second_scale, first_scale))
    state_ref[:, 2 * experts :] = extra
    for copy in saves + gates_sent + [keep]:
        copy.wait()


def forward(inputs, attn_gain, q_gain, k_gain, cosine, sine, mlp_gain, router_t, picks,
            w_query, w_key, w_value, w_out, gate_w, dout, collective_id):
    count, width = inputs.shape
    head = cosine.shape[1]
    length = 4 * count
    wide = w_query.shape[1]
    saved = [
        ((length, width), BF16), ((length, wide), BF16), ((length, head), BF16),
        ((length, head), BF16), ((length, wide), F32), ((length, head), F32),
        ((length, head), F32), ((length, wide), BF16),
    ]
    kept = [pltpu.VMEM(dims, dtype) for dims, dtype in saved]
    return pl.pallas_call(
        forward_kernel,
        out_shape=(
            shape((count, width + 128)),
            shape((count, width), F32),
            shape((count, 256), F32),
            *[shape(gate_w.shape[1:])] * 2,
            shape((32, *dout.shape)),
            *[shape(dims, dtype) for dims, dtype in saved],
        ),
        in_specs=[VMEM] * 9 + [ANY] * 6,
        out_specs=(VMEM, VMEM, VMEM, *[ANY] * 11),
        scratch_shapes=[
            kept[0],
            *[pltpu.VMEM(w.shape, BF16) for w in (w_query, w_key, w_value, w_out)],
            pltpu.VMEM((length, width), BF16),
            *kept[1:],
            *dma_sems(4, 8, 4, 4, 2, 2, 1),
            *line_scatter_scratch(count, width),
            *gather_sems(),
        ],
        compiler_params=pltpu.CompilerParams(
            collective_id=collective_id, has_side_effects=True, vmem_limit_bytes=60 * 2**20
        ),
        cost_estimate=pl.CostEstimate(flops=7 * 10**10, bytes_accessed=10**8, transcendentals=0),
        name="forward",
    )(inputs, attn_gain, q_gain, k_gain, cosine, sine, mlp_gain, router_t, picks,
      w_query, w_key, w_value, w_out, gate_w, dout)


LATE_EVERY = 12


def exchange_steps(buffer, inbox, peers, sems):
    send_sems, recv_sems, base = sems
    copies = [
        remote(buffer, inbox.at[base + i], send_sems.at[base + i], recv_sems.at[base + i], device)
        for i, device in enumerate(peers)
    ]
    for copy in copies:
        copy.start()
    yield
    for copy in copies:
        copy.wait()


def backward_kernel(
    grad_att_ref, inputs_ref, attn_gain_ref, q_gain_ref, k_gain_ref, cos_ref, sin_ref, state_ref,
    grad_hidden_ref, router_grad_ref, mlp_grad_ref,
    gw_b_ref, seq_ref, w_query_ref, w_key_ref, w_value_ref, w_out_ref,
    query_rot_ref, key_rot_ref, values_ref, query_unit_ref, key_unit_ref, stats_ref, context_ref,
    grad_inputs_ref, router_out_ref, gains_out_ref, all_w_ref, right_b_ref, left_b_ref,
    sum_left_ref, sum_right_ref,
    grad_rows, seq, w_query, w_key, w_value, w_out,
    query_rot, key_rot, values, query_unit, key_unit, stats, context,
    grad_context, grad_qkv, summed, out_w, qkv_w, gains,
    small, small_in, small_out, late, late_in, both_sum, load_sems, line_send, line_recv, small_send,
    small_recv, second_send, second_recv, *scratch,
):
    place = Place()
    count, width = inputs_ref.shape
    experts = router_grad_ref.shape[0]
    head = cos_ref.shape[1]
    pairs = (
        (context_ref, context), (w_out_ref, w_out), (query_rot_ref, query_rot),
        (key_rot_ref, key_rot), (values_ref, values), (stats_ref, stats),
        (query_unit_ref, query_unit), (key_unit_ref, key_unit), (w_query_ref, w_query),
        (w_key_ref, w_key), (w_value_ref, w_value), (seq_ref, seq),
    )
    loads = [
        pltpu.make_async_copy(source, target, load_sems.at[i])
        for i, (source, target) in enumerate(pairs)
    ]
    for load in loads:
        load.start()
    own = pl.ds(place.x * count, count)
    grad_rows[own] = grad_att_ref[...]
    far = {
        "x": [place.on_line(step) for step in (1, -1, 2)],
        "z": [place.device("z", step) for step in (1, -1, 2)],
        "y": [place.device("y", step) for step in (1, -1, 2)],
        "core": [place.device(other=1)],
    }
    greet([device for axis in ("x", "z", "y", "core") for device in far[axis]])
    line = line_gather_steps(place, grad_rows, count, (line_send, line_recv))
    next(line)

    part = small.shape[1]
    small[...] = jnp.zeros_like(small)
    for i in range(4):
        used = min(part, experts + 1 - i * part)
        from_router = min(used, experts - i * part)
        if from_router > 0:
            small[i, :from_router] = router_grad_ref[i * part : i * part + from_router]
    at_gain = experts // part
    small[at_gain, experts - at_gain * part : experts - at_gain * part + 1] = mlp_grad_ref[...]

    def small_total():
        def send(step, number):
            return remote(
                small.at[(place.x + step) % 4], small_in.at[number], small_send.at[number],
                small_recv.at[number], place.on_line(step),
            )

        copies = [send(step, i) for i, step in enumerate((1, -1, 2))]
        for copy in copies:
            copy.start()
        yield
        for copy in copies:
            copy.wait()
        mine = small.at[place.x]
        mine[...] = mine[...] + small_in[0] + small_in[1] + small_in[2]
        base = 3
        for axis in ("z", "y", "core"):
            peers = far[axis]
            yield from exchange_steps(mine, small_in, peers, (small_send, small_recv, base))
            total = mine[...]
            for i in range(len(peers)):
                total = total + small_in[base + i]
            mine[...] = total
            base += len(peers)
        done = small_out.at[place.x]
        done[...] = mine[...]
        copies = [
            remote(done, done, small_send.at[base + i], small_recv.at[base + i], device)
            for i, device in enumerate(far["x"])
        ]
        for copy in copies:
            copy.start()
        yield
        for i, step in enumerate((-1, 1, 2)):
            copies[i].wait_send()
            there = small_out.at[(place.x + step) % 4]
            remote(
                there, there, small_send.at[base + i], small_recv.at[base + i], far["x"][0]
            ).wait_recv()

    smalls = small_total()
    next(smalls)
    run(line)

    half = width // 2
    for load in loads[:2]:
        load.wait()
    for n in range(0, width, 512):
        where = (pl.ds((n // half) * context.shape[1], context.shape[1]), pl.ds(n % half, 512))
        out_w[where] = dot(context[...], grad_rows[:, pl.ds(n, 512)], TN).astype(BF16)

    def scattered(weights, columns, scratch):
        rows = weights.shape[0] // 32

        def block(dz, dy, other):
            return weights.at[pl.ds(place.block("z", dz, dy, other) * rows, rows)]

        def finish(row, value):
            both_sum[pl.ds(row, 16), columns] = value.astype(BF16)

        return plane_scatter_steps(place, rows, lambda dz, dy: None, block, scratch, finish)

    out_width = out_w.shape[1]
    scatter_out, scratch = scratch[:9], scratch[9:]
    scatter_qkv, scratch = scratch[:9], scratch[9:]
    gather_both, scratch = scratch[:4], scratch[4:]
    late_send, late_recv, keep_sem, *scratch = scratch
    sums_scratch, scratch = scratch[:6], scratch[6:]

    def out_total():
        return scattered(out_w, pl.ds(0, out_width), scatter_out)

    outs = out_total()
    next(outs)
    sums = first_sums_steps(place, gw_b_ref, sum_left_ref, sum_right_ref, *sums_scratch)
    next(sums)
    next(smalls)
    second = second_sends(
        place, gw_b_ref, sum_left_ref, sum_right_ref, right_b_ref, left_b_ref, second_send, second_recv
    )
    for load in loads[2:]:
        load.wait()
    back = attend_back(grad_rows, seq, w_query, w_key, w_value, w_out, q_gain_ref, k_gain_ref,
                       cos_ref, sin_ref, query_rot, key_rot, values, query_unit, key_unit, stats,
                       grad_context, grad_qkv, gains)
    gains[...] = jnp.zeros_like(gains)
    for at, _ in enumerate(back):
        next(outs, None)
        if at in (4, 9):
            next(smalls)
        if at == 9:
            for copy in second[:2]:
                copy.start()
    heads = query_rot.shape[1]
    for n in range(0, width, 512):
        here = pl.ds(n, 512)
        value = dot(grad_qkv[:, :heads], w_query[here], NT)
        value = value + dot(grad_qkv[:, heads : heads + head], w_key[here], NT)
        value = value + dot(grad_qkv[:, heads + head :], w_value[here], NT)
        summed[:, here] = value.astype(BF16)
    line_scatter = scratch
    line = line_scatter_steps(place, summed, count, line_scatter)
    next(line)
    for n in range(0, grad_qkv.shape[1], 256):
        here = pl.ds(n, 256)
        qkv_w[:, here] = dot(seq[...], grad_qkv[:, here], TN).astype(BF16)

    rows = both_sum.shape[0]

    def qkv_total():
        yield from scattered(qkv_w, pl.ds(out_width, qkv_w.shape[1]), scatter_qkv)
        for _ in outs:
            pass
        keep = pltpu.make_async_copy(
            both_sum, all_w_ref.at[pl.ds(place.block() * rows, rows)], keep_sem.at[0]
        )
        keep.start()
        yield from plane_gather_steps(
            place, both_sum, lambda at: all_w_ref.at[pl.ds(at * rows, rows)], gather_both
        )
        keep.wait()

    qkvs = qkv_total()
    for step in range(15):
        next(qkvs)
        if step == 4:
            run(sums)
        if step == 7:
            next(line)
        if step == 10:
            next(smalls)
    run(line)
    in_b = line_scatter[1]
    grad_normed = summed[own].astype(F32) + in_b[0].astype(F32) + in_b[1].astype(F32)
    float_in = inputs_ref[...].astype(F32)
    first_scale = state_ref[:, 2 * experts + 2 : 2 * experts + 3]
    grad_inputs_ref[...] = (
        grad_hidden_ref[...] + norm_back(float_in, first_scale, attn_gain_ref[...], grad_normed)
    ).astype(BF16)
    late[...] = jnp.zeros_like(late)
    late[0:1, :] = jnp.sum(grad_normed * float_in * first_scale, axis=0, keepdims=True)
    late[1:2, :head] = gains[0:1, :]
    late[1:2, head : 2 * head] = gains[1:2, :]

    def late_total():
        base = 0
        for axis in ("x", "z", "y", "core"):
            peers = far[axis]
            yield from exchange_steps(late, late_in, peers, (late_send, late_recv, base))
            total = late[...]
            for i in range(len(peers)):
                total = total + late_in[base + i]
            late[...] = total
            base += len(peers)

    lates = late_total()
    next(lates)
    for _ in range(4):
        next(qkvs)
    next(lates)
    for copy in second[2:]:
        copy.start()
    steps_done = 0
    for _ in qkvs:
        steps_done += 1
        if steps_done % LATE_EVERY == 0:
            next(lates, None)
    run(lates)
    run(smalls)
    gains_out_ref[0:2] = late[0:2]
    at_row = experts - at_gain * part
    gains_out_ref[2:3] = small_out[at_gain, at_row : at_row + 1]
    for i in range(4):
        from_router = min(part, experts - i * part)
        if from_router > 0:
            router_out_ref[i * part : i * part + from_router] = small_out[i, :from_router]
    for copy in second:
        copy.wait()


def backward(grad_att, inputs, attn_gain, q_gain, k_gain, cosine, sine, state, grad_hidden,
             router_grad, mlp_grad, gw_b, weights, saved, collective_id):
    count, width = inputs.shape
    length = 4 * count
    head = cosine.shape[1]
    seq, query_rot, key_rot, values, query_unit, key_unit, stats, context = saved
    w_query, w_key, w_value, w_out = weights
    wide = w_query.shape[1]
    total = wide + 2 * head
    experts = router_grad.shape[0]
    part = -(-(experts + 1) // 32) * 8
    rows = width // 32
    shard = gw_b.shape[1] // 4
    like = lambda array: pltpu.VMEM(array.shape, array.dtype)
    return pl.pallas_call(
        backward_kernel,
        out_shape=(
            shape((count, width)),
            shape((experts, width), F32),
            shape((8, width), F32),
            shape((width, width // 2 + total)),
            *[shape((3, shard, width))] * 2,
            *[shape((3, shard // 2, width))] * 2,
        ),
        in_specs=[VMEM] * 11 + [ANY] * 13,
        out_specs=(VMEM, VMEM, VMEM) + (ANY,) * 5,
        scratch_shapes=[
            pltpu.VMEM((length, width), BF16),
            *[like(a) for a in (seq, w_query, w_key, w_value, w_out)],
            *[like(a) for a in saved[1:]],
            pltpu.VMEM((length, wide), BF16),
            pltpu.VMEM((length, total), BF16),
            pltpu.VMEM((length, width), BF16),
            pltpu.VMEM((2 * wide, width // 2), BF16),
            pltpu.VMEM((width, total), BF16),
            pltpu.VMEM((8, head), F32),
            pltpu.VMEM((4, part, width), F32),
            pltpu.VMEM((10, part, width), F32),
            pltpu.VMEM((4, part, width), F32),
            pltpu.VMEM((8, width), F32),
            pltpu.VMEM((10, 8, width), F32),
            pltpu.VMEM((rows, width // 2 + total), BF16),
            *dma_sems(12, 4, 4, 13, 13, 4, 4),
            *scatter_scratch(2 * wide // 32, width // 2),
            *scatter_scratch(rows, total),
            *gather_sems(),
            *dma_sems(10, 10, 1),
            *first_sums_scratch(shard // 2, width),
            *line_scatter_scratch(count, width),
        ],
        compiler_params=pltpu.CompilerParams(
            collective_id=collective_id, has_side_effects=True, vmem_limit_bytes=62 * 2**20
        ),
        cost_estimate=pl.CostEstimate(flops=10**11, bytes_accessed=10**8, transcendentals=0),
        name="backward",
    )(grad_att, inputs, attn_gain, q_gain, k_gain, cosine, sine, state, grad_hidden, router_grad,
      mlp_grad, gw_b, seq, w_query, w_key, w_value, w_out, *saved[1:])


def attention_grads_kernel(all_ref, out_ref, query_ref, key_ref, value_ref):
    value = all_ref[...].astype(F32)
    at = 0
    for ref in (out_ref, query_ref, key_ref, value_ref):
        ref[...] = value[:, at : at + ref.shape[1]]
        at += ref.shape[1]


def attention_grads(total, wide, narrow):
    rows, full = total.shape
    half = full - wide - 2 * narrow
    step = 128
    steps = rows // step
    cut = wide // step
    return pl.pallas_call(
        attention_grads_kernel,
        grid=(steps,),
        out_shape=(
            shape((wide, half * steps // cut), F32), shape((rows, wide), F32),
            shape((rows, narrow), F32), shape((rows, narrow), F32),
        ),
        in_specs=[pl.BlockSpec((step, full), lambda i: (i, 0))],
        out_specs=(
            pl.BlockSpec((step, half), lambda i: (i % cut, i // cut)),
            pl.BlockSpec((step, wide), lambda i: (i, 0)),
            pl.BlockSpec((step, narrow), lambda i: (i, 0)),
            pl.BlockSpec((step, narrow), lambda i: (i, 0)),
        ),
        compiler_params=pltpu.CompilerParams(vmem_limit_bytes=32 * 2**20),
        name="attention_grads",
    )(total)


def expert_grads_kernel(
    own_a, right_low, left_high, raw_right, raw_left, right_last, left_last,
    own_b, right_b, left_b, *outs,
):
    step = pl.program_id(0)

    def add(own, right, left):
        for i, out in enumerate(outs):
            out[0] = own[i].astype(F32) + right[i].astype(F32) + left[i].astype(F32)

    @pl.when(step == 0)
    def _():
        add(own_a, right_low, [raw_left[0], raw_left[1], left_last[0]])

    @pl.when(step == 1)
    def _():
        add(own_a, [raw_right[0], raw_right[1], right_last[0]], left_high)

    @pl.when(step >= 2)
    def _():
        add(own_b, right_b, left_b)


def expert_grads(first, second):
    _, shard, width = second[1].shape
    half = shard // 2
    early = pl.BlockSpec((3, half, width), lambda i: (0, jnp.minimum(i, 1), 0))
    late = pl.BlockSpec((3, half, width), lambda i: (0, jnp.maximum(i - 2, 0), 0))
    whole = [pl.BlockSpec(part.shape, lambda i: (0, 0, 0)) for part in first[1:]]
    return pl.pallas_call(
        expert_grads_kernel,
        grid=(4,),
        out_shape=(shape((2, shard, width), F32),) * 3,
        in_specs=[early, *whole] + [late] * 3,
        out_specs=(pl.BlockSpec((1, half, width), lambda i: (i // 2, i % 2, 0)),) * 3,
        compiler_params=pltpu.CompilerParams(vmem_limit_bytes=48 * 2**20),
        name="expert_grads",
    )(*first, *second)


def along_line(value, step):
    return lax.ppermute(value, "tensor", [(i, (i + step) % 4) for i in range(4)])


def per_device(
    inputs,
    attn_gain,
    w_query,
    w_key,
    w_value,
    q_gain,
    k_gain,
    w_out,
    mlp_gain,
    w_router,
    w_gate,
    w_up,
    w_down,
    routes,
    grad_out,
):
    row_count, model_width = inputs.shape
    head_size = q_gain.shape[0]
    expert_count = w_router.shape[1]
    place = lax.axis_index("expert")
    first = (2 * place).astype(jnp.int32).reshape(1)

    chosen = routes[:, :, None] == jnp.arange(expert_count, dtype=jnp.int32)[None, None, :]
    picks = jnp.sum(chosen.astype(F32), axis=1)
    before = (jnp.arange(row_count)[:, None] > jnp.arange(row_count)[None, :]).astype(BF16)
    rank = jnp.dot(before, picks.astype(BF16), preferred_element_type=F32)
    base = 20 * ((place // 4) % 2 * 2 + place % 2)
    slots = jnp.where(picks > 0.0, rank + base.astype(F32), -1.0)
    slots = jnp.concatenate([slots, jnp.full_like(slots, -1.0)], axis=1).astype(BF16)
    dout = jnp.concatenate([grad_out, slots], axis=1)

    gate_t = jnp.swapaxes(w_gate, 1, 2)
    up_t = jnp.swapaxes(w_up, 1, 2)
    cosine, sine = rope_tables(4 * row_count, head_size)
    router_t = w_router.T
    q_gain, k_gain = q_gain[None], k_gain[None]
    attn_gain, mlp_gain = attn_gain[None], mlp_gain[None]
    mixed, hidden, state, left_a, right_a, dout_all, *saved = forward(
        inputs, attn_gain, q_gain, k_gain, cosine, sine, mlp_gain, router_t, picks,
        w_query, w_key, w_value, w_out, gate_t, dout, 0,
    )

    left_two_a, right_two_a, low_a, high_a, left_b, right_b, _, *rows = gather_select(
        mixed, dout_all, gate_t, up_t, w_down, left_a, right_a, 1
    )
    grad_a, grad_b, rows_a, rows_b, gate_a, gate_b = rows
    own_two, rows_a = lax.optimization_barrier((jnp.stack([up_t[1], w_down[1]]), rows_a))
    left_two_b, right_two_b = along_line(own_two, 1), along_line(own_two, -1)
    shards = (gate_t, up_t, w_down)
    out_a, back_a, gw_a = expert_layer(
        first, (*shards, left_a, left_two_a, right_a, right_two_a, low_a, high_a),
        rows_a, grad_a, gate_a,
    )
    rows_b, back_a, left_two_b, right_two_b = lax.optimization_barrier(
        (rows_b, back_a, left_two_b, right_two_b)
    )
    out_b, back_b, gw_b, raw_right, raw_left = expert_layer(
        first + 1, (*shards, left_b, left_two_b, right_b, right_two_b), rows_b, grad_b, gate_b,
        gw_a, 4,
    )
    shares, right_low, left_high, right_last, left_last, _, _, *results = combine_scatter(
        (back_a, back_b), (out_a, out_b), dout_all, gw_a, grad_out, hidden, mixed, state, picks,
        mlp_gain, router_t, 2,
    )
    grad_hidden, grad_att, router_grad, mlp_grad = results
    expert_mix = lax.psum_scatter(
        shares.reshape(-1, model_width), "expert", scatter_dimension=0, tiled=True
    )
    output = (hidden + expert_mix.astype(F32)).astype(BF16)

    results = backward(
        grad_att, inputs, attn_gain, q_gain, k_gain, cosine, sine, state, grad_hidden,
        router_grad, mlp_grad, gw_b, (w_query, w_key, w_value, w_out), saved, 3,
    )
    grad_inputs, router_grad, gains, all_w, right_b, left_b, _, _ = results
    out_w, query_w, key_w, value_w = attention_grads(all_w, w_query.shape[1], w_key.shape[1])
    gate_w, up_w, down_w = expert_grads(
        (gw_a, right_low, left_high, raw_right, raw_left, right_last, left_last),
        (gw_b, right_b, left_b),
    )
    return (
        output,
        grad_inputs,
        gains[0],
        query_w,
        key_w,
        value_w,
        gains[1, :head_size],
        gains[1, head_size : 2 * head_size],
        out_w,
        gains[2],
        router_grad.T,
        jnp.swapaxes(gate_w, 1, 2),
        jnp.swapaxes(up_w, 1, 2),
        down_w,
    )


def solution(mesh):
    placed = (
        P(("expert", "tensor"), None),
        P(),
        P(None, "tensor"),
        P(None, "tensor"),
        P(None, "tensor"),
        P(),
        P(),
        P("tensor", None),
        P(),
        P(),
        P("expert", None, "tensor"),
        P("expert", None, "tensor"),
        P("expert", "tensor", None),
        P(("expert", "tensor"), None),
        P(("expert", "tensor"), None),
    )
    return jax.shard_map(
        per_device,
        mesh=mesh,
        in_specs=placed,
        out_specs=(
            P(("expert", "tensor"), None),
            P(("expert", "tensor"), None),
            P(),
            P(None, "tensor"),
            P(None, "tensor"),
            P(None, "tensor"),
            P(),
            P(),
            P("tensor", None),
            P(),
            P(),
            P("expert", None, "tensor"),
            P("expert", None, "tensor"),
            P("expert", "tensor", None),
        ),
        check_vma=False,
    )
```
